32 devices in a mesh: grp: 4 (over x, core), ctx: 8 (over z, y).
Axes of the slice: x: 2, y: 2, z: 4, core: 2. Of those that a mesh axis runs over, the one named last changes fastest.
Arguments:
- tokens: bfloat16 [8192, 768], P(('grp', 'ctx')), may hold values from -6 to 6
- ln1_gain: bfloat16 [768], replicated, may hold values from 0.5 to 1.5
- ln1_bias: bfloat16 [768], replicated, may hold values from -1.75 to 1.75
- qkv_weight: bfloat16 [768, 2304], replicated, may hold values from -0.21875 to 0.21875
- qkv_bias: bfloat16 [2304], replicated, may hold values from -1.75 to 1.75
- out_weight: bfloat16 [768, 768], replicated, may hold values from -2 to 2
- out_bias: bfloat16 [768], replicated, may hold values from -1.75 to 1.75
- ln2_gain: bfloat16 [768], replicated, may hold values from 0.5 to 1.5
- ln2_bias: bfloat16 [768], replicated, may hold values from -1.75 to 1.75
- fc_weight: bfloat16 [768, 3072], replicated, may hold values from -0.21875 to 0.21875
- fc_bias: bfloat16 [3072], replicated, may hold values from -1.75 to 1.75
- proj_weight: bfloat16 [3072, 768], replicated, may hold values from -0.109375 to 0.109375
- proj_bias: bfloat16 [768], replicated, may hold values from -1.75 to 1.75
- doc_blocks: int32 [4, 5], P('grp'), may hold values from 0 to 128, as said below
- cotangent: bfloat16 [8192, 768], P(('grp', 'ctx')), may hold values from -6 to 6
Outputs:
- output: float32 [8192, 768], P(('grp', 'ctx'))
- grad_tokens: float32 [8192, 768], P(('grp', 'ctx'))
- grad_ln1_gain: float32 [768], P('ctx')
- grad_ln1_bias: float32 [768], P('ctx')
- grad_qkv_weight: float32 [768, 2304], P('ctx')
- grad_qkv_bias: float32 [2304], P('ctx')
- grad_out_weight: float32 [768, 768], P('ctx')
- grad_out_bias: float32 [768], P('ctx')
- grad_ln2_gain: float32 [768], P('ctx')
- grad_ln2_bias: float32 [768], P('ctx')
- grad_fc_weight: float32 [768, 3072], P('ctx')
- grad_fc_bias: float32 [3072], P('ctx')
- grad_proj_weight: float32 [3072, 768], P('ctx')
- grad_proj_bias: float32 [768], P('ctx')
The draws below stay inside these ranges and needn't reach their ends.
Inputs may be any that keep to these rules, and one draw needn't show every extreme that they name: `doc_blocks`: each group's row holds one or more entries of 128; its other entries are 32 or 0, and the row sums to 256.
All inputs are finite; a program needn't handle non-finite values.
Results may differ from the reference program's by a relative error of at most 0.01.
Values may be sent and summed in bfloat16 or wider, within the bound.
No kernel may reach another device: no remote copies, remote signals or barrier semaphores. Data moves between devices by JAX's collectives and lax.ppermute only.
A program may use at most 320 MiB of HBM per device.

```python
import math
import jax
import jax.numpy as jnp
from jax import lax

D = 768
H = 12
HD = 64
FF = 3072
TOK_DEV = 256
MOST_BLK = 128
DOCS = 5
TOKENS = 8192
N_GRP = 4
N_CTX = 8


def draw_doc_blocks(key, part):
    key = jax.random.fold_in(key, 11)
    ratio = TOK_DEV // MOST_BLK
    short_size = MOST_BLK // 4
    count_key, order_key = jax.random.split(key, 2)
    long_count = jax.random.randint(count_key, (N_GRP,), 1, ratio + 1).astype(jnp.int32)
    short_count = (ratio - long_count) * 4
    slots = jnp.arange(DOCS, dtype=jnp.int32)[None, :]
    sizes = jnp.where(slots < long_count[:, None], MOST_BLK, jnp.where(slots < (long_count + short_count)[:, None], short_size, 0)).astype(jnp.int32)
    row_keys = jax.random.split(order_key, N_GRP)
    orders = jax.vmap(lambda row_key: jax.random.permutation(row_key, DOCS))(row_keys).astype(jnp.int32)
    return jnp.take_along_axis(sizes, orders, axis=1).astype(jnp.int32)


def block_scale(key, dims, cuts, smallest, largest):
    level = 1.0
    for dim, shards_of in cuts:
        heights = jax.random.uniform(jax.random.fold_in(jax.random.fold_in(key, 6), dim), (shards_of,), jnp.float32, smallest / len(cuts), largest / len(cuts))
        level = level * jnp.repeat(jnp.exp(heights), dims[dim] // shards_of).reshape((-1,) + (1,) * (len(dims) - 1 - dim))
    return level


def centred(stream_key, shape, width, limit, shards=(), kind=jnp.bfloat16):
    entries = jax.random.normal(stream_key, shape, jnp.float32) * width
    if len(shards) > 0:
        entries = block_scale(stream_key, shape, shards, -0.22, 0.18) * entries
    return jnp.clip(entries, min=-limit, max=limit).astype(kind)


def setup_inputs(seed: int = 0) -> dict:
    arg_keys = jax.random.split(jax.random.key(seed), 16)
    return {
        "tokens": centred(arg_keys[0], (TOKENS, D), 1.0, 6.0, ((0, 32),)),
        "ln1_gain": jnp.clip(1.0 + 0.1 * jax.random.normal(arg_keys[1], (D,), jnp.float32), 0.5, 1.5).astype(jnp.bfloat16),
        "ln1_bias": centred(arg_keys[2], (D,), 0.3, 1.75),
        "qkv_weight": centred(arg_keys[3], (D, 3 * D), D ** -0.5, 0.21875),
        "qkv_bias": centred(arg_keys[4], (3 * D,), 0.3, 1.75),
        "out_weight": centred(arg_keys[5], (D, D), 8 ** -0.5, 2.0),
        "out_bias": centred(arg_keys[6], (D,), 0.3, 1.75),
        "ln2_gain": jnp.clip(1.0 + 0.1 * jax.random.normal(arg_keys[7], (D,), jnp.float32), 0.5, 1.5).astype(jnp.bfloat16),
        "ln2_bias": centred(arg_keys[8], (D,), 0.3, 1.75),
        "fc_weight": centred(arg_keys[9], (D, FF), D ** -0.5, 0.21875),
        "fc_bias": centred(arg_keys[10], (FF,), 0.3, 1.75),
        "proj_weight": centred(arg_keys[11], (FF, D), FF ** -0.5, 0.109375),
        "proj_bias": centred(arg_keys[12], (D,), 0.3, 1.75),
        "doc_blocks": draw_doc_blocks(jax.random.fold_in(arg_keys[15], 71), 0),
        "cotangent": centred(arg_keys[14], (TOKENS, D), 1.0, 6.0, ((0, 32),)),
    }


EXACT_MATMUL = lax.Precision.HIGHEST

@jax.custom_vjp
def low(v):
    return lax.optimization_barrier(v.astype(jnp.bfloat16)).astype(jnp.float32)

@jax.custom_vjp
def low_back(v):
    return v

def low_keep(v):
    return (low(v), None)

def low_pass(kept, grad):
    return (grad,)

def back_keep(v):
    return (v, None)

def back_low(kept, grad):
    return (low(grad),)
low.defvjp(low_keep, low_pass)
low_back.defvjp(back_keep, back_low)

def layer_norm(values, gain_vec, shift_vec):
    center = values - lax.optimization_barrier(jnp.mean(values, axis=-1, keepdims=True))
    spread = lax.optimization_barrier(jnp.mean(center * center, axis=-1, keepdims=True))
    return center * lax.rsqrt(spread + 1e-05) * gain_vec + shift_vec

def matmul(left_side, right_side):
    return jnp.dot(left_side, right_side, precision=EXACT_MATMUL)

def doc_layout(doc_sizes, per_device, device_count):
    doc_sizes = doc_sizes.astype(jnp.int32)
    offsets = (jnp.cumsum(doc_sizes) - doc_sizes).astype(jnp.int32)
    indices = jnp.arange(per_device * device_count, dtype=jnp.int32)
    device_ids = indices // per_device
    local_rows = indices % per_device
    doc_ids = lax.optimization_barrier(jnp.sum((local_rows[:, None] >= offsets[None, :]).astype(jnp.int32), axis=1)) - 1
    onehot = (doc_ids[:, None] == jnp.arange(doc_sizes.shape[0], dtype=jnp.int32)[None, :]).astype(jnp.int32)
    doc_width = lax.optimization_barrier(jnp.sum(onehot * doc_sizes[None, :], axis=1))
    doc_start = lax.optimization_barrier(jnp.sum(onehot * offsets[None, :], axis=1))
    return (doc_ids.astype(jnp.int32), (device_ids * doc_width + local_rows - doc_start).astype(jnp.int32))

def group_forward(inputs, params, doc_ids, positions):
    ln1_gain, ln1_bias, qkv_weight, qkv_bias, out_weight, out_bias, ln2_gain, ln2_bias, fc_weight, fc_bias, proj_weight, proj_bias = params
    count_rows = inputs.shape[0]
    scaling = HD ** (-0.5)
    normed = low(layer_norm(inputs, ln1_gain, ln1_bias))
    packed = low(low_back(matmul(normed, qkv_weight) + qkv_bias))
    queries = packed[:, :D].reshape(count_rows, H, HD)
    key_rows = packed[:, D:2 * D].reshape(count_rows, H, HD)
    values = packed[:, 2 * D:].reshape(count_rows, H, HD)
    same_doc = doc_ids[:, None] == doc_ids[None, :]
    select_mask = same_doc & (positions[None, :] < positions[:, None]) & (positions[None, :] >= 1)
    first_head = low_back(matmul(queries[:, 0], key_rows[:, 0].T) * scaling)
    picked_tokens = jnp.where(select_mask, jnp.square(jax.nn.relu(first_head)) / MOST_BLK, 0.0)
    penalty = jnp.cumsum(picked_tokens, axis=0) - picked_tokens
    block_rows = math.gcd(count_rows, 512)
    block_count = count_rows // block_rows

    def attend(pieces):
        query_block, first_block, penalty_block, doc_block, position_block = pieces
        other_heads = low_back(jnp.einsum('qhd,khd->hqk', query_block[:, 1:], key_rows[:, 1:], precision=EXACT_MATMUL) * scaling)
        logits = jnp.concatenate([first_block[None], other_heads], axis=0) - penalty_block[None]
        visible = (doc_block[:, None] == doc_ids[None, :]) & (positions[None, :] <= position_block[:, None])
        masked = jnp.where(visible[None], logits, -1e+30)
        top_value = lax.optimization_barrier(jnp.max(masked, axis=-1, keepdims=True))
        weights = jnp.where(visible[None], jnp.exp(masked - top_value), 0.0)
        probability = weights / lax.optimization_barrier(jnp.sum(weights, axis=-1, keepdims=True))
        return jnp.einsum('hqk,khd->qhd', low(probability), values, precision=EXACT_MATMUL)
    attended = lax.map(jax.checkpoint(attend), (queries.reshape(block_count, block_rows, H, HD), first_head.reshape(block_count, block_rows, count_rows), penalty.reshape(block_count, block_rows, count_rows), doc_ids.reshape(block_count, block_rows), positions.reshape(block_count, block_rows)))
    attended = low(low_back(attended.reshape(count_rows, D)))
    branch = low_back(matmul(attended, out_weight) + out_bias)
    middle = inputs + branch
    second_norm = low(layer_norm(middle, ln2_gain, ln2_bias))
    hidden_pre = low_back(matmul(second_norm, fc_weight) + fc_bias)
    activated = low(jax.nn.gelu(hidden_pre, approximate=True))
    return middle + matmul(activated, proj_weight) + proj_bias

def reference(tokens, ln1_gain, ln1_bias, qkv_weight, qkv_bias, out_weight, out_bias, ln2_gain, ln2_bias, fc_weight, fc_bias, proj_weight, proj_bias, doc_blocks, cotangent):
    params = tuple((weight.astype(jnp.float32) for weight in (ln1_gain, ln1_bias, qkv_weight, qkv_bias, out_weight, out_bias, ln2_gain, ln2_bias, fc_weight, fc_bias, proj_weight, proj_bias)))
    count_rows = TOK_DEV * N_CTX
    inputs_all = tokens.astype(jnp.float32).reshape(N_GRP, count_rows, D)
    cotangent_all = cotangent.astype(jnp.float32).reshape(N_GRP, count_rows, D)

    def one_group(totals, pieces):
        inputs, incoming, doc_sizes = pieces
        doc_ids, positions = doc_layout(doc_sizes, TOK_DEV, N_CTX)
        order = jnp.argsort(doc_ids * count_rows + positions).astype(jnp.int32)
        undo = jnp.argsort(order).astype(jnp.int32)

        def forward(values, weights):
            return group_forward(values[order], weights, doc_ids[order], positions[order])[undo]
        result, pullback = jax.vjp(forward, inputs, params)
        grad_inputs, grad_params = pullback(incoming)
        return (tuple((total + part for total, part in zip(totals, grad_params))), (result, grad_inputs))
    zeros = tuple((jnp.zeros_like(weight) for weight in params))
    totals, (results, grad_inputs) = lax.scan(one_group, zeros, (inputs_all, cotangent_all, doc_blocks))
    return (results.reshape(TOKENS, D), grad_inputs.reshape(TOKENS, D), totals[0], totals[1], totals[2], totals[3], totals[4], totals[5], totals[6], totals[7], totals[8], totals[9], totals[10], totals[11])
```

```python
import functools
import math

import jax
import jax.numpy as jnp
from jax import lax
from jax.experimental import pallas as pl
from jax.experimental.pallas import tpu as pltpu
from jax.sharding import Mesh
from jax.sharding import PartitionSpec as P

HEADS = 12
SEQ_LEN = 2048
FAR = 1e30
F32 = jnp.float32
BF16 = jnp.bfloat16
GRP = ("gx", "core")
CTX = ("hg", "part")
VMEM_BYTES = 56 * 1024 * 1024


class Sizes:
    def __init__(self, rows, width, hidden, docs, n_ctx, n_grp):
        self.rows, self.width, self.hidden, self.docs = rows, width, hidden, docs
        self.n_ctx, self.n_grp = n_ctx, n_grp
        self.head = width // HEADS
        self.block = min(rows // 2, SEQ_LEN // n_ctx)
        self.parts = rows // self.block
        self.groups = n_ctx // self.parts
        self.grain = self.block // 4
        self.grains = rows // self.grain
        self.per = -(-HEADS // self.groups)
        self.used = self.per * self.head
        self.lanes = -(-((self.per + 1) * self.head) // 128) * 128
        self.span = n_ctx * self.block
        self.tile = 256
        self.steps = self.span // self.tile
        self.gx = n_grp // 2
        self.scale = self.head ** (-0.5)


def dot(a, b):
    return lax.dot_general(a, b, (((1,), (0,)), ((), ())), preferred_element_type=F32)


def dot_nt(a, b):
    return lax.dot_general(a, b, (((1,), (1,)), ((), ())), preferred_element_type=F32)


def dot_tn(a, b):
    return lax.dot_general(a, b, (((0,), (0,)), ((), ())), preferred_element_type=F32)


def dot_split(mask, value, transposed):
    high = value.astype(BF16)
    low = (value - high.astype(F32)).astype(BF16)
    mul = dot_tn if transposed else dot
    return mul(mask, high) + mul(mask, low)


def shift(value, axis, size, step):
    return lax.ppermute(value, axis, [(i, (i + step) % size) for i in range(size)])


def whole_call(body, outs, n_scalars, args, name, scratch=(), flops=0, moved=0):
    specs = [pl.BlockSpec(memory_space=pltpu.SMEM)] * n_scalars
    specs += [pl.BlockSpec(memory_space=pltpu.VMEM)] * (len(args) - n_scalars)
    return pl.pallas_call(
        body,
        out_shape=[jax.ShapeDtypeStruct(s, t) for s, t in outs],
        in_specs=specs,
        out_specs=[pl.BlockSpec(memory_space=pltpu.VMEM)] * len(outs),
        scratch_shapes=list(scratch),
        compiler_params=pltpu.CompilerParams(vmem_limit_bytes=VMEM_BYTES),
        name=name,
    )(*args)


def source_grain(sz, doc_ref, place):
    is_long = [(doc_ref[0, d] == sz.block).astype(jnp.int32) for d in range(sz.docs)]
    longs = sum(is_long)
    seen_long, seen_short, begin, source = 0, 0, 0, 0
    for d in range(sz.docs):
        count = doc_ref[0, d] // sz.grain
        first = jnp.where(is_long[d] == 1, 4 * seen_long, 4 * longs + seen_short)
        inside = (place >= first) & (place < first + count)
        source = source + jnp.where(inside, begin + place - first, 0)
        seen_long = seen_long + is_long[d]
        seen_short = seen_short + jnp.where(is_long[d] == 1, 0, count)
        begin = begin + count
    return source


def part_is_long(sz, doc_ref, part):
    longs = sum((doc_ref[0, d] == sz.block).astype(jnp.int32) for d in range(sz.docs))
    return part < longs


def sort_rows(sz, place, docs, tokens, cotangent):
    def body(place_ref, doc_ref, tok_ref, cot_ref, *outs):
        part = place_ref[1]
        for s in range(sz.parts):
            base = 4 * ((part + s) % sz.parts)
            for a in range(4):
                src = source_grain(sz, doc_ref, base + a)
                at = pl.ds(a * sz.grain, sz.grain)
                outs[s][at, :] = tok_ref[src]
                outs[sz.parts + s][at, :] = cot_ref[src]

    shape = (sz.grains, sz.grain, sz.width)
    out = whole_call(
        body,
        [((sz.block, sz.width), BF16)] * (2 * sz.parts),
        2,
        (place, docs, tokens.reshape(shape), cotangent.reshape(shape)),
        "sort_rows",
    )
    return out[: sz.parts], out[sz.parts :]


def normalize(x):
    center = x - jnp.mean(x, axis=-1, keepdims=True)
    spread = jnp.mean(center * center, axis=-1, keepdims=True)
    r = lax.rsqrt(spread + 1e-05)
    return center * r, r


def pair_masks(sz, step, long_part):
    keys = (step + 1) * sz.tile
    q_row = step * sz.tile + lax.broadcasted_iota(jnp.int32, (sz.tile, 1), 0)
    k_row = lax.broadcasted_iota(jnp.int32, (1, keys), 1)
    q_doc = jnp.where(long_part, 0, (q_row % sz.block) // sz.grain)
    k_doc = jnp.where(long_part, 0, (k_row % sz.block) // sz.grain)
    k_in = jnp.where(long_part, k_row % sz.block, k_row % sz.grain)
    first = (k_row < sz.block) & (k_in == 0)
    same = q_doc == k_doc
    visible = same & (k_row <= q_row)
    select = same & (k_row < q_row) & jnp.logical_not(first)
    return visible, select


def slot_mask(sz, slot):
    lane = lax.broadcasted_iota(jnp.int32, (1, sz.lanes), 1)
    return lane // sz.head == slot


def lower_mask(sz):
    row = lax.broadcasted_iota(jnp.int32, (sz.tile, sz.tile), 0)
    col = lax.broadcasted_iota(jnp.int32, (sz.tile, sz.tile), 1)
    return jnp.where(row > col, 1.0, 0.0).astype(BF16)


def penalty_of(sz, step, long_part, lower, q_slot, k, carry):
    visible, select = pair_masks(sz, step, long_part)
    positive = jnp.maximum(dot_nt(q_slot, k), 0.0)
    chosen = jnp.where(select, positive * positive * (1.0 / sz.block), 0.0)
    penalty = dot_split(lower, chosen, False) + carry
    return jnp.where(visible, penalty, FAR), chosen, positive, select


def attend_forward(sz, place, docs, chunks, gain, bias, w_sel, b_sel):
    n_in = len(chunks)
    lw = sz.lanes

    def body(place_ref, doc_ref, *refs):
        xs = refs[:n_in]
        gain_ref, bias_ref, w_ref, b_ref = refs[n_in : n_in + 4]
        qkv_ref, normed_ref, hat_ref, lse_ref, out_ref, carry_ref = refs[n_in + 4 : n_in + 10]
        att_refs = refs[n_in + 10 : n_in + 10 + sz.groups]
        hg, part = place_ref[0], place_ref[1]
        long_part = part_is_long(sz, doc_ref, part)
        for k in range(sz.groups):
            for s in range(sz.parts):
                at = ((hg - k) % sz.groups) * sz.parts + (part - s) % sz.parts
                at = pl.ds(pl.multiple_of(at * sz.block, sz.block), sz.block)
                hat, _ = normalize(xs[k * sz.parts + s][...].astype(F32))
                normed = (hat * gain_ref[...] + bias_ref[...]).astype(BF16)
                hat_ref[at, :] = hat.astype(BF16)
                normed_ref[at, :] = normed
                qkv_ref[at, :] = (dot(normed, w_ref[...]) + b_ref[...]).astype(BF16)
        lower = lower_mask(sz)
        lane = lax.broadcasted_iota(jnp.int32, (1, 128), 1)
        carry_ref[...] = jnp.zeros_like(carry_ref)
        for step in range(sz.steps):
            keys = (step + 1) * sz.tile
            rows = slice(step * sz.tile, keys)
            q = qkv_ref[rows, :lw] * sz.scale
            k = qkv_ref[:keys, lw : 2 * lw]
            v = qkv_ref[:keys, 2 * lw :]
            q_slot = jnp.where(slot_mask(sz, sz.per), q, 0)
            pen, chosen, _, _ = penalty_of(
                sz, step, long_part, lower, q_slot, k, carry_ref[step : step + 1, :keys]
            )
            if step + 1 < sz.steps:
                carry_ref[step + 1 : step + 2, :keys] = carry_ref[step : step + 1, :keys] + jnp.sum(
                    chosen, axis=0, keepdims=True
                )
            total = jnp.zeros((sz.tile, lw), F32)
            lse = jnp.zeros((sz.tile, 128), F32)
            for h in range(sz.per):
                mask = slot_mask(sz, h)
                logits = dot_nt(jnp.where(mask, q, 0), k) - pen
                top = jnp.max(logits, axis=1, keepdims=True)
                weights = jnp.exp(logits - top)
                weight = jnp.sum(weights, axis=1, keepdims=True)
                mixed = dot(weights.astype(BF16), v) / weight
                total = jnp.where(mask, mixed, total)
                lse = jnp.where(lane == h, top + jnp.log(weight), lse)
            out_ref[rows, :] = total
            lse_ref[rows, :] = lse
        for k in range(sz.groups):
            at = pl.multiple_of(((hg + k) % sz.groups) * sz.rows, sz.rows)
            att_refs[k][...] = out_ref[pl.ds(at, sz.rows), : sz.used].astype(BF16)

    outs = [
        ((sz.span, 3 * lw), BF16),
        ((sz.span, sz.width), BF16),
        ((sz.span, sz.width), BF16),
        ((sz.span, 128), F32),
        ((sz.span, lw), F32),
        ((sz.steps, sz.span), F32),
    ] + [((sz.rows, sz.used), BF16)] * sz.groups
    out = whole_call(body, outs, 2, (place, docs, *chunks, gain, bias, w_sel, b_sel), "attend_forward")
    return out[:6], out[6:]


def attend_backward(sz, place, docs, saved, w_sel, grads):
    lw = sz.lanes
    qkv, _, hat, lse, att, carry = saved

    def body(place_ref, doc_ref, qkv_ref, hat_ref, lse_ref, att_ref, carry_ref, w_ref, *refs):
        grad_refs = refs[: sz.groups]
        outs = refs[sz.groups :]
        dqkv_ref, sums_ref, lnsum_ref = outs[:3]
        dnorm_refs = outs[3 : 3 + sz.n_ctx]
        dout, dk_sum, dv_sum, behind = outs[3 + sz.n_ctx :]
        hg, part = place_ref[0], place_ref[1]
        long_part = part_is_long(sz, doc_ref, part)
        dout[...] = jnp.zeros_like(dout)
        for k in range(sz.groups):
            at = pl.multiple_of(((hg - k) % sz.groups) * sz.rows, sz.rows)
            dout[pl.ds(at, sz.rows), : sz.used] = grad_refs[k][...]
        dk_sum[...] = jnp.zeros_like(dk_sum)
        dv_sum[...] = jnp.zeros_like(dv_sum)
        behind[...] = jnp.zeros_like(behind)
        lower = lower_mask(sz)
        for step in reversed(range(sz.steps)):
            keys = (step + 1) * sz.tile
            rows = slice(step * sz.tile, keys)
            q = qkv_ref[rows, :lw] * sz.scale
            k = qkv_ref[:keys, lw : 2 * lw]
            v = qkv_ref[:keys, 2 * lw :]
            d_rows = dout[rows, :]
            dot_rows = d_rows.astype(F32) * att_ref[rows, :]
            last = slot_mask(sz, sz.per)
            q_slot = jnp.where(last, q, 0)
            pen, _, positive, select = penalty_of(
                sz, step, long_part, lower, q_slot, k, carry_ref[step : step + 1, :keys]
            )
            dpen = jnp.zeros((sz.tile, keys), F32)
            dq = jnp.zeros((sz.tile, lw), F32)
            for h in range(sz.per):
                mask = slot_mask(sz, h)
                q_h = jnp.where(mask, q, 0)
                d_h = jnp.where(mask, d_rows, 0)
                probs = jnp.exp(dot_nt(q_h, k) - pen - lse_ref[rows, h : h + 1])
                delta = jnp.sum(jnp.where(mask, dot_rows, 0.0), axis=1, keepdims=True)
                ds = probs * (dot_nt(d_h, v) - delta)
                dpen = dpen - ds
                ds_low = ds.astype(BF16)
                dq = jnp.where(mask, dot(ds_low, k), dq)
                dk_sum[:keys, :] += dot_tn(ds_low, q_h)
                dv_sum[:keys, :] += dot_tn(probs.astype(BF16), d_h)
            dchosen = dot_split(lower, dpen, True) + behind[:1, :keys]
            behind[:1, :keys] += jnp.sum(dpen, axis=0, keepdims=True)
            ds_low = jnp.where(select, positive * dchosen * (2.0 / sz.block), 0.0).astype(BF16)
            dq = jnp.where(last, dot(ds_low, k), dq)
            dk_sum[:keys, :] += dot_tn(ds_low, q_slot)
            dqkv_ref[rows, :lw] = (dq * sz.scale).astype(BF16)
        dqkv_ref[:, lw : 2 * lw] = dk_sum[...].astype(BF16)
        dqkv_ref[:, 2 * lw :] = dv_sum[...].astype(BF16)
        sums_ref[...] = jnp.sum(dqkv_ref[...].astype(F32), axis=0, keepdims=True)
        gain_sum = jnp.zeros((1, sz.width), F32)
        bias_sum = jnp.zeros((1, sz.width), F32)
        for k in range(sz.groups):
            for s in range(sz.parts):
                at = ((hg + k) % sz.groups) * sz.parts + (part + s) % sz.parts
                at = pl.ds(pl.multiple_of(at * sz.block, sz.block), sz.block)
                dnorm = dot_nt(dqkv_ref[at, :], w_ref[...])
                dnorm_refs[k * sz.parts + s][...] = dnorm.astype(BF16)
                bias_sum += jnp.sum(dnorm, axis=0, keepdims=True)
                gain_sum += jnp.sum(dnorm * hat_ref[at, :].astype(F32), axis=0, keepdims=True)
        lnsum_ref[0:1, :] = gain_sum
        lnsum_ref[1:2, :] = bias_sum

    outs = [((sz.span, 3 * lw), BF16), ((1, 3 * lw), F32), ((2, sz.width), F32)]
    outs += [((sz.block, sz.width), BF16)] * sz.n_ctx
    scratch = [
        pltpu.VMEM((sz.span, lw), BF16),
        pltpu.VMEM((sz.span, lw), F32),
        pltpu.VMEM((sz.span, lw), F32),
        pltpu.VMEM((8, sz.span), F32),
    ]
    out = whole_call(
        body, outs, 2, (place, docs, qkv, hat, lse, att, carry, w_sel, *grads), "attend_backward", scratch
    )
    return out[0], out[1], out[2], out[3:]


def project_out(sz, place, att, tokens, out_weight, out_bias, gain, bias):
    def body(place_ref, *refs):
        att_refs = refs[: sz.groups]
        tok_refs = refs[sz.groups : sz.groups + sz.parts]
        w_ref, b_ref, gain_ref, bias_ref, middle_ref, second_ref = refs[sz.groups + sz.parts :]
        hg, part = place_ref[0], place_ref[1]
        for s in range(sz.parts):
            at = pl.ds(pl.multiple_of(((part - s) % sz.parts) * sz.block, sz.block), sz.block)
            middle_ref[at, :] = tok_refs[s][...].astype(F32) + b_ref[...]
        total = middle_ref[...]
        for k in range(sz.groups):
            at = pl.multiple_of(((hg - k) % sz.groups) * sz.used, 16)
            total += dot(att_refs[k][...], w_ref[pl.ds(at, sz.used), :])
        middle_ref[...] = total
        hat, _ = normalize(total)
        second_ref[...] = (hat * gain_ref[...] + bias_ref[...]).astype(BF16)

    outs = [((sz.rows, sz.width), F32), ((sz.rows, sz.width), BF16)]
    return whole_call(
        body, outs, 1, (place, *att, *tokens, out_weight, out_bias, gain, bias), "project_out"
    )


def feed_forward(sz, second, cot, fc, fc_bias, proj):
    rows, width = second.shape
    units = fc.shape[1]
    step = sz.rows
    root = math.sqrt(2.0 / math.pi)

    def body(second_ref, cot_ref, fc_ref, bias_ref, proj_ref, act_ref, grad_ref, back_ref, sums_ref):
        hidden = dot(second_ref[...], fc_ref[...]) + bias_ref[...]
        square = hidden * hidden
        t = jnp.tanh(root * (hidden + 0.044715 * hidden * square))
        half = 0.5 * (1.0 + t)
        act_ref[...] = (hidden * half).astype(BF16)
        slope = half + 0.5 * hidden * (1.0 - t * t) * (root * (1.0 + 3.0 * 0.044715 * square))
        grad = (dot_nt(cot_ref[...], proj_ref[...]) * slope).astype(BF16)
        grad_ref[...] = grad
        back_ref[...] = dot_nt(grad, fc_ref[...]).astype(BF16)

        @pl.when(pl.program_id(0) == 0)
        def _():
            sums_ref[...] = jnp.zeros_like(sums_ref)

        sums_ref[...] += jnp.sum(grad.astype(F32), axis=0, keepdims=True)

    def moving(n):
        return pl.BlockSpec((step, n), lambda i: (i, 0))

    def fixed(*shape):
        return pl.BlockSpec(shape, lambda i: (0, 0))

    return pl.pallas_call(
        body,
        grid=(rows // step,),
        out_shape=[
            jax.ShapeDtypeStruct((rows, units), BF16),
            jax.ShapeDtypeStruct((rows, units), BF16),
            jax.ShapeDtypeStruct((rows, width), BF16),
            jax.ShapeDtypeStruct((1, units), F32),
        ],
        in_specs=[
            moving(width),
            moving(width),
            fixed(width, units),
            fixed(1, units),
            fixed(units, width),
        ],
        out_specs=[moving(units), moving(units), moving(width), fixed(1, units)],
        compiler_params=pltpu.CompilerParams(vmem_limit_bytes=VMEM_BYTES),
        name="feed_forward",
    )(second, cot, fc, fc_bias, proj)


def middle_backward(sz, place, back, middle, cot, out_weight, gain):
    n_back = len(back)

    def body(place_ref, *refs):
        back_refs = refs[:n_back]
        cot_refs = refs[n_back : n_back + sz.parts]
        rest = refs[n_back + sz.parts :]
        middle_ref, w_ref, gain_ref = rest[:3]
        branch_ref, sums_ref = rest[3:5]
        gm_refs = rest[5 : 5 + sz.parts]
        datt_refs = rest[5 + sz.parts : 5 + sz.parts + sz.groups]
        total = rest[-1]
        hg, part = place_ref[0], place_ref[1]
        cot_sum = jnp.zeros((1, sz.width), F32)
        for s in range(sz.parts):
            at = pl.ds(pl.multiple_of(((part - s) % sz.parts) * sz.block, sz.block), sz.block)
            block = cot_refs[s][...].astype(F32)
            total[at, :] = block
            cot_sum += jnp.sum(block, axis=0, keepdims=True)
        e = back_refs[0][...].astype(F32)
        for ref in back_refs[1:]:
            e += ref[...].astype(F32)
        hat, r = normalize(middle_ref[...])
        eg = e * gain_ref[...]
        inner = eg - jnp.mean(eg, axis=-1, keepdims=True)
        inner -= hat * jnp.mean(eg * hat, axis=-1, keepdims=True)
        grad = total[...] + r * inner
        total[...] = grad
        branch = grad.astype(BF16)
        branch_ref[...] = branch
        for s in range(sz.parts):
            at = pl.ds(pl.multiple_of(((part + s) % sz.parts) * sz.block, sz.block), sz.block)
            gm_refs[s][...] = total[at, :]
        for k in range(sz.groups):
            at = pl.multiple_of(((hg + k) % sz.groups) * sz.used, 16)
            datt_refs[k][...] = dot_nt(branch, w_ref[pl.ds(at, sz.used), :]).astype(BF16)
        sums_ref[0:1, :] = jnp.sum(e * hat, axis=0, keepdims=True)
        sums_ref[1:2, :] = jnp.sum(e, axis=0, keepdims=True)
        sums_ref[2:3, :] = jnp.sum(branch.astype(F32), axis=0, keepdims=True)
        sums_ref[3:4, :] = cot_sum

    outs = [((sz.rows, sz.width), BF16), ((4, sz.width), F32)]
    outs += [((sz.block, sz.width), F32)] * sz.parts
    outs += [((sz.rows, sz.used), BF16)] * sz.groups
    out = whole_call(
        body,
        outs,
        1,
        (place, *back, *cot, middle, out_weight, gain),
        "middle_backward",
        [pltpu.VMEM((sz.rows, sz.width), F32)],
    )
    split = 2 + sz.parts
    return out[0], out[1], out[2:split], out[split:]


def finish_tokens(sz, place, docs, dnorm, tokens, grad_middle, gain):
    n = len(dnorm)

    def body(place_ref, doc_ref, *refs):
        d_refs = refs[:n]
        tok_refs = refs[n : n + sz.parts]
        gm_refs = refs[n + sz.parts : n + 2 * sz.parts]
        gain_ref, out_ref, held = refs[n + 2 * sz.parts :]
        part = place_ref[1]
        for s in range(sz.parts):
            e = d_refs[s][...].astype(F32)
            for k in range(1, sz.groups):
                e += d_refs[k * sz.parts + s][...].astype(F32)
            hat, r = normalize(tok_refs[(-s) % sz.parts][...].astype(F32))
            eg = e * gain_ref[...]
            inner = eg - jnp.mean(eg, axis=-1, keepdims=True)
            inner -= hat * jnp.mean(eg * hat, axis=-1, keepdims=True)
            held[...] = gm_refs[s][...] + r * inner
            base = 4 * ((part - s) % sz.parts)
            for a in range(4):
                src = source_grain(sz, doc_ref, base + a)
                out_ref[src] = held[pl.ds(a * sz.grain, sz.grain), :]

    out = whole_call(
        body,
        [((sz.grains, sz.grain, sz.width), F32)],
        2,
        (place, docs, *dnorm, *tokens, *grad_middle, gain),
        "finish_tokens",
        [pltpu.VMEM((sz.block, sz.width), F32)],
    )
    return out[0].reshape(sz.rows, sz.width)


def finish_middle(sz, place, mixed, middle, proj_bias):
    n = len(mixed)

    def body(place_ref, *refs):
        middle_ref, bias_ref = refs[n : n + 2]
        outs = refs[n + 2 :]
        part = place_ref[1]
        for s in range(sz.parts):
            at = pl.ds(pl.multiple_of(((part + s) % sz.parts) * sz.block, sz.block), sz.block)
            total = middle_ref[at, :] + bias_ref[...]
            for ref in refs[:n]:
                total += ref[at, :].astype(F32)
            outs[s][...] = total

    return whole_call(
        body,
        [((sz.block, sz.width), F32)] * sz.parts,
        1,
        (place, *mixed, middle, proj_bias),
        "finish_middle",
    )


def unsort_rows(sz, place, docs, blocks):
    def body(place_ref, doc_ref, *refs):
        out_ref = refs[-1]
        part = place_ref[1]
        for s in range(sz.parts):
            base = 4 * ((part - s) % sz.parts)
            for a in range(4):
                src = source_grain(sz, doc_ref, base + a)
                out_ref[src] = refs[s][pl.ds(a * sz.grain, sz.grain), :]

    out = whole_call(
        body,
        [((sz.grains, sz.grain, sz.width), F32)],
        2,
        (place, docs, *blocks),
        "unsort_rows",
    )
    return out[0].reshape(sz.rows, sz.width)


def gather_rows(sz, block):
    along = [block] + [shift(block, "gx", sz.gx, k) for k in range(1, sz.gx)]
    mine = jnp.concatenate(along, axis=0)
    other = shift(mine, "core", 2, 1)
    return jnp.concatenate([mine, other], axis=0)


def return_rows(sz, summed):
    half = sz.gx * sz.rows
    other = shift(summed[half:], "core", 2, 1)
    mine = summed[:half].astype(F32) + other.astype(F32)
    blocks = [mine[: sz.rows]]
    for k in range(1, sz.gx):
        blocks.append(shift(mine[k * sz.rows : (k + 1) * sz.rows].astype(BF16), "gx", sz.gx, -k))
    return blocks


def head_columns(sz, weight, hg):
    lead = weight.shape[:-1]
    pieces = []
    for third in range(3):
        full = weight[..., third * sz.width : (third + 1) * sz.width]
        spare = sz.groups * sz.used - sz.width
        if spare:
            full = jnp.pad(full, [(0, 0)] * len(lead) + [(0, spare)])
        own = lax.dynamic_slice_in_dim(full, hg * sz.used, sz.used, axis=len(lead))
        first = full[..., : sz.head] if third < 2 else jnp.zeros(lead + (sz.head,), weight.dtype)
        rest = sz.lanes - sz.used - sz.head
        pieces += [own, first]
        if rest:
            pieces.append(jnp.zeros(lead + (rest,), weight.dtype))
    return jnp.concatenate(pieces, axis=-1)


def body(
    tokens,
    ln1_gain,
    ln1_bias,
    qkv_weight,
    qkv_bias,
    out_weight,
    out_bias,
    ln2_gain,
    ln2_bias,
    fc_weight,
    fc_bias,
    proj_weight,
    proj_bias,
    doc_blocks,
    cotangent,
):
    rows, width = tokens.shape
    hidden = fc_weight.shape[1]
    n_ctx = lax.axis_size("hg") * lax.axis_size("part")
    n_grp = lax.axis_size("gx") * 2
    sz = Sizes(rows, width, hidden, doc_blocks.shape[1], n_ctx, n_grp)
    hg, part = lax.axis_index("hg"), lax.axis_index("part")
    gx, core = lax.axis_index("gx"), lax.axis_index("core")
    place = jnp.stack([hg, part]).astype(jnp.int32)

    def vector(v):
        return v.astype(F32)[None, :]

    gain1, bias1 = vector(ln1_gain), vector(ln1_bias)
    gain2, bias2 = vector(ln2_gain), vector(ln2_bias)

    tok_parts, cot_parts = sort_rows(sz, place, doc_blocks, tokens, cotangent)
    tok_mine = [tok_parts[0]] + [shift(tok_parts[s], "part", sz.parts, s) for s in range(1, sz.parts)]
    order = sorted(range(1, sz.groups), key=lambda k: -min(k, sz.groups - k))
    chunks = {(0, s): tok_mine[s] for s in range(sz.parts)}
    for s in range(sz.parts):
        for k in order:
            chunks[k, s] = shift(tok_mine[s], "hg", sz.groups, k)
    chunks = [chunks[k, s] for k in range(sz.groups) for s in range(sz.parts)]
    cot_mine = [cot_parts[0]] + [shift(cot_parts[s], "part", sz.parts, s) for s in range(1, sz.parts)]

    w_sel = head_columns(sz, qkv_weight, hg)
    b_sel = head_columns(sz, vector(qkv_bias), hg)
    spare = sz.groups * sz.used - sz.width
    w_out = jnp.pad(out_weight, ((0, spare), (0, 0))) if spare else out_weight
    share = hidden // (n_ctx * n_grp)
    mine = gx * 2 + core
    fc = lax.dynamic_index_in_dim(
        fc_weight.reshape(width, n_ctx, n_grp, share), mine, 2, keepdims=False
    ).reshape(width, n_ctx * share)
    fc_b = lax.dynamic_index_in_dim(
        vector(fc_bias).reshape(1, n_ctx, n_grp, share), mine, 2, keepdims=False
    ).reshape(1, n_ctx * share)
    proj = lax.dynamic_index_in_dim(
        proj_weight.reshape(n_ctx, n_grp, share, width), mine, 1, keepdims=False
    ).reshape(n_ctx * share, width)

    cot_rows = jnp.concatenate(
        [
            lax.dynamic_index_in_dim(jnp.stack(cot_mine), (part - j) % sz.parts, 0, keepdims=False)
            for j in range(sz.parts)
        ],
        axis=0,
    )
    cot_all = gather_rows(sz, cot_rows)

    saved, att_out = attend_forward(sz, place, doc_blocks, chunks, gain1, bias1, w_sel, b_sel)
    att = [att_out[0]] + [shift(att_out[k], "hg", sz.groups, k) for k in range(1, sz.groups)]
    middle, second = project_out(sz, place, att, tok_mine, w_out, vector(out_bias), gain2, bias2)

    second_all = gather_rows(sz, second)
    act, grad_hidden, back, fc_sum = feed_forward(sz, second_all, cot_all, fc, fc_b, proj)
    back = return_rows(sz, back)
    branch, mid_sums, gm_parts, datt_out = middle_backward(sz, place, back, middle, cot_mine, w_out, gain2)
    datt = [datt_out[0]] + [shift(datt_out[k], "hg", sz.groups, k) for k in range(1, sz.groups)]

    mixed = return_rows(sz, dot(act, proj).astype(BF16))
    out_parts = finish_middle(sz, place, mixed, middle, vector(proj_bias))
    out_mine = [out_parts[0]] + [shift(out_parts[s], "part", sz.parts, s) for s in range(1, sz.parts)]
    output = unsort_rows(sz, place, doc_blocks, out_mine)
    gm_mine = [gm_parts[0]] + [shift(gm_parts[s], "part", sz.parts, s) for s in range(1, sz.parts)]

    band = width // n_ctx
    half = width // 2
    d_fc = dot_tn(second_all, grad_hidden).astype(BF16).reshape(n_ctx, band, n_ctx * share)
    d_proj = dot_tn(act, cot_all).astype(BF16).reshape(n_ctx, share, width)
    att_rows = jnp.concatenate(
        [
            lax.dynamic_index_in_dim(jnp.stack(att), (hg - j) % sz.groups, 0, keepdims=False)
            for j in range(sz.groups)
        ],
        axis=1,
    )[:, :width]
    d_out = dot_tn(att_rows, branch).astype(BF16)

    def core_half(full):
        other = lax.dynamic_slice_in_dim(full, (1 - core) * half, half, axis=1)
        own = lax.dynamic_slice_in_dim(full, core * half, half, axis=1)
        return own.astype(F32) + shift(other, "core", 2, 1).astype(F32)

    d_out = core_half(d_out).astype(BF16).reshape(n_ctx, band, half)
    packed = jnp.concatenate(
        [d_fc.reshape(n_ctx, -1), d_proj.reshape(n_ctx, -1), d_out.reshape(n_ctx, -1)], axis=1
    )
    packed = packed.reshape(n_ctx, -1, 128)
    packed = lax.psum_scatter(packed, CTX, scatter_dimension=0)
    n_fc = band * n_ctx * share // 128
    n_proj = share * width // 128
    ff_share = packed[: n_fc + n_proj]
    out_share = packed[n_fc + n_proj :].astype(F32)
    out_share = out_share + sum(shift(packed[n_fc + n_proj :], "gx", sz.gx, k).astype(F32) for k in range(1, sz.gx))
    ff_all = lax.all_gather(ff_share, GRP)
    grad_fc = ff_all[:, :n_fc].reshape(n_grp, band, n_ctx, share).transpose(1, 2, 0, 3).reshape(band, hidden)
    grad_proj = ff_all[:, n_fc:].reshape(n_grp * share, width)
    out_pair = lax.all_gather(out_share.astype(BF16), "core").reshape(2, band, half)
    grad_out = out_pair.transpose(1, 0, 2).reshape(band, width)

    dqkv, qkv_sum, ln1_sums, dnorm_out = attend_backward(sz, place, doc_blocks, saved, w_sel, datt)
    dnorm = []
    for k in range(sz.groups):
        for s in range(sz.parts):
            step = lambda i: ((i // sz.parts + k) % sz.groups) * sz.parts + (i % sz.parts + s) % sz.parts
            block = dnorm_out[k * sz.parts + s]
            if k or s:
                block = lax.ppermute(block, CTX, [(i, step(i)) for i in range(n_ctx)])
            dnorm.append(block)
    grad_tokens = finish_tokens(sz, place, doc_blocks, dnorm, tok_parts, gm_mine, gain1)

    normed = saved[1]
    d_sel = dot_tn(normed, dqkv)
    w3 = 3 * sz.lanes
    d_sel = lax.all_to_all(d_sel.astype(BF16).reshape(n_ctx, band, w3), CTX, 0, 0, tiled=True)
    d_sel = d_sel.astype(F32).reshape(sz.groups, sz.parts, band, w3).sum(axis=1)
    d_sel = lax.psum(d_sel, GRP)

    def join_heads(sel):
        n = sel.shape[1]
        thirds = sel.reshape(sz.groups, n, 3, sz.lanes)
        own = thirds[..., : sz.used].transpose(2, 1, 0, 3).reshape(3, n, sz.groups * sz.used)
        own = own[..., : sz.width]
        first = thirds[..., sz.used : sz.used + sz.head].sum(axis=0).transpose(1, 0, 2)
        own = own.at[:, :, : sz.head].add(first)
        return own.transpose(1, 0, 2).reshape(n, 3 * sz.width)

    grad_qkv = join_heads(d_sel)

    placed = jnp.zeros((sz.groups, 1, w3), F32)
    placed = lax.dynamic_update_slice(placed, qkv_sum[None], (hg, 0, 0))
    fc_placed = jnp.zeros((n_ctx, n_grp, share), F32)
    fc_placed = lax.dynamic_update_slice(fc_placed, fc_sum.reshape(n_ctx, 1, share), (0, mine, 0))
    vectors = [
        ln1_sums[0],
        ln1_sums[1],
        join_heads(placed)[0],
        mid_sums[2],
        mid_sums[0],
        mid_sums[1],
        fc_placed.reshape(-1),
        mid_sums[3],
    ]
    small = jnp.concatenate([v.reshape(n_ctx, -1) for v in vectors], axis=1)
    small = lax.all_to_all(small, CTX, 0, 0, tiled=True).sum(axis=0)
    small = lax.psum(small, GRP)
    cuts, at = [], 0
    for v in vectors:
        n = v.shape[0] // n_ctx
        cuts.append(small[at : at + n])
        at += n
    g_ln1_gain, g_ln1_bias, g_qkv_bias, g_out_bias, g_ln2_gain, g_ln2_bias, g_fc_bias, g_proj_bias = cuts
    return (
        output,
        grad_tokens,
        g_ln1_gain,
        g_ln1_bias,
        grad_qkv,
        g_qkv_bias,
        grad_out.astype(F32),
        g_out_bias,
        g_ln2_gain,
        g_ln2_bias,
        grad_fc.astype(F32),
        g_fc_bias,
        grad_proj.astype(F32),
        g_proj_bias,
    )


def solution(mesh):
    n_grp, n_ctx = mesh.devices.shape
    split = P(GRP + CTX, None)

    def run(tokens, *rest):
        rows = tokens.shape[0] // (n_grp * n_ctx)
        parts = rows // min(rows // 2, SEQ_LEN // n_ctx)
        fine = Mesh(mesh.devices.reshape(n_grp // 2, 2, n_ctx // parts, parts), GRP + CTX)
        each = jax.shard_map(
            body,
            mesh=fine,
            in_specs=(split,) + (P(),) * 12 + (P(GRP, None), split),
            out_specs=(
                split,
                split,
                P(CTX),
                P(CTX),
                P(CTX, None),
                P(CTX),
                P(CTX, None),
                P(CTX),
                P(CTX),
                P(CTX),
                P(CTX, None),
                P(CTX),
                P(CTX, None),
                P(CTX),
            ),
            check_vma=False,
        )
        return each(tokens, *rest)

    return run
```

```python
import functools
import math

import jax
import jax.numpy as jnp
from jax import lax
from jax.experimental import pallas as pl
from jax.experimental.pallas import tpu as pltpu
from jax.sharding import Mesh
from jax.sharding import PartitionSpec as P

HEADS = 12
SEQ_LEN = 2048
FAR = 1e30
F32 = jnp.float32
BF16 = jnp.bfloat16
GRP = ("gx", "core")
CTX = ("hg", "part")
VMEM_BYTES = 56 * 1024 * 1024


class Sizes:
    def __init__(self, rows, width, hidden, docs, n_ctx, n_grp):
        self.rows, self.width, self.hidden, self.docs = rows, width, hidden, docs
        self.n_ctx, self.n_grp = n_ctx, n_grp
        self.head = width // HEADS
        self.block = min(rows // 2, SEQ_LEN // n_ctx)
        self.parts = rows // self.block
        self.groups = n_ctx // self.parts
        self.grain = self.block // 4
        self.grains = rows // self.grain
        self.per = -(-HEADS // self.groups)
        self.used = self.per * self.head
        self.lanes = -(-((self.per + 1) * self.head) // 128) * 128
        self.span = n_ctx * self.block
        self.tile = 256
        self.steps = self.span // self.tile
        self.gx = n_grp // 2
        self.scale = self.head ** (-0.5)
        band, share = width // n_ctx, hidden // (n_ctx * n_grp)
        self.aligned = band % 32 == 0 and share % 32 == 0 and share * n_ctx == width
        self.packed = band % (16 * self.gx) == 0 and 3 * self.lanes == width


def dot(a, b):
    return lax.dot_general(a, b, (((1,), (0,)), ((), ())), preferred_element_type=F32)


def dot_nt(a, b):
    return lax.dot_general(a, b, (((1,), (1,)), ((), ())), preferred_element_type=F32)


def dot_tn(a, b):
    return lax.dot_general(a, b, (((0,), (0,)), ((), ())), preferred_element_type=F32)


def dot_split(mask, value, transposed):
    high = value.astype(BF16)
    low = (value - high.astype(F32)).astype(BF16)
    mul = dot_tn if transposed else dot
    return mul(mask, high) + mul(mask, low)


def shift(value, axis, size, step):
    return lax.ppermute(value, axis, [(i, (i + step) % size) for i in range(size)])


def cost(flops, *arrays):
    size = sum(math.prod(a.shape) * a.dtype.itemsize for a in arrays)
    return pl.CostEstimate(flops=int(flops), bytes_accessed=int(size), transcendentals=0)


def whole_call(body, outs, n_scalars, args, name, scratch=(), flops=0):
    shapes = [jax.ShapeDtypeStruct(s, t) for s, t in outs]
    specs = [pl.BlockSpec(memory_space=pltpu.SMEM)] * n_scalars
    specs += [pl.BlockSpec(memory_space=pltpu.VMEM)] * (len(args) - n_scalars)
    return pl.pallas_call(
        body,
        out_shape=shapes,
        in_specs=specs,
        out_specs=[pl.BlockSpec(memory_space=pltpu.VMEM)] * len(outs),
        scratch_shapes=list(scratch),
        compiler_params=pltpu.CompilerParams(vmem_limit_bytes=VMEM_BYTES),
        cost_estimate=cost(flops, *args, *shapes),
        name=name,
    )(*args)


def source_grain(sz, doc_ref, place):
    is_long = [(doc_ref[0, d] == sz.block).astype(jnp.int32) for d in range(sz.docs)]
    longs = sum(is_long)
    seen_long, seen_short, begin, source = 0, 0, 0, 0
    for d in range(sz.docs):
        count = doc_ref[0, d] // sz.grain
        first = jnp.where(is_long[d] == 1, 4 * seen_long, 4 * longs + seen_short)
        inside = (place >= first) & (place < first + count)
        source = source + jnp.where(inside, begin + place - first, 0)
        seen_long = seen_long + is_long[d]
        seen_short = seen_short + jnp.where(is_long[d] == 1, 0, count)
        begin = begin + count
    return source


def part_is_long(sz, doc_ref, part):
    longs = sum((doc_ref[0, d] == sz.block).astype(jnp.int32) for d in range(sz.docs))
    return part < longs


def sort_rows(sz, place, docs, tokens, cotangent):
    def body(place_ref, doc_ref, tok_ref, cot_ref, *outs):
        part = place_ref[1]
        for s in range(sz.parts):
            base = 4 * ((part + s) % sz.parts)
            for a in range(4):
                src = source_grain(sz, doc_ref, base + a)
                at = pl.ds(a * sz.grain, sz.grain)
                outs[s][at, :] = tok_ref[src]
                outs[sz.parts + s][at, :] = cot_ref[src]

    shape = (sz.grains, sz.grain, sz.width)
    out = whole_call(
        body,
        [((sz.block, sz.width), BF16)] * (2 * sz.parts),
        2,
        (place, docs, tokens.reshape(shape), cotangent.reshape(shape)),
        "sort_rows",
    )
    return out[: sz.parts], out[sz.parts :]


def normalize(x):
    center = x - jnp.mean(x, axis=-1, keepdims=True)
    spread = jnp.mean(center * center, axis=-1, keepdims=True)
    r = lax.rsqrt(spread + 1e-05)
    return center * r, r


def pair_masks(sz, step, long_part):
    keys = (step + 1) * sz.tile
    q_row = step * sz.tile + lax.broadcasted_iota(jnp.int32, (sz.tile, 1), 0)
    k_row = lax.broadcasted_iota(jnp.int32, (1, keys), 1)
    q_doc = jnp.where(long_part, 0, (q_row % sz.block) // sz.grain)
    k_doc = jnp.where(long_part, 0, (k_row % sz.block) // sz.grain)
    k_in = jnp.where(long_part, k_row % sz.block, k_row % sz.grain)
    first = (k_row < sz.block) & (k_in == 0)
    same = q_doc == k_doc
    visible = same & (k_row <= q_row)
    select = same & (k_row < q_row) & jnp.logical_not(first)
    return visible, select


def slot_mask(sz, slot):
    lane = lax.broadcasted_iota(jnp.int32, (1, sz.lanes), 1)
    return lane // sz.head == slot


def lower_mask(sz):
    row = lax.broadcasted_iota(jnp.int32, (sz.tile, sz.tile), 0)
    col = lax.broadcasted_iota(jnp.int32, (sz.tile, sz.tile), 1)
    return jnp.where(row > col, 1.0, 0.0).astype(BF16)


def penalty_of(sz, step, long_part, lower, q_slot, k, carry):
    visible, select = pair_masks(sz, step, long_part)
    positive = jnp.maximum(dot_nt(q_slot, k), 0.0)
    chosen = jnp.where(select, positive * positive * (1.0 / sz.block), 0.0)
    penalty = dot_split(lower, chosen, False) + carry
    return jnp.where(visible, penalty, FAR), chosen, positive, select


def attend_forward(sz, place, docs, chunks, gain, bias, w_sel, b_sel):
    n_in = len(chunks)
    lw = sz.lanes

    def body(place_ref, doc_ref, *refs):
        xs = refs[:n_in]
        gain_ref, bias_ref, w_ref, b_ref = refs[n_in : n_in + 4]
        qkv_ref, normed_ref, hat_ref, lse_ref, out_ref, carry_ref = refs[n_in + 4 : n_in + 10]
        att_refs = refs[n_in + 10 : n_in + 10 + sz.groups]
        hg, part = place_ref[0], place_ref[1]
        long_part = part_is_long(sz, doc_ref, part)
        for k in range(sz.groups):
            for s in range(sz.parts):
                at = ((hg - k) % sz.groups) * sz.parts + (part - s) % sz.parts
                at = pl.ds(pl.multiple_of(at * sz.block, sz.block), sz.block)
                hat, _ = normalize(xs[k * sz.parts + s][...].astype(F32))
                normed = (hat * gain_ref[...] + bias_ref[...]).astype(BF16)
                hat_ref[at, :] = hat.astype(BF16)
                normed_ref[at, :] = normed
                qkv_ref[at, :] = (dot(normed, w_ref[...]) + b_ref[...]).astype(BF16)
        lower = lower_mask(sz)
        lane = lax.broadcasted_iota(jnp.int32, (1, 128), 1)
        carry_ref[...] = jnp.zeros_like(carry_ref)
        for step in range(sz.steps):
            keys = (step + 1) * sz.tile
            rows = slice(step * sz.tile, keys)
            q = qkv_ref[rows, :lw] * sz.scale
            k = qkv_ref[:keys, lw : 2 * lw]
            v = qkv_ref[:keys, 2 * lw :]
            q_slot = jnp.where(slot_mask(sz, sz.per), q, 0)
            pen, chosen, _, _ = penalty_of(
                sz, step, long_part, lower, q_slot, k, carry_ref[step : step + 1, :keys]
            )
            if step + 1 < sz.steps:
                carry_ref[step + 1 : step + 2, :keys] = carry_ref[step : step + 1, :keys] + jnp.sum(
                    chosen, axis=0, keepdims=True
                )
            total = jnp.zeros((sz.tile, lw), F32)
            lse = jnp.zeros((sz.tile, 128), F32)
            for h in range(sz.per):
                mask = slot_mask(sz, h)
                logits = dot_nt(jnp.where(mask, q, 0), k) - pen
                top = jnp.max(logits, axis=1, keepdims=True)
                weights = jnp.exp(logits - top)
                weight = jnp.sum(weights, axis=1, keepdims=True)
                mixed = dot(weights.astype(BF16), v) / weight
                total = jnp.where(mask, mixed, total)
                lse = jnp.where(lane == h, top + jnp.log(weight), lse)
            out_ref[rows, :] = total
            lse_ref[rows, :] = lse
        for k in range(sz.groups):
            at = pl.multiple_of(((hg + k) % sz.groups) * sz.rows, sz.rows)
            att_refs[k][...] = out_ref[pl.ds(at, sz.rows), : sz.used].astype(BF16)

    outs = [
        ((sz.span, 3 * lw), BF16),
        ((sz.span, sz.width), BF16),
        ((sz.span, sz.width), BF16),
        ((sz.span, 128), F32),
        ((sz.span, lw), F32),
        ((sz.steps, sz.span), F32),
    ] + [((sz.rows, sz.used), BF16)] * sz.groups
    out = whole_call(body, outs, 2, (place, docs, *chunks, gain, bias, w_sel, b_sel), "attend_forward", flops=9e9)
    return out[:6], out[6:]


def attend_backward(sz, place, docs, saved, w_sel, grads):
    lw = sz.lanes
    qkv, _, hat, lse, att, carry = saved

    def body(place_ref, doc_ref, qkv_ref, hat_ref, lse_ref, att_ref, carry_ref, w_ref, *refs):
        grad_refs = refs[: sz.groups]
        outs = refs[sz.groups :]
        dqkv_ref, sums_ref, lnsum_ref = outs[:3]
        dnorm_ref, dout, dk_sum, dv_sum, behind = outs[3:]
        hg, part = place_ref[0], place_ref[1]
        long_part = part_is_long(sz, doc_ref, part)
        dout[...] = jnp.zeros_like(dout)
        for k in range(sz.groups):
            at = pl.multiple_of(((hg - k) % sz.groups) * sz.rows, sz.rows)
            dout[pl.ds(at, sz.rows), : sz.used] = grad_refs[k][...]
        dk_sum[...] = jnp.zeros_like(dk_sum)
        dv_sum[...] = jnp.zeros_like(dv_sum)
        behind[...] = jnp.zeros_like(behind)
        lower = lower_mask(sz)
        for step in reversed(range(sz.steps)):
            keys = (step + 1) * sz.tile
            rows = slice(step * sz.tile, keys)
            q = qkv_ref[rows, :lw] * sz.scale
            k = qkv_ref[:keys, lw : 2 * lw]
            v = qkv_ref[:keys, 2 * lw :]
            d_rows = dout[rows, :]
            dot_rows = d_rows.astype(F32) * att_ref[rows, :]
            last = slot_mask(sz, sz.per)
            q_slot = jnp.where(last, q, 0)
            pen, _, positive, select = penalty_of(
                sz, step, long_part, lower, q_slot, k, carry_ref[step : step + 1, :keys]
            )
            dpen = jnp.zeros((sz.tile, keys), F32)
            dq = jnp.zeros((sz.tile, lw), F32)
            for h in range(sz.per):
                mask = slot_mask(sz, h)
                q_h = jnp.where(mask, q, 0)
                d_h = jnp.where(mask, d_rows, 0)
                probs = jnp.exp(dot_nt(q_h, k) - pen - lse_ref[rows, h : h + 1])
                delta = jnp.sum(jnp.where(mask, dot_rows, 0.0), axis=1, keepdims=True)
                ds = probs * (dot_nt(d_h, v) - delta)
                dpen = dpen - ds
                ds_low = ds.astype(BF16)
                dq = jnp.where(mask, dot(ds_low, k), dq)
                dk_sum[:keys, :] += dot_tn(ds_low, q_h)
                dv_sum[:keys, :] += dot_tn(probs.astype(BF16), d_h)
            dchosen = dot_split(lower, dpen, True) + behind[:1, :keys]
            behind[:1, :keys] += jnp.sum(dpen, axis=0, keepdims=True)
            ds_low = jnp.where(select, positive * dchosen * (2.0 / sz.block), 0.0).astype(BF16)
            dq = jnp.where(last, dot(ds_low, k), dq)
            dk_sum[:keys, :] += dot_tn(ds_low, q_slot)
            dqkv_ref[rows, :lw] = (dq * sz.scale).astype(BF16)
        dqkv_ref[:, lw : 2 * lw] = dk_sum[...].astype(BF16)
        dqkv_ref[:, 2 * lw :] = dv_sum[...].astype(BF16)
        sums_ref[...] = jnp.sum(dqkv_ref[...].astype(F32), axis=0, keepdims=True)
        gain_sum = jnp.zeros((1, sz.width), F32)
        bias_sum = jnp.zeros((1, sz.width), F32)
        for i in range(sz.n_ctx):
            at = slice(i * sz.block, (i + 1) * sz.block)
            dnorm = dot_nt(dqkv_ref[at, :], w_ref[...])
            dnorm_ref[i] = dnorm.astype(BF16)
            bias_sum += jnp.sum(dnorm, axis=0, keepdims=True)
            gain_sum += jnp.sum(dnorm * hat_ref[at, :].astype(F32), axis=0, keepdims=True)
        lnsum_ref[0:1, :] = gain_sum
        lnsum_ref[1:2, :] = bias_sum

    outs = [((sz.span, 3 * lw), BF16), ((1, 3 * lw), F32), ((2, sz.width), F32)]
    outs += [((sz.n_ctx, sz.block, sz.width), BF16)]
    scratch = [
        pltpu.VMEM((sz.span, lw), BF16),
        pltpu.VMEM((sz.span, lw), F32),
        pltpu.VMEM((sz.span, lw), F32),
        pltpu.VMEM((8, sz.span), F32),
    ]
    out = whole_call(
        body, outs, 2, (place, docs, qkv, hat, lse, att, carry, w_sel, *grads), "attend_backward", scratch, 17e9
    )
    return out


def project_out(sz, place, att, tokens, out_weight, out_bias, gain, bias):
    def body(place_ref, *refs):
        att_refs = refs[: sz.groups]
        tok_refs = refs[sz.groups : sz.groups + sz.parts]
        w_ref, b_ref, gain_ref, bias_ref, middle_ref, second_ref = refs[sz.groups + sz.parts :]
        hg, part = place_ref[0], place_ref[1]
        for s in range(sz.parts):
            at = pl.ds(pl.multiple_of(((part - s) % sz.parts) * sz.block, sz.block), sz.block)
            middle_ref[at, :] = tok_refs[s][...].astype(F32) + b_ref[...]
        total = middle_ref[...]
        for k in range(sz.groups):
            at = pl.multiple_of(((hg - k) % sz.groups) * sz.used, 16)
            total += dot(att_refs[k][...], w_ref[pl.ds(at, sz.used), :])
        middle_ref[...] = total
        hat, _ = normalize(total)
        second_ref[...] = (hat * gain_ref[...] + bias_ref[...]).astype(BF16)

    outs = [((sz.rows, sz.width), F32), ((sz.rows, sz.width), BF16)]
    return whole_call(
        body, outs, 1, (place, *att, *tokens, out_weight, out_bias, gain, bias), "project_out"
    )


def feed_forward(sz, second, cot, fc, fc_bias, proj, name):
    n = len(second)
    units = fc.shape[1]
    root = math.sqrt(2.0 / math.pi)

    def body(*refs):
        second_refs, cot_refs = refs[:n], refs[n : 2 * n]
        fc_ref, bias_ref, proj_ref = refs[2 * n : 2 * n + 3]
        outs = refs[2 * n + 3 :]
        act_refs, grad_refs, back_refs, sums_ref = outs[:n], outs[n : 2 * n], outs[2 * n : 3 * n], outs[3 * n]
        total = jnp.zeros((1, units), F32)
        for i in range(n):
            hidden = dot(second_refs[i][...], fc_ref[...]) + bias_ref[...]
            square = hidden * hidden
            t = jnp.tanh(root * (hidden + 0.044715 * hidden * square))
            half = 0.5 * (1.0 + t)
            act_refs[i][...] = (hidden * half).astype(BF16)
            slope = half + 0.5 * hidden * (1.0 - t * t) * (root * (1.0 + 3.0 * 0.044715 * square))
            grad = (dot_nt(cot_refs[i][...], proj_ref[...]) * slope).astype(BF16)
            grad_refs[i][...] = grad
            back_refs[i][...] = dot_nt(grad, fc_ref[...]).astype(BF16)
            total += jnp.sum(grad.astype(F32), axis=0, keepdims=True)
        sums_ref[...] = total

    outs = [((sz.rows, units), BF16)] * (2 * n) + [((sz.rows, sz.width), BF16)] * n + [((1, units), F32)]
    out = whole_call(body, outs, 0, (*second, *cot, fc, fc_bias, proj), name)
    return out[:n], out[n : 2 * n], out[2 * n : 3 * n], out[3 * n]


def middle_backward(sz, place, back, middle, cot, out_weight, gain):
    n_back = len(back)

    def body(place_ref, *refs):
        back_refs = refs[:n_back]
        cot_refs = refs[n_back : n_back + sz.parts]
        rest = refs[n_back + sz.parts :]
        middle_ref, w_ref, gain_ref = rest[:3]
        branch_ref, sums_ref = rest[3:5]
        gm_refs = rest[5 : 5 + sz.parts]
        datt_refs = rest[5 + sz.parts : 5 + sz.parts + sz.groups]
        total = rest[-1]
        hg, part = place_ref[0], place_ref[1]
        cot_sum = jnp.zeros((1, sz.width), F32)
        for s in range(sz.parts):
            at = pl.ds(pl.multiple_of(((part - s) % sz.parts) * sz.block, sz.block), sz.block)
            block = cot_refs[s][...].astype(F32)
            total[at, :] = block
            cot_sum += jnp.sum(block, axis=0, keepdims=True)
        e = back_refs[0][...].astype(F32)
        for ref in back_refs[1:]:
            e += ref[...].astype(F32)
        hat, r = normalize(middle_ref[...])
        eg = e * gain_ref[...]
        inner = eg - jnp.mean(eg, axis=-1, keepdims=True)
        inner -= hat * jnp.mean(eg * hat, axis=-1, keepdims=True)
        grad = total[...] + r * inner
        total[...] = grad
        branch = grad.astype(BF16)
        branch_ref[...] = branch
        for s in range(sz.parts):
            at = pl.ds(pl.multiple_of(((part + s) % sz.parts) * sz.block, sz.block), sz.block)
            gm_refs[s][...] = total[at, :]
        for k in range(sz.groups):
            at = pl.multiple_of(((hg + k) % sz.groups) * sz.used, 16)
            datt_refs[k][...] = dot_nt(branch, w_ref[pl.ds(at, sz.used), :]).astype(BF16)
        sums_ref[0:1, :] = jnp.sum(e * hat, axis=0, keepdims=True)
        sums_ref[1:2, :] = jnp.sum(e, axis=0, keepdims=True)
        sums_ref[2:3, :] = jnp.sum(branch.astype(F32), axis=0, keepdims=True)
        sums_ref[3:4, :] = cot_sum

    outs = [((sz.rows, sz.width), BF16), ((4, sz.width), F32)]
    outs += [((sz.block, sz.width), F32)] * sz.parts
    outs += [((sz.rows, sz.used), BF16)] * sz.groups
    out = whole_call(
        body,
        outs,
        1,
        (place, *back, *cot, middle, out_weight, gain),
        "middle_backward",
        [pltpu.VMEM((sz.rows, sz.width), F32)],
        4 * sz.rows * sz.width * sz.width,
    )
    split = 2 + sz.parts
    return out[0], out[1], out[2:split], out[split:]


def weight_terms(sz, place, left, right, name):
    n = len(left)
    width = sz.width
    rows = left[0].shape[1] // sz.n_ctx

    if not sz.aligned:
        both = dot_tn(jnp.concatenate(left, axis=0), jnp.concatenate(right, axis=0)).astype(BF16)
        both = both.reshape(sz.groups, sz.parts, -1, width)
        pieces = []
        for s in range(sz.parts):
            piece = lax.dynamic_index_in_dim(both, (place[1] + s) % sz.parts, 1, keepdims=False)
            pieces.append(jnp.roll(piece, -place[0], axis=0))
        return pieces

    def body(place_ref, *refs):
        piece_refs = refs[2 * n : -1]
        held = refs[-1]
        hg, part = place_ref[0], place_ref[1]
        held[...] = sum(dot_tn(a[...], b[...]) for a, b in zip(refs[:n], refs[n : 2 * n])).astype(BF16)
        for s in range(sz.parts):
            for k in range(sz.groups):
                to = ((hg + k) % sz.groups) * sz.parts + (part + s) % sz.parts
                at = pl.multiple_of(to * rows, 16)
                piece_refs[s][k] = held[pl.ds(at, rows), :]

    return whole_call(
        body,
        [((sz.groups, rows, width), BF16)] * sz.parts,
        1,
        (place, *left, *right),
        name,
        [pltpu.VMEM((left[0].shape[1], width), BF16)],
    )


def feed_forward_out(sz, act, proj):
    n = len(act)

    def body(*refs):
        for i in range(n):
            refs[n + 1 + i][...] = dot(refs[i][...], refs[n][...]).astype(BF16)

    return whole_call(body, [((sz.rows, sz.width), BF16)] * n, 0, (*act, proj), "feed_forward_out")


def out_weights(sz, place, att, branch):
    half = sz.width // 2

    def body(place_ref, *refs):
        branch_ref, own_ref, other_ref = refs[sz.groups :]
        hg, core = place_ref[0], place_ref[2]
        for k in range(sz.groups):
            at = pl.multiple_of(((hg - k) % sz.groups) * sz.used, 16)

            @pl.when(at < sz.width)
            def _():
                grad_w = dot_tn(refs[k][...], branch_ref[...]).astype(BF16)
                left, right = grad_w[:, :half], grad_w[:, half:]
                own_ref[pl.ds(at, sz.used), :] = jnp.where(core == 0, left, right)
                other_ref[pl.ds(at, sz.used), :] = jnp.where(core == 0, right, left)

    return whole_call(body, [((sz.width, half), BF16)] * 2, 1, (place, *att, branch), "out_weights")


def sum_near(sz, pieces):
    if not sz.aligned:
        total = sum(p.astype(F32) for p in pieces).astype(BF16)
        return [total[k] for k in range(sz.groups)]
    n = len(pieces)

    def body(*refs):
        for k in range(sz.groups):
            total = refs[0][k].astype(F32)
            for s in range(1, n):
                total += refs[s][k].astype(F32)
            refs[n + k][...] = total.astype(BF16)

    return whole_call(body, [(pieces[0].shape[1:], BF16)] * sz.groups, 0, tuple(pieces), "sum_near")


def pack_sums(sz, place, terms, tail):
    rows, lanes = terms[0][0].shape[1:]
    full = rows * len(terms) + tail.shape[1]
    if not sz.packed:
        sums = [sum(t.astype(F32) for t in pair).astype(BF16) for pair in terms]
        sums = jnp.concatenate(sums + [tail], axis=1).reshape((sz.groups, sz.parts, full, lanes))
        sums = jnp.roll(sums, (-place[0], -place[1]), axis=(0, 1))
        return [sums[:, s] for s in range(sz.parts)]
    flat = [t for pair in terms for t in pair]
    per = len(terms[0])

    def body(place_ref, *refs):
        tail_ref = refs[len(flat)]
        outs = refs[len(flat) + 1 :]
        for k in range(sz.groups):
            for s in range(sz.parts):
                to = ((place_ref[0] + k) % sz.groups) * sz.parts + (place_ref[1] + s) % sz.parts
                for i in range(len(terms)):
                    total = sum(refs[i * per + j][to].astype(F32) for j in range(per))
                    outs[s][k, i * rows : (i + 1) * rows, :] = total.astype(BF16)
                outs[s][k, rows * len(terms) :, :] = tail_ref[to]

    return whole_call(
        body, [((sz.groups, full, lanes), BF16)] * sz.parts, 1, (place, *flat, tail), "pack_sums"
    )


def add_halves(value):
    half = value.shape[-2] // 2
    value = value.astype(F32)
    return value[..., :half, :] + value[..., half:, :]


def split_halves(value, axis):
    high = value.astype(BF16)
    return jnp.concatenate([high, (value - high.astype(F32)).astype(BF16)], axis=axis)


def sum_packed(sz, pieces, rows):
    if not sz.packed:
        total = sum(p[:, : 2 * rows].astype(F32) for p in pieces).astype(BF16)
        tail = split_halves(sum(add_halves(p[:, 2 * rows :]) for p in pieces), 1)
        total = jnp.concatenate([total, tail], axis=1)
        return [total[k] for k in range(sz.groups)]
    n = len(pieces)

    def body(*refs):
        for k in range(sz.groups):
            out = refs[n + k]
            out[: 2 * rows, :] = sum(r[k, : 2 * rows, :].astype(F32) for r in refs[:n]).astype(BF16)
            out[2 * rows :, :] = split_halves(sum(add_halves(r[k, 2 * rows :, :]) for r in refs[:n]), 0)

    return whole_call(body, [(pieces[0].shape[1:], BF16)] * sz.groups, 0, tuple(pieces), "sum_packed")


def unpack_sums(sz, place, blocks, rows):
    full, lanes = blocks[0].shape
    if not sz.packed:
        got = jnp.stack(blocks)
        sel = jnp.roll(got[::-1, :rows], place[0] + 1, axis=0)
        total = got[:, rows : 2 * rows].astype(F32).sum(axis=0).astype(BF16)
        return jnp.concatenate([sel, total[None]], axis=0), add_halves(got[:, 2 * rows :]).sum(axis=0)

    def body(place_ref, *refs):
        sel_ref, small_ref = refs[sz.groups :]
        for k in range(sz.groups):
            sel_ref[(place_ref[0] - k) % sz.groups] = refs[k][:rows, :]
        total = sum(r[rows : 2 * rows, :].astype(F32) for r in refs[: sz.groups])
        sel_ref[sz.groups] = total.astype(BF16)
        small_ref[...] = sum(add_halves(r[2 * rows :, :]) for r in refs[: sz.groups])

    return whole_call(
        body,
        [((sz.groups + 1, rows, lanes), BF16), (((full - 2 * rows) // 2, lanes), F32)],
        1,
        (place, *blocks),
        "unpack_sums",
    )


def join_shares(sz, place, fc_shares, proj_shares):
    band, width = sz.width // sz.n_ctx, sz.width
    share = sz.hidden // (sz.n_ctx * sz.n_grp)
    n = sz.n_grp

    def body(place_ref, *refs):
        fc_ref, proj_ref, held, held_proj = refs[2 * n :]
        core, gx = place_ref[2], place_ref[3]
        for c in range(2):
            for k in range(sz.gx):
                at = ((gx - k) % sz.gx) * 2 + (core + c) % 2
                held[at] = refs[c * sz.gx + k][...]
                held_proj[at] = refs[n + c * sz.gx + k][...]
        for j in range(sz.n_ctx):
            cut = slice(j * share, (j + 1) * share)
            fc_ref[:, j * share * n : (j + 1) * share * n] = jnp.concatenate(
                [held[q, :, cut].astype(F32) for q in range(n)], axis=1
            )
        for q in range(n):
            proj_ref[q * share : (q + 1) * share, :] = held_proj[q].astype(F32)

    if not sz.aligned:
        fc = order_grp(sz, place, fc_shares).reshape(n, band, sz.n_ctx, share)
        fc = fc.transpose(1, 2, 0, 3).reshape(band, sz.hidden)
        return fc, order_grp(sz, place, proj_shares).reshape(n * share, width)
    return whole_call(
        body,
        [((band, sz.hidden), F32), ((n * share, width), F32)],
        1,
        (place, *fc_shares, *proj_shares),
        "join_shares",
        [pltpu.VMEM((n,) + fc_shares[0].shape, BF16), pltpu.VMEM((n,) + proj_shares[0].shape, BF16)],
    )


def order_grp(sz, place, values):
    held = jnp.stack(values).reshape((2, sz.gx) + values[0].shape)
    held = jnp.roll(held[:, ::-1], place[3] + 1, axis=1)
    return jnp.roll(held, place[2], axis=0).swapaxes(0, 1).astype(F32)


def qkv_weights(sz, place, normed, dqkv):
    w3 = 3 * sz.lanes
    half = w3 // 2

    def body(place_ref, normed_ref, dqkv_ref, own_ref, other_ref):
        core = place_ref[2]
        grad = dot_tn(normed_ref[...], dqkv_ref[...]).astype(BF16)
        own_ref[...] = jnp.where(core == 0, grad[:, :half], grad[:, half:])
        other_ref[...] = jnp.where(core == 0, grad[:, half:], grad[:, :half])

    return whole_call(body, [((sz.width, half), BF16)] * 2, 1, (place, normed, dqkv), "qkv_weights")


def join_heads(sz, place, pieces):
    rows, lanes = pieces[0].shape[1:]
    w3 = 3 * sz.lanes
    if not sz.packed:
        held = order_grp(sz, place, pieces)
        sel = held[:, :, : sz.groups].transpose(2, 0, 3, 1, 4).reshape(sz.groups, sz.gx * rows, w3)
        out = held[:, :, sz.groups].transpose(0, 2, 1, 3).reshape(sz.gx * rows, 2 * lanes)
        return join_slots(sz, sel), out

    def body(place_ref, *refs):
        sel_ref, out_ref, held = refs[sz.n_grp :]
        core, gx = place_ref[2], place_ref[3]
        for c in range(2):
            for k in range(sz.gx):
                held[((gx - k) % sz.gx) * 2 + (core + c) % 2] = refs[c * sz.gx + k][...]
        for x in range(sz.gx):
            at_rows = slice(x * rows, (x + 1) * rows)
            both = [
                jnp.concatenate([held[2 * x, g], held[2 * x + 1, g]], axis=1).astype(F32)
                for g in range(sz.groups)
            ]
            for third in range(3):
                at = third * sz.lanes
                own = jnp.concatenate([b[:, at : at + sz.used] for b in both], axis=1)[:, : sz.width]
                first = sum(b[:, at + sz.used : at + sz.used + sz.head] for b in both)
                rest = jnp.zeros((rows, sz.width - sz.head), F32)
                sel_ref[at_rows, third * sz.width : (third + 1) * sz.width] = own + jnp.concatenate(
                    [first, rest], axis=1
                )
            for c in range(2):
                out_ref[at_rows, c * lanes : (c + 1) * lanes] = held[2 * x + c, sz.groups].astype(F32)

    return whole_call(
        body,
        [((sz.gx * rows, 3 * sz.width), F32), ((sz.gx * rows, sz.width), F32)],
        1,
        (place, *pieces),
        "join_heads",
        [pltpu.VMEM((sz.n_grp,) + pieces[0].shape, BF16)],
    )


def join_slots(sz, sel):
    n = sel.shape[1]
    thirds = sel.reshape(sz.groups, n, 3, sz.lanes)
    own = thirds[..., : sz.used].transpose(2, 1, 0, 3).reshape(3, n, sz.groups * sz.used)
    own = own[..., : sz.width]
    first = thirds[..., sz.used : sz.used + sz.head].sum(axis=0).transpose(1, 0, 2)
    own = own.at[:, :, : sz.head].add(first)
    return own.transpose(1, 0, 2).reshape(n, 3 * sz.width)


def finish_tokens(sz, place, docs, dnorm, tokens, grad_middle, gain):
    def body(place_ref, doc_ref, d_ref, *refs):
        tok_refs = refs[: sz.parts]
        gm_refs = refs[sz.parts : 2 * sz.parts]
        gain_ref, out_ref, held = refs[2 * sz.parts :]
        part = place_ref[1]
        for s in range(sz.parts):
            base = (part - s) % sz.parts
            e = d_ref[base].astype(F32)
            for k in range(1, sz.groups):
                e += d_ref[k * sz.parts + base].astype(F32)
            hat, r = normalize(tok_refs[(-s) % sz.parts][...].astype(F32))
            eg = e * gain_ref[...]
            inner = eg - jnp.mean(eg, axis=-1, keepdims=True)
            inner -= hat * jnp.mean(eg * hat, axis=-1, keepdims=True)
            held[...] = gm_refs[s][...] + r * inner
            for a in range(4):
                src = source_grain(sz, doc_ref, 4 * base + a)
                out_ref[src] = held[pl.ds(a * sz.grain, sz.grain), :]

    out = whole_call(
        body,
        [((sz.grains, sz.grain, sz.width), F32)],
        2,
        (place, docs, dnorm, *tokens, *grad_middle, gain),
        "finish_tokens",
        [pltpu.VMEM((sz.block, sz.width), F32)],
    )
    return out[0].reshape(sz.rows, sz.width)


def finish_middle(sz, place, mixed, middle, proj_bias):
    n = len(mixed)

    def body(place_ref, *refs):
        middle_ref, bias_ref = refs[n : n + 2]
        outs = refs[n + 2 :]
        part = place_ref[1]
        for s in range(sz.parts):
            at = pl.ds(pl.multiple_of(((part + s) % sz.parts) * sz.block, sz.block), sz.block)
            total = middle_ref[at, :] + bias_ref[...]
            for ref in refs[:n]:
                total += ref[at, :].astype(F32)
            outs[s][...] = total

    return whole_call(
        body,
        [((sz.block, sz.width), F32)] * sz.parts,
        1,
        (place, *mixed, middle, proj_bias),
        "finish_middle",
    )


def unsort_rows(sz, place, docs, blocks):
    def body(place_ref, doc_ref, *refs):
        out_ref = refs[-1]
        part = place_ref[1]
        for s in range(sz.parts):
            base = 4 * ((part - s) % sz.parts)
            for a in range(4):
                src = source_grain(sz, doc_ref, base + a)
                out_ref[src] = refs[s][pl.ds(a * sz.grain, sz.grain), :]

    out = whole_call(
        body,
        [((sz.grains, sz.grain, sz.width), F32)],
        2,
        (place, docs, *blocks),
        "unsort_rows",
    )
    return out[0].reshape(sz.rows, sz.width)


def order_rows(sz, place, blocks):
    def body(place_ref, *refs):
        for s in range(sz.parts):
            at = pl.multiple_of(((place_ref[1] - s) % sz.parts) * sz.block, sz.block)
            refs[-1][pl.ds(at, sz.block), :] = refs[s][...]

    return whole_call(body, [((sz.rows, sz.width), BF16)], 1, (place, *blocks), "order_rows")[0]


def gather_rows(sz, block):
    near = [block, shift(block, "core", 2, 1)]
    far = []
    for k in range(1, sz.gx):
        along = shift(block, "gx", sz.gx, k)
        far += [along, shift(along, "core", 2, 1)]
    return near, far


def return_rows(sz, near, far, later):
    terms = [near[0], shift(near[1], "core", 2, 1)]
    for k in range(1, sz.gx):
        mine, other = far[2 * k - 2 : 2 * k]
        mine = (mine.astype(F32) + shift(other, "core", 2, 1).astype(F32)).astype(BF16)
        mine, later = lax.optimization_barrier((mine, later))
        terms.append(shift(mine, "gx", sz.gx, -k))
    return terms, later


def all_grp(sz, value):
    along = [value] + [shift(value, "gx", sz.gx, k) for k in range(1, sz.gx)]
    return along + [shift(v, "core", 2, 1) for v in along]


def after(gate, value):
    return lax.optimization_barrier((gate, value))[1]


def head_columns(sz, weight, hg):
    lead = weight.shape[:-1]
    pieces = []
    for third in range(3):
        full = weight[..., third * sz.width : (third + 1) * sz.width]
        spare = sz.groups * sz.used - sz.width
        if spare:
            full = jnp.pad(full, [(0, 0)] * len(lead) + [(0, spare)])
        own = lax.dynamic_slice_in_dim(full, hg * sz.used, sz.used, axis=len(lead))
        first = full[..., : sz.head] if third < 2 else jnp.zeros(lead + (sz.head,), weight.dtype)
        rest = sz.lanes - sz.used - sz.head
        pieces += [own, first]
        if rest:
            pieces.append(jnp.zeros(lead + (rest,), weight.dtype))
    return jnp.concatenate(pieces, axis=-1)


def weight_shares(sz, place, qkv_weight, fc_weight, proj_weight):
    share = sz.hidden // (sz.n_ctx * sz.n_grp)
    units = sz.n_ctx * share
    if not sz.aligned:
        mine = place[3] * 2 + place[2]
        w_sel = head_columns(sz, qkv_weight, place[0])
        fc = fc_weight.reshape(sz.width, sz.n_ctx, sz.n_grp, share)
        fc = lax.dynamic_index_in_dim(fc, mine, 2, keepdims=False).reshape(sz.width, units)
        proj = proj_weight.reshape(sz.n_ctx, sz.n_grp, share, sz.width)
        proj = lax.dynamic_index_in_dim(proj, mine, 1, keepdims=False).reshape(units, sz.width)
        return w_sel, fc, proj

    def body(place_ref, qkv_ref, fc_in, proj_in, sel_ref, fc_ref, proj_ref):
        hg, mine = place_ref[0], place_ref[3] * 2 + place_ref[2]
        for third in range(3):
            to, base = third * sz.lanes, third * sz.width
            end = jnp.zeros((sz.width, sz.lanes - sz.used), BF16)
            if third < 2:
                end = qkv_ref[:, base : base + 128][:, : sz.head]
                if sz.lanes - sz.used > sz.head:
                    end = jnp.concatenate(
                        [end, jnp.zeros((sz.width, sz.lanes - sz.used - sz.head), BF16)], axis=1
                    )
            for g in range(sz.groups):

                @pl.when(hg == g)
                def _():
                    own = qkv_ref[:, base : base + sz.width][:, g * sz.used : (g + 1) * sz.used]
                    sel_ref[:, to : to + sz.lanes] = jnp.concatenate([own, end], axis=1)

        wide = share * sz.n_grp
        for q in range(sz.n_grp):

            @pl.when(mine == q)
            def _():
                fc_ref[...] = jnp.concatenate(
                    [
                        fc_in[:, j * wide : (j + 1) * wide][:, q * share : (q + 1) * share]
                        for j in range(sz.n_ctx)
                    ],
                    axis=1,
                )

        for j in range(sz.n_ctx):
            at = pl.multiple_of(j * wide + mine * share, 16)
            proj_ref[j * share : (j + 1) * share, :] = proj_in[pl.ds(at, share), :]

    return whole_call(
        body,
        [((sz.width, 3 * sz.lanes), BF16), ((sz.width, units), BF16), ((units, sz.width), BF16)],
        1,
        (place, qkv_weight, fc_weight, proj_weight),
        "weight_shares",
    )


def body(
    tokens,
    ln1_gain,
    ln1_bias,
    qkv_weight,
    qkv_bias,
    out_weight,
    out_bias,
    ln2_gain,
    ln2_bias,
    fc_weight,
    fc_bias,
    proj_weight,
    proj_bias,
    doc_blocks,
    cotangent,
):
    rows, width = tokens.shape
    hidden = fc_weight.shape[1]
    n_ctx = lax.axis_size("hg") * lax.axis_size("part")
    n_grp = lax.axis_size("gx") * 2
    sz = Sizes(rows, width, hidden, doc_blocks.shape[1], n_ctx, n_grp)
    hg, part = lax.axis_index("hg"), lax.axis_index("part")
    gx, core = lax.axis_index("gx"), lax.axis_index("core")
    place = jnp.stack([hg, part, core, gx]).astype(jnp.int32)
    mine = gx * 2 + core

    def vector(v):
        return v.astype(F32)[None, :]

    gain1, bias1 = vector(ln1_gain), vector(ln1_bias)
    gain2, bias2 = vector(ln2_gain), vector(ln2_bias)
    share = hidden // (n_ctx * n_grp)
    b_sel = head_columns(sz, vector(qkv_bias), hg)
    fc_b = lax.dynamic_index_in_dim(
        vector(fc_bias).reshape(1, n_ctx, n_grp, share), mine, 2, keepdims=False
    ).reshape(1, n_ctx * share)
    spare = sz.groups * sz.used - sz.width
    w_out = jnp.pad(out_weight, ((0, spare), (0, 0))) if spare else out_weight

    tok_parts, cot_parts = sort_rows(sz, place, doc_blocks, tokens, cotangent)
    tok_mine = [tok_parts[0]] + [shift(tok_parts[s], "part", sz.parts, s) for s in range(1, sz.parts)]
    order = sorted(range(1, sz.groups), key=lambda k: -min(k, sz.groups - k))
    chunks = {(0, s): tok_mine[s] for s in range(sz.parts)}
    for s in range(sz.parts):
        for k in order:
            chunks[k, s] = shift(tok_mine[s], "hg", sz.groups, k)
    chunks = [chunks[k, s] for k in range(sz.groups) for s in range(sz.parts)]

    cot_parts, qkv_weight, fc_weight, proj_weight = after(
        chunks[order[0] * sz.parts], (cot_parts, qkv_weight, fc_weight, proj_weight)
    )
    cot_mine = [cot_parts[0]] + [shift(cot_parts[s], "part", sz.parts, s) for s in range(1, sz.parts)]
    cot_rows = order_rows(sz, place, cot_mine)
    cot_near, cot_far = gather_rows(sz, cot_rows)
    w_sel, fc, proj = weight_shares(sz, place, qkv_weight, fc_weight, proj_weight)

    chunks = after(cot_rows, chunks)
    saved, att_out = attend_forward(sz, place, doc_blocks, chunks, gain1, bias1, w_sel, b_sel)
    att = [att_out[0]] + [shift(att_out[k], "hg", sz.groups, k) for k in range(1, sz.groups)]

    middle, second = project_out(sz, place, after(cot_far, att), tok_mine, w_out, vector(out_bias), gain2, bias2)

    sec_near, sec_far = gather_rows(sz, second)
    act_n, gh_n, back_n, fc_sum_n = feed_forward(sz, sec_near, cot_near, fc, fc_b, proj, "feed_forward_near")
    act_f, gh_f, back_f, fc_sum_f = feed_forward(
        sz, after(back_n, sec_far), cot_far, fc, fc_b, proj, "feed_forward_far"
    )
    fc_sum = fc_sum_n + fc_sum_f
    back, act_f = return_rows(sz, back_n, back_f, act_f)
    proj_pieces = weight_terms(sz, place, act_n + act_f, cot_near + cot_far, "proj_terms")
    gh_f = after(proj_pieces, gh_f)
    fc_pieces = weight_terms(sz, place, sec_near + sec_far, gh_n + gh_f, "fc_terms")
    mixed = feed_forward_out(sz, act_n + after(fc_pieces, act_f), proj)
    back = after(mixed, back)
    branch, mid_sums, gm_parts, datt_out = middle_backward(
        sz, place, back, middle, cot_mine, w_out, gain2
    )
    datt = [datt_out[0]] + [shift(datt_out[k], "hg", sz.groups, k) for k in range(1, sz.groups)]

    band = width // n_ctx
    half = width // 2
    n_rows = band // sz.gx
    def near_sums(pieces):
        return sum_near(
            sz, [pieces[0]] + [shift(pieces[s], "part", sz.parts, s) for s in range(1, sz.parts)]
        )

    def far_sum(near):
        total = near[0].astype(F32)
        for k in range(1, sz.groups):
            total = total + shift(near[k], "hg", sz.groups, k).astype(F32)
        return total.astype(BF16)

    proj_share = far_sum(near_sums(proj_pieces))
    fc_near = near_sums(fc_pieces)
    fc_share = far_sum(fc_near)
    grad_fc, grad_proj = join_shares(sz, place, all_grp(sz, fc_share), all_grp(sz, proj_share))

    def over_grp(own, other):
        both = own.astype(F32) + shift(other, "core", 2, 1).astype(F32)
        both = both.astype(BF16).reshape(n_ctx, sz.gx, n_rows, own.shape[1])
        pieces = []
        for k in range(sz.gx):
            piece = lax.dynamic_index_in_dim(both, (gx + k) % sz.gx, 1, keepdims=False)
            pieces.append(shift(piece, "gx", sz.gx, k) if k else piece)
        return pieces

    d_out = out_weights(sz, place, att, branch)
    out_terms = over_grp(*d_out)
    datt = after((proj_share, fc_near, d_out), datt)

    mixed, _ = return_rows(sz, mixed[:2], mixed[2:], place)
    out_parts = finish_middle(sz, place, mixed, middle, vector(proj_bias))
    out_mine = [out_parts[0]] + [shift(out_parts[s], "part", sz.parts, s) for s in range(1, sz.parts)]
    output = unsort_rows(sz, place, doc_blocks, out_mine)

    dqkv, qkv_sum, ln1_sums, dnorm = attend_backward(sz, place, doc_blocks, saved, w_sel, datt)
    dnorm = lax.all_to_all(after(fc_share, dnorm), CTX, 0, 0, tiled=True)
    gm_mine = [gm_parts[0]] + [shift(gm_parts[s], "part", sz.parts, s) for s in range(1, sz.parts)]
    dnorm = after((output, grad_fc), dnorm)
    grad_tokens = finish_tokens(sz, place, doc_blocks, dnorm, tok_parts, gm_mine, gain1)

    w3 = 3 * sz.lanes
    w_half = w3 // 2
    sel_terms = over_grp(*qkv_weights(sz, place, saved[1], dqkv))

    placed = jnp.zeros((sz.groups, 1, w3), F32)
    placed = lax.dynamic_update_slice(placed, qkv_sum[None], (hg, 0, 0))
    fc_placed = jnp.zeros((n_ctx, n_grp, share), F32)
    fc_placed = lax.dynamic_update_slice(fc_placed, fc_sum.reshape(n_ctx, 1, share), (0, mine, 0))
    vectors = [
        ln1_sums[0],
        ln1_sums[1],
        join_slots(sz, placed)[0],
        mid_sums[2],
        mid_sums[0],
        mid_sums[1],
        fc_placed.reshape(-1),
        mid_sums[3],
    ]
    small = jnp.concatenate([v.reshape(n_ctx, -1) for v in vectors], axis=1)
    small = small + shift(small, "core", 2, 1)
    small = small + sum(shift(small, "gx", sz.gx, k) for k in range(1, sz.gx))
    n_small = small.shape[1]
    small = jnp.pad(small, ((0, 0), (0, -n_small % (8 * w_half)))).reshape(n_ctx, -1, w_half)
    pieces = pack_sums(sz, place, [sel_terms, out_terms], split_halves(small, 1))
    pieces = [pieces[0]] + [shift(pieces[s], "part", sz.parts, s) for s in range(1, sz.parts)]
    blocks = sum_packed(sz, pieces, n_rows)
    blocks = [blocks[0]] + [shift(blocks[k], "hg", sz.groups, k) for k in range(1, sz.groups)]
    sums, small = unpack_sums(sz, place, after(grad_tokens, blocks), n_rows)
    grad_qkv, grad_out = join_heads(sz, place, all_grp(sz, sums))

    small = small.reshape(-1)
    cuts, at = [], 0
    for v in vectors:
        n = v.shape[0] // n_ctx
        cuts.append(small[at : at + n])
        at += n
    g_ln1_gain, g_ln1_bias, g_qkv_bias, g_out_bias, g_ln2_gain, g_ln2_bias, g_fc_bias, g_proj_bias = cuts
    return (
        output,
        grad_tokens,
        g_ln1_gain,
        g_ln1_bias,
        grad_qkv,
        g_qkv_bias,
        grad_out,
        g_out_bias,
        g_ln2_gain,
        g_ln2_bias,
        grad_fc,
        g_fc_bias,
        grad_proj,
        g_proj_bias,
    )


def solution(mesh):
    n_grp, n_ctx = mesh.devices.shape
    split = P(GRP + CTX, None)

    def run(tokens, *rest):
        rows = tokens.shape[0] // (n_grp * n_ctx)
        parts = rows // min(rows // 2, SEQ_LEN // n_ctx)
        fine = Mesh(mesh.devices.reshape(n_grp // 2, 2, n_ctx // parts, parts), GRP + CTX)
        each = jax.shard_map(
            body,
            mesh=fine,
            in_specs=(split,) + (P(),) * 12 + (P(GRP, None), split),
            out_specs=(
                split,
                split,
                P(CTX),
                P(CTX),
                P(CTX, None),
                P(CTX),
                P(CTX, None),
                P(CTX),
                P(CTX),
                P(CTX),
                P(CTX, None),
                P(CTX),
                P(CTX, None),
                P(CTX),
            ),
            check_vma=False,
        )
        return each(tokens, *rest)

    return run
```

```python
import functools
import math

import jax
import jax.numpy as jnp
from jax import lax
from jax.experimental import pallas as pl
from jax.experimental.pallas import tpu as pltpu
from jax.sharding import Mesh
from jax.sharding import PartitionSpec as P

HEADS = 12
SEQ_LEN = 2048
FAR = 1e30
F32 = jnp.float32
BF16 = jnp.bfloat16
GRP = ("gx", "core")
CTX = ("hg", "part")
VMEM_BYTES = 56 * 1024 * 1024


QUARTER, PART, CORE, GX, HG, ROW = range(6)


class Sizes:
    def __init__(self, rows, width, hidden, docs, n_ctx, n_grp):
        self.rows, self.width, self.hidden, self.docs = rows, width, hidden, docs
        self.n_ctx, self.n_grp = n_ctx, n_grp
        self.head = width // HEADS
        self.block = min(rows // 2, SEQ_LEN // n_ctx)
        self.parts = rows // self.block
        self.groups = n_ctx // self.parts
        self.grain = self.block // 4
        self.grains = rows // self.grain
        self.per = -(-HEADS // self.groups)
        self.used = self.per * self.head
        self.lanes = -(-((self.per + 1) * self.head) // 128) * 128
        self.span = n_ctx * self.block
        self.half = self.groups // 2
        self.tile = 256
        self.steps = self.span // self.tile
        self.gx = n_grp // 2
        self.scale = self.head ** (-0.5)
        band, share = width // n_ctx, hidden // (n_ctx * n_grp)
        self.aligned = band % 32 == 0 and share % 32 == 0 and share * n_ctx == width
        self.packed = band % (32 * self.gx // 2) == 0 and 3 * self.lanes == width


def peer(sz, quarter, at, sign):
    return (((quarter >> 1) + sign * (at >> 1)) % sz.half) * 2 + ((quarter + at) & 1)


def dot(a, b):
    return lax.dot_general(a, b, (((1,), (0,)), ((), ())), preferred_element_type=F32)


def dot_nt(a, b):
    return lax.dot_general(a, b, (((1,), (1,)), ((), ())), preferred_element_type=F32)


def dot_tn(a, b):
    return lax.dot_general(a, b, (((0,), (0,)), ((), ())), preferred_element_type=F32)


def dot_split(mask, value, transposed):
    high = value.astype(BF16)
    low = (value - high.astype(F32)).astype(BF16)
    mul = dot_tn if transposed else dot
    return mul(mask, high) + mul(mask, low)


def shift(value, axis, size, step):
    return lax.ppermute(value, axis, [(i, (i + step) % size) for i in range(size)])


def to_peer(sz, value, at):
    if at == 0:
        return value
    pairs = []
    for core in range(2):
        for hg in range(sz.groups):
            to = (hg // sz.half) * sz.half + (hg + at // 2) % sz.half
            pairs.append((core * sz.groups + hg, ((core + at) % 2) * sz.groups + to))
    return lax.ppermute(value, ("core", "hg"), pairs)


def owner_pairs(sz, t):
    pairs = []
    for core in range(2):
        for hg in range(sz.groups):
            for row in range(sz.parts):
                part = (row + t) % sz.parts
                to_hg = (part % 2) * sz.half + hg // 2
                to_row = (part // 2) * 2 + core
                to = ((hg % 2) * sz.groups + to_hg) * sz.parts + to_row
                pairs.append(((core * sz.groups + hg) * sz.parts + row, to))
    return pairs


def to_owner(sz, blocks):
    return [lax.ppermute(b, ("core",) + CTX, owner_pairs(sz, t)) for t, b in enumerate(blocks)]


def from_owner(sz, blocks):
    return [
        lax.ppermute(b, ("core",) + CTX, [(b_, a_) for a_, b_ in owner_pairs(sz, t)])
        for t, b in enumerate(blocks)
    ]


def cost(flops, *arrays):
    size = sum(math.prod(a.shape) * a.dtype.itemsize for a in arrays)
    return pl.CostEstimate(flops=int(flops), bytes_accessed=int(size), transcendentals=0)


def whole_call(body, outs, n_scalars, args, name, scratch=(), flops=0):
    shapes = [jax.ShapeDtypeStruct(s, t) for s, t in outs]
    specs = [pl.BlockSpec(memory_space=pltpu.SMEM)] * n_scalars
    specs += [pl.BlockSpec(memory_space=pltpu.VMEM)] * (len(args) - n_scalars)
    return pl.pallas_call(
        body,
        out_shape=shapes,
        in_specs=specs,
        out_specs=[pl.BlockSpec(memory_space=pltpu.VMEM)] * len(outs),
        scratch_shapes=list(scratch),
        compiler_params=pltpu.CompilerParams(vmem_limit_bytes=VMEM_BYTES),
        cost_estimate=cost(flops, *args, *shapes),
        name=name,
    )(*args)


def source_grain(sz, doc_ref, place):
    is_long = [(doc_ref[0, d] == sz.block).astype(jnp.int32) for d in range(sz.docs)]
    longs = sum(is_long)
    seen_long, seen_short, begin, source = 0, 0, 0, 0
    for d in range(sz.docs):
        count = doc_ref[0, d] // sz.grain
        first = jnp.where(is_long[d] == 1, 4 * seen_long, 4 * longs + seen_short)
        inside = (place >= first) & (place < first + count)
        source = source + jnp.where(inside, begin + place - first, 0)
        seen_long = seen_long + is_long[d]
        seen_short = seen_short + jnp.where(is_long[d] == 1, 0, count)
        begin = begin + count
    return source


def part_is_long(sz, doc_ref, part):
    longs = sum((doc_ref[0, d] == sz.block).astype(jnp.int32) for d in range(sz.docs))
    return part < longs


def sort_rows(sz, place, docs, tokens, cotangent):
    def body(place_ref, doc_ref, tok_ref, cot_ref, *outs):
        for t in range(sz.parts):
            for a in range(4):
                src = source_grain(sz, doc_ref, 4 * ((place_ref[ROW] + t) % sz.parts) + a)
                at = pl.ds(a * sz.grain, sz.grain)
                outs[t][at, :] = tok_ref[src]
                outs[sz.parts + t][at, :] = cot_ref[src]

    shape = (sz.grains, sz.grain, sz.width)
    out = whole_call(
        body,
        [((sz.block, sz.width), BF16)] * (2 * sz.parts),
        2,
        (place, docs, tokens.reshape(shape), cotangent.reshape(shape)),
        "sort_rows",
    )
    return out[: sz.parts], out[sz.parts :]


def block_rows(sz, place_ref, quarter, t):
    at = quarter * sz.parts + (place_ref[PART] - t) % sz.parts
    return pl.ds(pl.multiple_of(at * sz.block, sz.block), sz.block)


def normalize(x):
    center = x - jnp.mean(x, axis=-1, keepdims=True)
    spread = jnp.mean(center * center, axis=-1, keepdims=True)
    r = lax.rsqrt(spread + 1e-05)
    return center * r, r


def pair_masks(sz, step, long_part):
    keys = (step + 1) * sz.tile
    q_row = step * sz.tile + lax.broadcasted_iota(jnp.int32, (sz.tile, 1), 0)
    k_row = lax.broadcasted_iota(jnp.int32, (1, keys), 1)
    q_doc = jnp.where(long_part, 0, (q_row % sz.block) // sz.grain)
    k_doc = jnp.where(long_part, 0, (k_row % sz.block) // sz.grain)
    k_in = jnp.where(long_part, k_row % sz.block, k_row % sz.grain)
    first = (k_row < sz.block) & (k_in == 0)
    same = q_doc == k_doc
    visible = same & (k_row <= q_row)
    select = same & (k_row < q_row) & jnp.logical_not(first)
    return visible, select


def slot_mask(sz, slot):
    lane = lax.broadcasted_iota(jnp.int32, (1, sz.lanes), 1)
    return lane // sz.head == slot


def lower_mask(sz):
    row = lax.broadcasted_iota(jnp.int32, (sz.tile, sz.tile), 0)
    col = lax.broadcasted_iota(jnp.int32, (sz.tile, sz.tile), 1)
    return jnp.where(row > col, 1.0, 0.0).astype(BF16)


def penalty_of(sz, step, long_part, lower, q_slot, k, carry):
    visible, select = pair_masks(sz, step, long_part)
    positive = jnp.maximum(dot_nt(q_slot, k), 0.0)
    chosen = jnp.where(select, positive * positive * (1.0 / sz.block), 0.0)
    penalty = dot_split(lower, chosen, False) + carry
    return jnp.where(visible, penalty, FAR), chosen, positive, select


def attend_forward(sz, place, docs, chunks, gain, bias, w_sel, b_sel):
    lw = sz.lanes
    n = len(chunks)

    def body(place_ref, doc_ref, *refs):
        xs = refs[:n]
        gain_ref, bias_ref, w_ref, b_ref = refs[n : n + 4]
        qkv_ref, normed_ref, hat_ref, lse_ref, out_ref, carry_ref = refs[n + 4 : n + 10]
        att_refs = refs[n + 10 :]
        quarter = place_ref[QUARTER]
        long_part = part_is_long(sz, doc_ref, place_ref[PART])
        for i in range(n):
            hat, _ = normalize(xs[i][...].astype(F32))
            normed = (hat * gain_ref[...] + bias_ref[...]).astype(BF16)
            packed = (dot(normed, w_ref[...]) + b_ref[...]).astype(BF16)
            low = hat.astype(BF16)
            for t in range(sz.parts):
                at = block_rows(sz, place_ref, peer(sz, quarter, i, -1), t)
                here = slice(t * sz.block, (t + 1) * sz.block)
                hat_ref[at, :] = low[here]
                normed_ref[at, :] = normed[here]
                qkv_ref[at, :] = packed[here]
        lower = lower_mask(sz)
        lane = lax.broadcasted_iota(jnp.int32, (1, 128), 1)
        carry_ref[...] = jnp.zeros_like(carry_ref)
        for step in range(sz.steps):
            keys = (step + 1) * sz.tile
            rows = slice(step * sz.tile, keys)
            q = qkv_ref[rows, :lw] * sz.scale
            k = qkv_ref[:keys, lw : 2 * lw]
            v = qkv_ref[:keys, 2 * lw :]
            q_slot = jnp.where(slot_mask(sz, sz.per), q, 0)
            pen, chosen, _, _ = penalty_of(
                sz, step, long_part, lower, q_slot, k, carry_ref[step : step + 1, :keys]
            )
            if step + 1 < sz.steps:
                carry_ref[step + 1 : step + 2, :keys] = carry_ref[step : step + 1, :keys] + jnp.sum(
                    chosen, axis=0, keepdims=True
                )
            total = jnp.zeros((sz.tile, lw), F32)
            lse = jnp.zeros((sz.tile, 128), F32)
            for h in range(sz.per):
                mask = slot_mask(sz, h)
                logits = dot_nt(jnp.where(mask, q, 0), k) - pen
                top = jnp.max(logits, axis=1, keepdims=True)
                weights = jnp.exp(logits - top)
                weight = jnp.sum(weights, axis=1, keepdims=True)
                mixed = dot(weights.astype(BF16), v) / weight
                total = jnp.where(mask, mixed, total)
                lse = jnp.where(lane == h, top + jnp.log(weight), lse)
            out_ref[rows, :] = total
            lse_ref[rows, :] = lse
        for i in range(n):
            for t in range(sz.parts):
                at = block_rows(sz, place_ref, peer(sz, quarter, i, 1), t)
                att_refs[i][t * sz.block : (t + 1) * sz.block, :] = out_ref[at, : sz.used].astype(BF16)

    outs = [
        ((sz.span, 3 * lw), BF16),
        ((sz.span, sz.width), BF16),
        ((sz.span, sz.width), BF16),
        ((sz.span, 128), F32),
        ((sz.span, lw), F32),
        ((sz.steps, sz.span), F32),
    ] + [((sz.rows, sz.used), BF16)] * sz.groups
    out = whole_call(body, outs, 2, (place, docs, *chunks, gain, bias, w_sel, b_sel), "attend_forward", flops=9e9)
    return out[:6], out[6:]


def attend_backward(sz, place, docs, saved, w_sel, grads):
    lw = sz.lanes
    qkv, _, hat, lse, att, carry = saved

    def body(place_ref, doc_ref, qkv_ref, hat_ref, lse_ref, att_ref, carry_ref, w_ref, *refs):
        grad_refs = refs[: sz.groups]
        outs = refs[sz.groups :]
        dqkv_ref, sums_ref, lnsum_ref = outs[:3]
        dnorm_refs = outs[3 : 3 + sz.groups]
        dout, dk_sum, dv_sum, behind = outs[3 + sz.groups :]
        quarter = place_ref[QUARTER]
        long_part = part_is_long(sz, doc_ref, place_ref[PART])
        dout[...] = jnp.zeros_like(dout)
        for i in range(sz.groups):
            for t in range(sz.parts):
                at = block_rows(sz, place_ref, peer(sz, quarter, i, -1), t)
                dout[at, : sz.used] = grad_refs[i][t * sz.block : (t + 1) * sz.block, :]
        dk_sum[...] = jnp.zeros_like(dk_sum)
        dv_sum[...] = jnp.zeros_like(dv_sum)
        behind[...] = jnp.zeros_like(behind)
        lower = lower_mask(sz)
        for step in reversed(range(sz.steps)):
            keys = (step + 1) * sz.tile
            rows = slice(step * sz.tile, keys)
            q = qkv_ref[rows, :lw] * sz.scale
            k = qkv_ref[:keys, lw : 2 * lw]
            v = qkv_ref[:keys, 2 * lw :]
            d_rows = dout[rows, :]
            dot_rows = d_rows.astype(F32) * att_ref[rows, :]
            last = slot_mask(sz, sz.per)
            q_slot = jnp.where(last, q, 0)
            pen, _, positive, select = penalty_of(
                sz, step, long_part, lower, q_slot, k, carry_ref[step : step + 1, :keys]
            )
            dpen = jnp.zeros((sz.tile, keys), F32)
            dq = jnp.zeros((sz.tile, lw), F32)
            for h in range(sz.per):
                mask = slot_mask(sz, h)
                q_h = jnp.where(mask, q, 0)
                d_h = jnp.where(mask, d_rows, 0)
                probs = jnp.exp(dot_nt(q_h, k) - pen - lse_ref[rows, h : h + 1])
                delta = jnp.sum(jnp.where(mask, dot_rows, 0.0), axis=1, keepdims=True)
                ds = probs * (dot_nt(d_h, v) - delta)
                dpen = dpen - ds
                ds_low = ds.astype(BF16)
                dq = jnp.where(mask, dot(ds_low, k), dq)
                dk_sum[:keys, :] += dot_tn(ds_low, q_h)
                dv_sum[:keys, :] += dot_tn(probs.astype(BF16), d_h)
            dchosen = dot_split(lower, dpen, True) + behind[:1, :keys]
            behind[:1, :keys] += jnp.sum(dpen, axis=0, keepdims=True)
            ds_low = jnp.where(select, positive * dchosen * (2.0 / sz.block), 0.0).astype(BF16)
            dq = jnp.where(last, dot(ds_low, k), dq)
            dk_sum[:keys, :] += dot_tn(ds_low, q_slot)
            dqkv_ref[rows, :lw] = (dq * sz.scale).astype(BF16)
        dqkv_ref[:, lw : 2 * lw] = dk_sum[...].astype(BF16)
        dqkv_ref[:, 2 * lw :] = dv_sum[...].astype(BF16)
        sums_ref[...] = jnp.sum(dqkv_ref[...].astype(F32), axis=0, keepdims=True)
        gain_sum = jnp.zeros((1, sz.width), F32)
        bias_sum = jnp.zeros((1, sz.width), F32)
        for i in range(sz.groups):
            for t in range(sz.parts):
                at = block_rows(sz, place_ref, peer(sz, quarter, i, 1), t)
                dnorm = dot_nt(dqkv_ref[at, :], w_ref[...])
                dnorm_refs[i][t * sz.block : (t + 1) * sz.block, :] = dnorm.astype(BF16)
                bias_sum += jnp.sum(dnorm, axis=0, keepdims=True)
                gain_sum += jnp.sum(dnorm * hat_ref[at, :].astype(F32), axis=0, keepdims=True)
        lnsum_ref[0:1, :] = gain_sum
        lnsum_ref[1:2, :] = bias_sum

    outs = [((sz.span, 3 * lw), BF16), ((1, 3 * lw), F32), ((2, sz.width), F32)]
    outs += [((sz.rows, sz.width), BF16)] * sz.groups
    scratch = [
        pltpu.VMEM((sz.span, lw), BF16),
        pltpu.VMEM((sz.span, lw), F32),
        pltpu.VMEM((sz.span, lw), F32),
        pltpu.VMEM((8, sz.span), F32),
    ]
    out = whole_call(
        body, outs, 2, (place, docs, qkv, hat, lse, att, carry, w_sel, *grads), "attend_backward", scratch, 17e9
    )
    return out[0], out[1], out[2], out[3:]


def project_out(sz, place, att, tokens, out_weight, out_bias, gain, bias):
    def body(place_ref, *refs):
        att_refs = refs[: sz.groups]
        tok_ref, w_ref, b_ref, gain_ref, bias_ref, middle_ref, second_ref = refs[sz.groups :]
        total = tok_ref[...].astype(F32) + b_ref[...]
        for k in range(sz.groups):
            at = pl.multiple_of(peer(sz, place_ref[QUARTER], k, -1) * sz.used, 16)
            total += dot(att_refs[k][...], w_ref[pl.ds(at, sz.used), :])
        middle_ref[...] = total
        hat, _ = normalize(total)
        second_ref[...] = (hat * gain_ref[...] + bias_ref[...]).astype(BF16)

    outs = [((sz.rows, sz.width), F32), ((sz.rows, sz.width), BF16)]
    return whole_call(
        body, outs, 1, (place, *att, tokens, out_weight, out_bias, gain, bias), "project_out"
    )


def feed_forward(sz, second, cot, fc, fc_bias, proj, name):
    n = len(second)
    units = fc.shape[1]
    root = math.sqrt(2.0 / math.pi)

    def body(*refs):
        second_refs, cot_refs = refs[:n], refs[n : 2 * n]
        fc_ref, bias_ref, proj_ref = refs[2 * n : 2 * n + 3]
        outs = refs[2 * n + 3 :]
        act_refs, grad_refs, back_refs, sums_ref = outs[:n], outs[n : 2 * n], outs[2 * n : 3 * n], outs[3 * n]
        total = jnp.zeros((1, units), F32)
        for i in range(n):
            hidden = dot(second_refs[i][...], fc_ref[...]) + bias_ref[...]
            square = hidden * hidden
            t = jnp.tanh(root * (hidden + 0.044715 * hidden * square))
            half = 0.5 * (1.0 + t)
            act_refs[i][...] = (hidden * half).astype(BF16)
            slope = half + 0.5 * hidden * (1.0 - t * t) * (root * (1.0 + 3.0 * 0.044715 * square))
            grad = (dot_nt(cot_refs[i][...], proj_ref[...]) * slope).astype(BF16)
            grad_refs[i][...] = grad
            back_refs[i][...] = dot_nt(grad, fc_ref[...]).astype(BF16)
            total += jnp.sum(grad.astype(F32), axis=0, keepdims=True)
        sums_ref[...] = total

    outs = [((sz.rows, units), BF16)] * (2 * n) + [((sz.rows, sz.width), BF16)] * n + [((1, units), F32)]
    out = whole_call(body, outs, 0, (*second, *cot, fc, fc_bias, proj), name)
    return out[:n], out[n : 2 * n], out[2 * n : 3 * n], out[3 * n]


def middle_backward(sz, place, back, middle, cot, out_weight, gain):
    n_back = len(back)

    def body(place_ref, *refs):
        back_refs = refs[:n_back]
        cot_ref, middle_ref, w_ref, gain_ref, grad_ref, branch_ref, sums_ref = refs[n_back : n_back + 7]
        datt_refs = refs[n_back + 7 :]
        cot = cot_ref[...].astype(F32)
        e = back_refs[0][...].astype(F32)
        for ref in back_refs[1:]:
            e += ref[...].astype(F32)
        hat, r = normalize(middle_ref[...])
        eg = e * gain_ref[...]
        inner = eg - jnp.mean(eg, axis=-1, keepdims=True)
        inner -= hat * jnp.mean(eg * hat, axis=-1, keepdims=True)
        grad = cot + r * inner
        grad_ref[...] = grad
        branch = grad.astype(BF16)
        branch_ref[...] = branch
        for k in range(sz.groups):
            at = pl.multiple_of(peer(sz, place_ref[QUARTER], k, 1) * sz.used, 16)
            datt_refs[k][...] = dot_nt(branch, w_ref[pl.ds(at, sz.used), :]).astype(BF16)
        sums_ref[0:1, :] = jnp.sum(e * hat, axis=0, keepdims=True)
        sums_ref[1:2, :] = jnp.sum(e, axis=0, keepdims=True)
        sums_ref[2:3, :] = jnp.sum(branch.astype(F32), axis=0, keepdims=True)
        sums_ref[3:4, :] = jnp.sum(cot, axis=0, keepdims=True)

    outs = [((sz.rows, sz.width), F32), ((sz.rows, sz.width), BF16), ((4, sz.width), F32)]
    outs += [((sz.rows, sz.used), BF16)] * sz.groups
    out = whole_call(body, outs, 1, (place, *back, cot, middle, out_weight, gain), "middle_backward")
    return out[0], out[1], out[2], out[3:]


def feed_forward_weights(sz, place, second, grad_hidden, act, cot):
    n = len(second)
    width, units = sz.width, act[0].shape[1]
    band, share = width // sz.n_ctx, units // sz.n_ctx
    both = band * units // width + share

    if not sz.aligned:
        second, grad_hidden, act, cot = (jnp.concatenate(v, axis=0) for v in (second, grad_hidden, act, cot))
        d_fc = dot_tn(second, grad_hidden).astype(BF16).reshape(sz.groups, sz.parts, -1, width)
        d_proj = dot_tn(act, cot).astype(BF16).reshape(sz.groups, sz.parts, -1, width)
        total = jnp.roll(jnp.concatenate([d_fc, d_proj], axis=2), -place[ROW], axis=1)
        return [total[:, s] for s in range(sz.parts)]

    def body(place_ref, *refs):
        second_refs, grad_refs, act_refs, cot_refs = (refs[i * n : (i + 1) * n] for i in range(4))
        outs, held = refs[4 * n : -1], refs[-1]
        held[:width, :] = sum(dot_tn(x[...], g[...]) for x, g in zip(second_refs, grad_refs)).astype(BF16)
        held[width:, :] = sum(dot_tn(a[...], c[...]) for a, c in zip(act_refs, cot_refs)).astype(BF16)
        for s in range(sz.parts):
            for g in range(sz.groups):
                to = g * sz.parts + (place_ref[ROW] + s) % sz.parts
                outs[s][g, :band, :] = held[pl.ds(pl.multiple_of(to * band, 16), band), :]
                outs[s][g, band:, :] = held[pl.ds(pl.multiple_of(width + to * share, 16), share), :]

    return whole_call(
        body,
        [((sz.groups, both, width), BF16)] * sz.parts,
        1,
        (place, *second, *grad_hidden, *act, *cot),
        "feed_forward_weights",
        [pltpu.VMEM((width + units, width), BF16)],
    )


def feed_forward_out(sz, act, proj):
    n = len(act)

    def body(*refs):
        for i in range(n):
            refs[n + 1 + i][...] = dot(refs[i][...], refs[n][...]).astype(BF16)

    return whole_call(body, [((sz.rows, sz.width), BF16)] * n, 0, (*act, proj), "feed_forward_out")


def out_weights(sz, place, att, branch):
    half = sz.width // 2

    def body(place_ref, *refs):
        branch_ref, own_ref, other_ref = refs[sz.groups :]
        core = place_ref[CORE]
        for k in range(sz.groups):
            at = pl.multiple_of(peer(sz, place_ref[QUARTER], k, -1) * sz.used, 16)

            @pl.when(at < sz.width)
            def _():
                grad_w = dot_tn(refs[k][...], branch_ref[...]).astype(BF16)
                left, right = grad_w[:, :half], grad_w[:, half:]
                own_ref[pl.ds(at, sz.used), :] = jnp.where(core == 0, left, right)
                other_ref[pl.ds(at, sz.used), :] = jnp.where(core == 0, right, left)

    return whole_call(body, [((sz.width, half), BF16)] * 2, 1, (place, *att, branch), "out_weights")


def sum_arrays(sz, pieces, name):
    def body(*refs):
        refs[-1][...] = sum(r[...].astype(F32) for r in refs[:-1]).astype(BF16)

    return whole_call(body, [(pieces[0].shape, BF16)], 0, tuple(pieces), name)[0]


def sum_first(sz, value, name):
    def body(ref, out_ref):
        out_ref[...] = sum(ref[k].astype(F32) for k in range(value.shape[0])).astype(BF16)

    return whole_call(body, [(value.shape[1:], BF16)], 0, (value,), name)[0]


def pack_sums(sz, place, sel, out, tail):
    rows, lanes = sel[0].shape[1:]
    n_tail = tail.shape[1]
    full = rows + n_tail + rows // 2
    if not sz.packed:
        sel = sum(t.astype(F32) for t in sel).astype(BF16)
        out = sum(t.astype(F32) for t in out).astype(BF16)
        out = jnp.concatenate([out[:, : rows // 2], out[:, rows // 2 :]], axis=2)
        both = jnp.concatenate([sel, tail, out], axis=1).reshape((sz.groups, sz.parts, full, lanes))
        both = jnp.roll(both, (-place[HG], -place[ROW]), axis=(0, 1))
        return [both[:, s] for s in range(sz.parts)]
    n = len(sel)

    def body(place_ref, *refs):
        tail_ref, outs = refs[2 * n], refs[2 * n + 1 :]
        for k in range(sz.groups):
            for s in range(sz.parts):
                to = ((place_ref[HG] + k) % sz.groups) * sz.parts + (place_ref[ROW] + s) % sz.parts
                outs[s][k, :rows, :] = sum(r[to].astype(F32) for r in refs[:n]).astype(BF16)
                outs[s][k, rows : rows + n_tail, :] = tail_ref[to]
                total = sum(r[to].astype(F32) for r in refs[n : 2 * n]).astype(BF16)
                outs[s][k, rows + n_tail :, : lanes // 2] = total[: rows // 2]
                outs[s][k, rows + n_tail :, lanes // 2 :] = total[rows // 2 :]

    return whole_call(
        body, [((sz.groups, full, lanes), BF16)] * sz.parts, 1, (place, *sel, *out, tail), "pack_sums"
    )


def add_halves(value):
    half = value.shape[-2] // 2
    value = value.astype(F32)
    return value[..., :half, :] + value[..., half:, :]


def split_halves(value, axis):
    high = value.astype(BF16)
    return jnp.concatenate([high, (value - high.astype(F32)).astype(BF16)], axis=axis)


def sum_packed(sz, pieces, rows, n_tail):
    end = rows + n_tail
    if not sz.packed:
        total = sum(p.astype(F32) for p in pieces).astype(BF16)
        tail = split_halves(sum(add_halves(p[:, rows:end]) for p in pieces), 1)
        total = jnp.concatenate([total[:, :rows], tail, total[:, end:]], axis=1)
        return [total[k] for k in range(sz.groups)]
    n = len(pieces)

    def body(*refs):
        for k in range(sz.groups):
            out = refs[n + k]
            for cut in (slice(0, rows), slice(end, None)):
                out[cut, :] = sum(r[k, cut, :].astype(F32) for r in refs[:n]).astype(BF16)
            out[rows:end, :] = split_halves(sum(add_halves(r[k, rows:end, :]) for r in refs[:n]), 0)

    return whole_call(body, [(pieces[0].shape[1:], BF16)] * sz.groups, 0, tuple(pieces), "sum_packed")


def unpack_sums(sz, place, blocks, rows, n_tail):
    full, lanes = blocks[0].shape
    end = rows + n_tail
    if not sz.packed:
        got = jnp.stack(blocks)
        total = got.astype(F32).sum(axis=0).astype(BF16)
        sel = got[:, :rows].astype(F32)
        sel = sel[: sz.half] + sel[sz.half :]
        sel = jnp.roll(sel[::-1], place[HG] + 1, axis=0).astype(BF16).reshape(-1, lanes)
        tail = split_halves(add_halves(got[:, rows:end]).sum(axis=0), 0)
        return jnp.concatenate([sel, tail, total[end:]], axis=0)

    def body(place_ref, *refs):
        blocks, out_ref = refs[: sz.groups], refs[sz.groups]
        for k in range(sz.half):
            at = pl.multiple_of(((place_ref[HG] - k) % sz.half) * rows, 16)
            total = blocks[k][:rows, :].astype(F32) + blocks[k + sz.half][:rows, :].astype(F32)
            out_ref[pl.ds(at, rows), :] = total.astype(BF16)
        at = sz.half * rows
        out_ref[at : at + n_tail, :] = split_halves(sum(add_halves(r[rows:end, :]) for r in blocks), 0)
        out_ref[at + n_tail :, :] = sum(r[end:, :].astype(F32) for r in blocks).astype(BF16)

    shape = (sz.half * rows + full - rows, lanes)
    return whole_call(body, [(shape, BF16)], 1, (place, *blocks), "unpack_sums")[0]


def small_cuts(sz):
    band, units = sz.width // sz.n_ctx, sz.hidden // sz.n_ctx
    one = [(0, i * band, band) for i in range(6)]
    return one[:2] + [(1, 0, 3 * band)] + one[2:5] + [(1, 3 * band, units)] + one[5:]


def pack_vectors(sz, place, ln1, qkv, middle, fc_sums):
    band, units = sz.width // sz.n_ctx, sz.hidden // sz.n_ctx
    share = units // sz.n_grp
    w3 = 3 * sz.lanes
    lanes = w3

    if not sz.packed:
        hg, mine = place[QUARTER], place[GX] * 2 + place[CORE]
        placed = jnp.zeros((sz.groups, 1, w3), F32)
        placed = lax.dynamic_update_slice(placed, qkv[None], (hg, 0, 0))
        fc_placed = jnp.zeros((sz.n_ctx, sz.n_grp, share), F32)
        fc_placed = lax.dynamic_update_slice(fc_placed, sum(fc_sums).reshape(sz.n_ctx, 1, share), (0, mine, 0))
        vectors = [ln1[0], ln1[1], join_slots(sz, placed)[0], middle[2], middle[0], middle[1]]
        vectors += [fc_placed.reshape(-1), middle[3]]
        out = jnp.zeros((sz.n_ctx, 8, lanes), F32)
        for v, (row, at, n) in zip(vectors, small_cuts(sz)):
            out = out.at[:, row, at : at + n].set(v.reshape(sz.n_ctx, n))
        return split_halves(out, 1)

    def body(place_ref, ln1_ref, qkv_ref, mid_ref, *refs):
        out_ref, held, fc_held, whole = refs[len(fc_sums) :]
        hg, mine = place_ref[QUARTER], place_ref[GX] * 2 + place_ref[CORE]
        held[...] = jnp.zeros_like(held)
        for g in range(sz.groups):

            @pl.when(hg == g)
            def _():
                for third in range(3):
                    at = third * sz.width + g * sz.used
                    held[0:1, at : at + sz.used] = qkv_ref[:, third * sz.lanes : third * sz.lanes + sz.used]

        for third in range(3):
            at, base = third * sz.width, third * sz.lanes + sz.used
            held[0:1, at : at + sz.head] += qkv_ref[:, base : base + sz.head]
        fc = sum(r[...] for r in refs[: len(fc_sums)])
        fc_held[...] = jnp.zeros_like(fc_held)
        for q in range(sz.n_grp):

            @pl.when(mine == q)
            def _():
                for j in range(sz.n_ctx):
                    fc_held[j : j + 1, q * share : (q + 1) * share] = fc[:, j * share : (j + 1) * share]

        whole[...] = jnp.zeros_like(whole)
        for j in range(sz.n_ctx):
            cut = slice(j * band, (j + 1) * band)
            singles = [ln1_ref[0:1, cut], ln1_ref[1:2, cut], mid_ref[2:3, cut], mid_ref[0:1, cut]]
            singles += [mid_ref[1:2, cut], mid_ref[3:4, cut]]
            whole[j, 0:1, : 6 * band] = jnp.concatenate(singles, axis=1)
            seconds = [held[0:1, 3 * j * band : 3 * (j + 1) * band], fc_held[j : j + 1, :]]
            whole[j, 1:2, : 3 * band + units] = jnp.concatenate(seconds, axis=1)
            out_ref[j] = split_halves(whole[j], 0)

    return whole_call(
        body,
        [((sz.n_ctx, 16, lanes), BF16)],
        1,
        (place, ln1, qkv, middle, *fc_sums),
        "pack_vectors",
        [
            pltpu.VMEM((8, 3 * sz.width), F32),
            pltpu.VMEM((sz.n_ctx, units), F32),
            pltpu.VMEM((sz.n_ctx, 8, lanes), F32),
        ],
    )[0]


def join_shares(sz, place, shares):
    band, width = sz.width // sz.n_ctx, sz.width
    share = sz.hidden // (sz.n_ctx * sz.n_grp)
    n = sz.n_grp
    n_fc = shares[0].shape[0] - share

    def body(place_ref, *refs):
        fc_ref, proj_ref, held = refs[n:]
        core, gx = place_ref[CORE], place_ref[GX]
        for c in range(2):
            for k in range(sz.gx):
                held[((gx - k) % sz.gx) * 2 + (core + c) % 2] = refs[c * sz.gx + k][...]
        for j in range(sz.n_ctx):
            cut = slice(j * share, (j + 1) * share)
            fc_ref[:, j * share * n : (j + 1) * share * n] = jnp.concatenate(
                [held[q, :n_fc, cut].astype(F32) for q in range(n)], axis=1
            )
        for q in range(n):
            proj_ref[q * share : (q + 1) * share, :] = held[q, n_fc:, :].astype(F32)

    if not sz.aligned:
        held = order_grp(sz, place, shares).reshape((n,) + shares[0].shape)
        fc = held[:, :n_fc].reshape(n, band, sz.n_ctx, share)
        fc = fc.transpose(1, 2, 0, 3).reshape(band, sz.hidden)
        return fc, held[:, n_fc:].reshape(n * share, width)
    return whole_call(
        body,
        [((band, sz.hidden), F32), ((n * share, width), F32)],
        1,
        (place, *shares),
        "join_shares",
        [pltpu.VMEM((n,) + shares[0].shape, BF16)],
    )


def order_grp(sz, place, values):
    held = jnp.stack(values).reshape((2, sz.gx) + values[0].shape)
    held = jnp.roll(held[:, ::-1], place[GX] + 1, axis=1)
    return jnp.roll(held, place[CORE], axis=0).swapaxes(0, 1).astype(F32)


def qkv_weights(sz, normed, dqkv):
    band = sz.width // sz.n_ctx
    w3 = 3 * sz.lanes

    def body(normed_ref, dqkv_ref, out_ref):
        grad = dot_tn(normed_ref[...], dqkv_ref[...]).astype(BF16)
        for i in range(sz.n_ctx):
            out_ref[i] = grad[i * band : (i + 1) * band, :]

    if not sz.packed:
        return dot_tn(normed, dqkv).astype(BF16).reshape(sz.n_ctx, band, w3)
    return whole_call(body, [((sz.n_ctx, band, w3), BF16)], 0, (normed, dqkv), "qkv_weights")[0]


def join_heads(sz, place, pieces, rows, n_tail):
    lanes = pieces[0].shape[1]
    start = sz.half * rows
    end = start + n_tail
    half = sz.width // 2
    if not sz.packed:
        held = order_grp(sz, place, pieces)
        sel = held[:, :, :start].reshape(sz.gx, 2, sz.half, rows, lanes)
        sel = sel.transpose(2, 1, 0, 3, 4).reshape(sz.groups, sz.gx * rows, lanes)
        out = held[:, :, end:].reshape(sz.gx, 2, rows // 2, 2, half)
        out = out.transpose(0, 3, 2, 1, 4).reshape(sz.gx * rows, sz.width)
        small = add_halves(held[:, :, start:end]).sum(axis=(0, 1))
        return join_slots(sz, sel), out, *(small[row, at : at + n] for row, at, n in small_cuts(sz))

    def body(place_ref, *refs):
        sel_ref, out_ref = refs[sz.n_grp : sz.n_grp + 2]
        small_refs, held = refs[sz.n_grp + 2 : -1], refs[-1]
        core, gx = place_ref[CORE], place_ref[GX]
        small = sum(add_halves(r[start:end, :]) for r in refs[: sz.n_grp])
        for ref, (row, at, n) in zip(small_refs, small_cuts(sz)):
            ref[...] = small[row, at : at + n]
        for c in range(2):
            for k in range(sz.gx):
                held[((gx - k) % sz.gx) * 2 + (core + c) % 2] = refs[c * sz.gx + k][...]
        for x in range(sz.gx):
            at_rows = slice(x * rows, (x + 1) * rows)
            both = [
                held[2 * x + g % 2, (g // 2) * rows : (g // 2 + 1) * rows, :].astype(F32) for g in range(sz.groups)
            ]
            for third in range(3):
                at = third * sz.lanes
                own = jnp.concatenate([b[:, at : at + sz.used] for b in both], axis=1)[:, : sz.width]
                first = sum(b[:, at + sz.used : at + sz.used + sz.head] for b in both)
                rest = jnp.zeros((rows, sz.width - sz.head), F32)
                sel_ref[at_rows, third * sz.width : (third + 1) * sz.width] = own + jnp.concatenate(
                    [first, rest], axis=1
                )
            for c in range(2):
                piece = held[2 * x + c, end:, :].astype(F32)
                columns = slice(c * half, (c + 1) * half)
                out_ref[x * rows : x * rows + rows // 2, columns] = piece[:, :half]
                out_ref[x * rows + rows // 2 : (x + 1) * rows, columns] = piece[:, half:]

    return whole_call(
        body,
        [((sz.gx * rows, 3 * sz.width), F32), ((sz.gx * rows, sz.width), F32)]
        + [((n,), F32) for _, _, n in small_cuts(sz)],
        1,
        (place, *pieces),
        "join_heads",
        [pltpu.VMEM((sz.n_grp,) + pieces[0].shape, BF16)],
    )


def join_slots(sz, sel):
    n = sel.shape[1]
    thirds = sel.reshape(sz.groups, n, 3, sz.lanes)
    own = thirds[..., : sz.used].transpose(2, 1, 0, 3).reshape(3, n, sz.groups * sz.used)
    own = own[..., : sz.width]
    first = thirds[..., sz.used : sz.used + sz.head].sum(axis=0).transpose(1, 0, 2)
    own = own.at[:, :, : sz.head].add(first)
    return own.transpose(1, 0, 2).reshape(n, 3 * sz.width)


def finish_tokens(sz, dnorm, tokens, grad_middle, gain):
    n = len(dnorm)

    def body(*refs):
        tok_ref, grad_ref, gain_ref = refs[n : n + 3]
        outs = refs[n + 3 :]
        e = refs[0][...].astype(F32)
        for ref in refs[1:n]:
            e += ref[...].astype(F32)
        hat, r = normalize(tok_ref[...].astype(F32))
        eg = e * gain_ref[...]
        inner = eg - jnp.mean(eg, axis=-1, keepdims=True)
        inner -= hat * jnp.mean(eg * hat, axis=-1, keepdims=True)
        total = (grad_ref[...] + r * inner).astype(BF16)
        for t in range(sz.parts):
            outs[t][...] = total[t * sz.block : (t + 1) * sz.block]

    return whole_call(
        body,
        [((sz.block, sz.width), BF16)] * sz.parts,
        0,
        (*dnorm, tokens, grad_middle, gain),
        "finish_tokens",
    )


def finish_middle(sz, mixed, middle, proj_bias):
    n = len(mixed)

    def body(*refs):
        middle_ref, bias_ref = refs[n : n + 2]
        outs = refs[n + 2 :]
        total = middle_ref[...] + bias_ref[...]
        for ref in refs[:n]:
            total += ref[...].astype(F32)
        total = total.astype(BF16)
        for t in range(sz.parts):
            outs[t][...] = total[t * sz.block : (t + 1) * sz.block]

    return whole_call(
        body,
        [((sz.block, sz.width), BF16)] * sz.parts,
        0,
        (*mixed, middle, proj_bias),
        "finish_middle",
    )


def unsort_rows(sz, place, docs, blocks):
    def body(place_ref, doc_ref, *refs):
        out_ref = refs[-1]
        for t in range(sz.parts):
            for a in range(4):
                src = source_grain(sz, doc_ref, 4 * ((place_ref[ROW] + t) % sz.parts) + a)
                out_ref[src] = refs[t][pl.ds(a * sz.grain, sz.grain), :].astype(F32)

    out = whole_call(
        body,
        [((sz.grains, sz.grain, sz.width), F32)],
        2,
        (place, docs, *blocks),
        "unsort_rows",
    )
    return out[0].reshape(sz.rows, sz.width)


def gather_near(sz, block):
    return [block, shift(block, "core", 2, 1)]


def gather_far(sz, block, before):
    far = []
    for k in range(1, sz.gx):
        along = after(before, shift(block, "gx", sz.gx, k))
        far += [along, shift(along, "core", 2, 1)]
    return far


def return_rows(sz, near, far, later):
    terms = [near[0], shift(near[1], "core", 2, 1)]
    for k in range(1, sz.gx):
        mine, other = far[2 * k - 2 : 2 * k]
        mine = (mine.astype(F32) + shift(other, "core", 2, 1).astype(F32)).astype(BF16)
        mine, later = lax.optimization_barrier((mine, later))
        terms.append(shift(mine, "gx", sz.gx, -k))
    return terms, later


def all_grp(sz, value):
    along = [value] + [shift(value, "gx", sz.gx, k) for k in range(1, sz.gx)]
    return along + [shift(v, "core", 2, 1) for v in along]


def after(gate, value):
    return lax.optimization_barrier((gate, value))[1]


def head_columns(sz, weight, hg):
    lead = weight.shape[:-1]
    pieces = []
    for third in range(3):
        full = weight[..., third * sz.width : (third + 1) * sz.width]
        spare = sz.groups * sz.used - sz.width
        if spare:
            full = jnp.pad(full, [(0, 0)] * len(lead) + [(0, spare)])
        own = lax.dynamic_slice_in_dim(full, hg * sz.used, sz.used, axis=len(lead))
        first = full[..., : sz.head] if third < 2 else jnp.zeros(lead + (sz.head,), weight.dtype)
        rest = sz.lanes - sz.used - sz.head
        pieces += [own, first]
        if rest:
            pieces.append(jnp.zeros(lead + (rest,), weight.dtype))
    return jnp.concatenate(pieces, axis=-1)


def weight_shares(sz, place, qkv_weight, fc_weight, proj_weight):
    share = sz.hidden // (sz.n_ctx * sz.n_grp)
    units = sz.n_ctx * share
    if not sz.aligned:
        mine = place[GX] * 2 + place[CORE]
        w_sel = head_columns(sz, qkv_weight, place[QUARTER])
        fc = fc_weight.reshape(sz.width, sz.n_ctx, sz.n_grp, share)
        fc = lax.dynamic_index_in_dim(fc, mine, 2, keepdims=False).reshape(sz.width, units)
        proj = proj_weight.reshape(sz.n_ctx, sz.n_grp, share, sz.width)
        proj = lax.dynamic_index_in_dim(proj, mine, 1, keepdims=False).reshape(units, sz.width)
        return w_sel, fc, proj

    def body(place_ref, qkv_ref, fc_in, proj_in, sel_ref, fc_ref, proj_ref):
        hg, mine = place_ref[QUARTER], place_ref[GX] * 2 + place_ref[CORE]
        for third in range(3):
            to, base = third * sz.lanes, third * sz.width
            end = jnp.zeros((sz.width, sz.lanes - sz.used), BF16)
            if third < 2:
                end = qkv_ref[:, base : base + 128][:, : sz.head]
                if sz.lanes - sz.used > sz.head:
                    end = jnp.concatenate(
                        [end, jnp.zeros((sz.width, sz.lanes - sz.used - sz.head), BF16)], axis=1
                    )
            for g in range(sz.groups):

                @pl.when(hg == g)
                def _():
                    own = qkv_ref[:, base : base + sz.width][:, g * sz.used : (g + 1) * sz.used]
                    sel_ref[:, to : to + sz.lanes] = jnp.concatenate([own, end], axis=1)

        wide = share * sz.n_grp
        for q in range(sz.n_grp):

            @pl.when(mine == q)
            def _():
                fc_ref[...] = jnp.concatenate(
                    [
                        fc_in[:, j * wide : (j + 1) * wide][:, q * share : (q + 1) * share]
                        for j in range(sz.n_ctx)
                    ],
                    axis=1,
                )

        for j in range(sz.n_ctx):
            at = pl.multiple_of(j * wide + mine * share, 16)
            proj_ref[j * share : (j + 1) * share, :] = proj_in[pl.ds(at, share), :]

    return whole_call(
        body,
        [((sz.width, 3 * sz.lanes), BF16), ((sz.width, units), BF16), ((units, sz.width), BF16)],
        1,
        (place, qkv_weight, fc_weight, proj_weight),
        "weight_shares",
    )


def body(
    tokens,
    ln1_gain,
    ln1_bias,
    qkv_weight,
    qkv_bias,
    out_weight,
    out_bias,
    ln2_gain,
    ln2_bias,
    fc_weight,
    fc_bias,
    proj_weight,
    proj_bias,
    doc_blocks,
    cotangent,
):
    rows, width = tokens.shape
    hidden = fc_weight.shape[1]
    n_ctx = lax.axis_size("hg") * lax.axis_size("part")
    n_grp = lax.axis_size("gx") * 2
    sz = Sizes(rows, width, hidden, doc_blocks.shape[1], n_ctx, n_grp)
    hg, part = lax.axis_index("hg"), lax.axis_index("part")
    gx, core = lax.axis_index("gx"), lax.axis_index("core")
    quarter = hg % sz.half * 2 + core
    my_part = part // 2 * 2 + hg // sz.half
    place = jnp.stack([quarter, my_part, core, gx, hg, part]).astype(jnp.int32)
    mine = gx * 2 + core

    def vector(v):
        return v.astype(F32)[None, :]

    gain1, bias1 = vector(ln1_gain), vector(ln1_bias)
    gain2, bias2 = vector(ln2_gain), vector(ln2_bias)
    share = hidden // (n_ctx * n_grp)
    b_sel = head_columns(sz, vector(qkv_bias), quarter)
    fc_b = lax.dynamic_index_in_dim(
        vector(fc_bias).reshape(1, n_ctx, n_grp, share), mine, 2, keepdims=False
    ).reshape(1, n_ctx * share)
    spare = sz.groups * sz.used - sz.width
    w_out = jnp.pad(out_weight, ((0, spare), (0, 0))) if spare else out_weight

    tok_parts, cot_parts = sort_rows(sz, place, doc_blocks, tokens, cotangent)
    tok_rows = jnp.concatenate(to_owner(sz, tok_parts), axis=0)
    docs = jnp.where(core == part % 2, doc_blocks, shift(doc_blocks, "core", 2, 1))

    chunks = []
    for k in range(sz.half):
        block = to_peer(sz, tok_rows, 2 * k)
        chunks += [block, to_peer(sz, block, 1)]

    qkv_weight, fc_weight, proj_weight, cot_parts = after(
        tok_rows, (qkv_weight, fc_weight, proj_weight, cot_parts)
    )
    w_sel, fc, proj = weight_shares(sz, place, qkv_weight, fc_weight, proj_weight)
    cot_rows = jnp.concatenate(to_owner(sz, cot_parts), axis=0)
    cot_near = gather_near(sz, cot_rows)
    cot_along = [shift(cot_rows, "gx", sz.gx, k) for k in range(1, sz.gx)]

    chunks = after(cot_rows, chunks)
    saved, att_out = attend_forward(sz, place, docs, chunks, gain1, bias1, w_sel, b_sel)
    cot_far = [b for along in cot_along for b in (along, shift(along, "core", 2, 1))]
    att_out = after((cot_along, cot_near), att_out)
    att = [to_peer(sz, att_out[k], k) for k in range(sz.groups)]
    middle, second = project_out(
        sz, place, att, tok_rows, w_out, vector(out_bias), gain2, bias2
    )

    sec_near = gather_near(sz, second)
    act_n, gh_n, back_n, fc_sum_n = feed_forward(sz, sec_near, cot_near, fc, fc_b, proj, "feed_forward_near")
    mixed_n = feed_forward_out(sz, act_n, proj)
    sec_far = gather_far(sz, second, (back_n, mixed_n))
    act_f, gh_f, back_f, fc_sum_f = feed_forward(sz, sec_far, cot_far, fc, fc_b, proj, "feed_forward_far")
    back, act_f = return_rows(sz, back_n, back_f, act_f)
    ff_sent = feed_forward_weights(
        sz, place, sec_near + sec_far, gh_n + gh_f, act_n + act_f, cot_near + cot_far
    )
    mixed_f = feed_forward_out(sz, after(ff_sent, act_f), proj)
    back = after(mixed_f, back)
    grad_middle, branch, mid_sums, datt_out = middle_backward(
        sz, place, back, middle, cot_rows, w_out, gain2
    )
    datt = [to_peer(sz, datt_out[k], k) for k in range(sz.groups)]

    band = width // n_ctx
    half = width // 2
    n_rows = band // sz.gx
    ff_got = [shift(ff_sent[s], "part", sz.parts, s) for s in range(1, sz.parts)]
    mixed, _ = return_rows(sz, mixed_n, mixed_f, place)

    def over_gx(value):
        value = value.reshape(n_ctx, sz.gx, n_rows, value.shape[2])
        pieces = []
        for k in range(sz.gx):
            piece = lax.dynamic_index_in_dim(value, (gx + k) % sz.gx, 1, keepdims=False)
            pieces.append(shift(piece, "gx", sz.gx, k) if k else piece)
        return pieces

    own, other = out_weights(sz, place, att, branch)
    own = own.astype(F32) + shift(other, "core", 2, 1).astype(F32)
    out_terms = over_gx(own.astype(BF16).reshape(n_ctx, band, half))

    dqkv, qkv_sum, ln1_sums, dnorm_out = attend_backward(sz, place, docs, saved, w_sel, datt)
    dnorm = [dnorm_out[0], to_peer(sz, dnorm_out[1], 1)]
    for k in range(1, sz.half):
        both = dnorm_out[2 * k].astype(F32) + to_peer(sz, dnorm_out[2 * k + 1], 1).astype(F32)
        both = both.astype(BF16)
        dnorm.append(to_peer(sz, both, 2 * k))
    grad_parts = finish_tokens(sz, dnorm, tok_rows, grad_middle, gain1)
    grad_tokens = unsort_rows(sz, place, doc_blocks, from_owner(sz, grad_parts))

    out_parts = finish_middle(sz, after(dqkv, mixed), middle, vector(proj_bias))
    output = unsort_rows(sz, place, doc_blocks, from_owner(sz, out_parts))

    d_sel = qkv_weights(sz, saved[1], after((both, ff_got, mixed, own), dqkv))
    sel_terms = after(grad_parts, over_gx(d_sel))
    tail = pack_vectors(sz, place, ln1_sums, qkv_sum, mid_sums, [fc_sum_n, fc_sum_f])
    n_tail = tail.shape[1]
    pieces = pack_sums(sz, place, sel_terms, out_terms, tail)
    pieces = [pieces[0]] + [shift(pieces[s], "part", sz.parts, s) for s in range(1, sz.parts)]
    blocks = sum_packed(sz, pieces, n_rows, n_tail)
    blocks = [blocks[0]] + [shift(blocks[k], "hg", sz.groups, k) for k in range(1, sz.groups)]
    sums = unpack_sums(sz, place, blocks, n_rows, n_tail)
    grad_qkv, grad_out, *cuts = join_heads(sz, place, all_grp(sz, sums), n_rows, n_tail)

    ff_near = sum_arrays(sz, [ff_sent[0]] + after((d_sel, dnorm), ff_got), "sum_parts")
    ff_share = sum_first(sz, lax.all_to_all(ff_near, "hg", 0, 0, tiled=True), "sum_groups")
    grad_fc, grad_proj = join_shares(sz, place, all_grp(sz, ff_share))

    g_ln1_gain, g_ln1_bias, g_qkv_bias, g_out_bias, g_ln2_gain, g_ln2_bias, g_fc_bias, g_proj_bias = cuts
    return (
        output,
        grad_tokens,
        g_ln1_gain,
        g_ln1_bias,
        grad_qkv,
        g_qkv_bias,
        grad_out,
        g_out_bias,
        g_ln2_gain,
        g_ln2_bias,
        grad_fc,
        g_fc_bias,
        grad_proj,
        g_proj_bias,
    )


def solution(mesh):
    n_grp, n_ctx = mesh.devices.shape
    split = P(GRP + CTX, None)

    def run(tokens, *rest):
        rows = tokens.shape[0] // (n_grp * n_ctx)
        parts = rows // min(rows // 2, SEQ_LEN // n_ctx)
        fine = Mesh(mesh.devices.reshape(n_grp // 2, 2, n_ctx // parts, parts), GRP + CTX)
        each = jax.shard_map(
            body,
            mesh=fine,
            in_specs=(split,) + (P(),) * 12 + (P(GRP, None), split),
            out_specs=(
                split,
                split,
                P(CTX),
                P(CTX),
                P(CTX, None),
                P(CTX),
                P(CTX, None),
                P(CTX),
                P(CTX),
                P(CTX),
                P(CTX, None),
                P(CTX),
                P(CTX, None),
                P(CTX),
            ),
            check_vma=False,
        )
        return each(tokens, *rest)

    return run
```

```python
import functools
import math

import jax
import jax.numpy as jnp
from jax import lax
from jax.experimental import pallas as pl
from jax.experimental.pallas import tpu as pltpu
from jax.sharding import Mesh
from jax.sharding import PartitionSpec as P

HEADS = 12
SEQ_LEN = 2048
FAR = 1e30
F32 = jnp.float32
BF16 = jnp.bfloat16
GRP = ("gx", "core")
CTX = ("hg", "part")
VMEM_BYTES = 56 * 1024 * 1024


QUARTER, PART, CORE, GX, HG, ROW = range(6)


class Sizes:
    def __init__(self, rows, width, hidden, docs, n_ctx, n_grp):
        self.rows, self.width, self.hidden, self.docs = rows, width, hidden, docs
        self.n_ctx, self.n_grp = n_ctx, n_grp
        self.head = width // HEADS
        self.block = min(rows // 2, SEQ_LEN // n_ctx)
        self.parts = rows // self.block
        self.groups = n_ctx // self.parts
        self.grain = self.block // 4
        self.grains = rows // self.grain
        self.per = -(-HEADS // self.groups)
        self.used = self.per * self.head
        self.lanes = -(-((self.per + 1) * self.head) // 128) * 128
        self.span = n_ctx * self.block
        self.half = self.groups // 2
        self.tile = 256
        self.steps = self.span // self.tile
        self.gx = n_grp // 2
        self.scale = self.head ** (-0.5)
        band, share = width // n_ctx, hidden // (n_ctx * n_grp)
        self.aligned = band % 32 == 0 and share % 32 == 0 and share * n_ctx == width
        self.packed = band % (32 * self.gx // 2) == 0 and 3 * self.lanes == width


def peer(sz, quarter, at, sign):
    return (((quarter >> 1) + sign * (at >> 1)) % sz.half) * 2 + ((quarter + at) & 1)


def dot(a, b):
    return lax.dot_general(a, b, (((1,), (0,)), ((), ())), preferred_element_type=F32)


def dot_nt(a, b):
    return lax.dot_general(a, b, (((1,), (1,)), ((), ())), preferred_element_type=F32)


def dot_tn(a, b):
    return lax.dot_general(a, b, (((0,), (0,)), ((), ())), preferred_element_type=F32)


def dot_split(mask, value, transposed):
    high = value.astype(BF16)
    low = (value - high.astype(F32)).astype(BF16)
    mul = dot_tn if transposed else dot
    return mul(mask, high) + mul(mask, low)


def shift(value, axis, size, step):
    return lax.ppermute(value, axis, [(i, (i + step) % size) for i in range(size)])


def to_peer(sz, value, at):
    if at == 0:
        return value
    pairs = []
    for core in range(2):
        for hg in range(sz.groups):
            to = (hg // sz.half) * sz.half + (hg + at // 2) % sz.half
            pairs.append((core * sz.groups + hg, ((core + at) % 2) * sz.groups + to))
    return lax.ppermute(value, ("core", "hg"), pairs)


def owner_pairs(sz, t):
    pairs = []
    for core in range(2):
        for hg in range(sz.groups):
            for row in range(sz.parts):
                part = (row + t) % sz.parts
                to_hg = (part % 2) * sz.half + hg // 2
                to_row = (part // 2) * 2 + core
                to = ((hg % 2) * sz.groups + to_hg) * sz.parts + to_row
                pairs.append(((core * sz.groups + hg) * sz.parts + row, to))
    return pairs


def to_owner(sz, blocks):
    return [lax.ppermute(b, ("core",) + CTX, owner_pairs(sz, t)) for t, b in enumerate(blocks)]


def from_owner(sz, blocks):
    return [
        lax.ppermute(b, ("core",) + CTX, [(b_, a_) for a_, b_ in owner_pairs(sz, t)])
        for t, b in enumerate(blocks)
    ]


def cost(flops, *arrays):
    size = sum(math.prod(a.shape) * a.dtype.itemsize for a in arrays)
    return pl.CostEstimate(flops=int(flops), bytes_accessed=int(size), transcendentals=0)


def whole_call(body, outs, n_scalars, args, name, scratch=(), flops=0):
    shapes = [jax.ShapeDtypeStruct(s, t) for s, t in outs]
    specs = [pl.BlockSpec(memory_space=pltpu.SMEM)] * n_scalars
    specs += [pl.BlockSpec(memory_space=pltpu.VMEM)] * (len(args) - n_scalars)
    return pl.pallas_call(
        body,
        out_shape=shapes,
        in_specs=specs,
        out_specs=[pl.BlockSpec(memory_space=pltpu.VMEM)] * len(outs),
        scratch_shapes=list(scratch),
        compiler_params=pltpu.CompilerParams(vmem_limit_bytes=VMEM_BYTES),
        cost_estimate=cost(flops, *args, *shapes),
        name=name,
    )(*args)


def source_grain(sz, doc_ref, place):
    is_long = [(doc_ref[0, d] == sz.block).astype(jnp.int32) for d in range(sz.docs)]
    longs = sum(is_long)
    seen_long, seen_short, begin, source = 0, 0, 0, 0
    for d in range(sz.docs):
        count = doc_ref[0, d] // sz.grain
        first = jnp.where(is_long[d] == 1, 4 * seen_long, 4 * longs + seen_short)
        inside = (place >= first) & (place < first + count)
        source = source + jnp.where(inside, begin + place - first, 0)
        seen_long = seen_long + is_long[d]
        seen_short = seen_short + jnp.where(is_long[d] == 1, 0, count)
        begin = begin + count
    return source


def part_is_long(sz, doc_ref, part):
    longs = sum((doc_ref[0, d] == sz.block).astype(jnp.int32) for d in range(sz.docs))
    return part < longs


def sort_rows(sz, place, docs, tokens, cotangent):
    def body(place_ref, doc_ref, tok_ref, cot_ref, *outs):
        for t in range(sz.parts):
            for a in range(4):
                src = source_grain(sz, doc_ref, 4 * ((place_ref[ROW] + t) % sz.parts) + a)
                at = pl.ds(a * sz.grain, sz.grain)
                outs[t][at, :] = tok_ref[src]
                outs[sz.parts + t][at, :] = cot_ref[src]

    shape = (sz.grains, sz.grain, sz.width)
    out = whole_call(
        body,
        [((sz.block, sz.width), BF16)] * (2 * sz.parts),
        2,
        (place, docs, tokens.reshape(shape), cotangent.reshape(shape)),
        "sort_rows",
    )
    return out[: sz.parts], out[sz.parts :]


def block_rows(sz, place_ref, quarter, t):
    at = quarter * sz.parts + (place_ref[PART] - t) % sz.parts
    return pl.ds(pl.multiple_of(at * sz.block, sz.block), sz.block)


def normalize(x):
    center = x - jnp.mean(x, axis=-1, keepdims=True)
    spread = jnp.mean(center * center, axis=-1, keepdims=True)
    r = lax.rsqrt(spread + 1e-05)
    return center * r, r


def pair_masks(sz, step, long_part):
    keys = (step + 1) * sz.tile
    q_row = step * sz.tile + lax.broadcasted_iota(jnp.int32, (sz.tile, 1), 0)
    k_row = lax.broadcasted_iota(jnp.int32, (1, keys), 1)
    q_doc = jnp.where(long_part, 0, (q_row % sz.block) // sz.grain)
    k_doc = jnp.where(long_part, 0, (k_row % sz.block) // sz.grain)
    k_in = jnp.where(long_part, k_row % sz.block, k_row % sz.grain)
    first = (k_row < sz.block) & (k_in == 0)
    same = q_doc == k_doc
    visible = same & (k_row <= q_row)
    select = same & (k_row < q_row) & jnp.logical_not(first)
    return visible, select


def slot_mask(sz, slot):
    lane = lax.broadcasted_iota(jnp.int32, (1, sz.lanes), 1)
    return lane // sz.head == slot


def lower_mask(sz):
    row = lax.broadcasted_iota(jnp.int32, (sz.tile, sz.tile), 0)
    col = lax.broadcasted_iota(jnp.int32, (sz.tile, sz.tile), 1)
    return jnp.where(row > col, 1.0, 0.0).astype(BF16)


def penalty_of(sz, step, long_part, lower, q_slot, k, carry):
    visible, select = pair_masks(sz, step, long_part)
    positive = jnp.maximum(dot_nt(q_slot, k), 0.0)
    chosen = jnp.where(select, positive * positive * (1.0 / sz.block), 0.0)
    penalty = dot_split(lower, chosen, False) + carry
    return jnp.where(visible, penalty, FAR), chosen, positive, select


def attend_forward(sz, place, docs, chunks, gain, bias, w_sel, b_sel):
    lw = sz.lanes
    n = len(chunks)

    def body(place_ref, doc_ref, *refs):
        xs = refs[:n]
        gain_ref, bias_ref, w_ref, b_ref = refs[n : n + 4]
        qkv_ref, normed_ref, hat_ref, lse_ref, out_ref, carry_ref = refs[n + 4 : n + 10]
        att_refs = refs[n + 10 :]
        quarter = place_ref[QUARTER]
        long_part = part_is_long(sz, doc_ref, place_ref[PART])
        for i in range(n):
            hat, _ = normalize(xs[i][...].astype(F32))
            normed = (hat * gain_ref[...] + bias_ref[...]).astype(BF16)
            packed = (dot(normed, w_ref[...]) + b_ref[...]).astype(BF16)
            low = hat.astype(BF16)
            for t in range(sz.parts):
                at = block_rows(sz, place_ref, peer(sz, quarter, i, -1), t)
                here = slice(t * sz.block, (t + 1) * sz.block)
                hat_ref[at, :] = low[here]
                normed_ref[at, :] = normed[here]
                qkv_ref[at, :] = packed[here]
        lower = lower_mask(sz)
        lane = lax.broadcasted_iota(jnp.int32, (1, 128), 1)
        carry_ref[...] = jnp.zeros_like(carry_ref)
        for step in range(sz.steps):
            keys = (step + 1) * sz.tile
            rows = slice(step * sz.tile, keys)
            q = qkv_ref[rows, :lw] * sz.scale
            k = qkv_ref[:keys, lw : 2 * lw]
            v = qkv_ref[:keys, 2 * lw :]
            q_slot = jnp.where(slot_mask(sz, sz.per), q, 0)
            pen, chosen, _, _ = penalty_of(
                sz, step, long_part, lower, q_slot, k, carry_ref[step : step + 1, :keys]
            )
            if step + 1 < sz.steps:
                carry_ref[step + 1 : step + 2, :keys] = carry_ref[step : step + 1, :keys] + jnp.sum(
                    chosen, axis=0, keepdims=True
                )
            total = jnp.zeros((sz.tile, lw), F32)
            lse = jnp.zeros((sz.tile, 128), F32)
            for h in range(sz.per):
                mask = slot_mask(sz, h)
                logits = dot_nt(jnp.where(mask, q, 0), k) - pen
                top = jnp.max(logits, axis=1, keepdims=True)
                weights = jnp.exp(logits - top)
                weight = jnp.sum(weights, axis=1, keepdims=True)
                mixed = dot(weights.astype(BF16), v) / weight
                total = jnp.where(mask, mixed, total)
                lse = jnp.where(lane == h, top + jnp.log(weight), lse)
            out_ref[rows, :] = total
            lse_ref[rows, :] = lse
        for i in range(n):
            for t in range(sz.parts):
                at = block_rows(sz, place_ref, peer(sz, quarter, i, 1), t)
                att_refs[i][t * sz.block : (t + 1) * sz.block, :] = out_ref[at, : sz.used].astype(BF16)

    outs = [
        ((sz.span, 3 * lw), BF16),
        ((sz.span, sz.width), BF16),
        ((sz.span, sz.width), BF16),
        ((sz.span, 128), F32),
        ((sz.span, lw), F32),
        ((sz.steps, sz.span), F32),
    ] + [((sz.rows, sz.used), BF16)] * sz.groups
    out = whole_call(body, outs, 2, (place, docs, *chunks, gain, bias, w_sel, b_sel), "attend_forward", flops=9e9)
    return out[:6], out[6:]


def attend_backward(sz, place, docs, saved, w_sel, grads):
    lw = sz.lanes
    qkv, _, hat, lse, att, carry = saved

    def body(place_ref, doc_ref, qkv_ref, hat_ref, lse_ref, att_ref, carry_ref, w_ref, *refs):
        grad_refs = refs[: sz.groups]
        outs = refs[sz.groups :]
        dqkv_ref, sums_ref, lnsum_ref = outs[:3]
        dnorm_refs = outs[3 : 3 + sz.groups]
        dout, dk_sum, dv_sum, behind = outs[3 + sz.groups :]
        quarter = place_ref[QUARTER]
        long_part = part_is_long(sz, doc_ref, place_ref[PART])
        dout[...] = jnp.zeros_like(dout)
        for i in range(sz.groups):
            for t in range(sz.parts):
                at = block_rows(sz, place_ref, peer(sz, quarter, i, -1), t)
                dout[at, : sz.used] = grad_refs[i][t * sz.block : (t + 1) * sz.block, :]
        dk_sum[...] = jnp.zeros_like(dk_sum)
        dv_sum[...] = jnp.zeros_like(dv_sum)
        behind[...] = jnp.zeros_like(behind)
        lower = lower_mask(sz)
        for step in reversed(range(sz.steps)):
            keys = (step + 1) * sz.tile
            rows = slice(step * sz.tile, keys)
            q = qkv_ref[rows, :lw] * sz.scale
            k = qkv_ref[:keys, lw : 2 * lw]
            v = qkv_ref[:keys, 2 * lw :]
            d_rows = dout[rows, :]
            dot_rows = d_rows.astype(F32) * att_ref[rows, :]
            last = slot_mask(sz, sz.per)
            q_slot = jnp.where(last, q, 0)
            pen, _, positive, select = penalty_of(
                sz, step, long_part, lower, q_slot, k, carry_ref[step : step + 1, :keys]
            )
            dpen = jnp.zeros((sz.tile, keys), F32)
            dq = jnp.zeros((sz.tile, lw), F32)
            for h in range(sz.per):
                mask = slot_mask(sz, h)
                q_h = jnp.where(mask, q, 0)
                d_h = jnp.where(mask, d_rows, 0)
                probs = jnp.exp(dot_nt(q_h, k) - pen - lse_ref[rows, h : h + 1])
                delta = jnp.sum(jnp.where(mask, dot_rows, 0.0), axis=1, keepdims=True)
                ds = probs * (dot_nt(d_h, v) - delta)
                dpen = dpen - ds
                ds_low = ds.astype(BF16)
                dq = jnp.where(mask, dot(ds_low, k), dq)
                dk_sum[:keys, :] += dot_tn(ds_low, q_h)
                dv_sum[:keys, :] += dot_tn(probs.astype(BF16), d_h)
            dchosen = dot_split(lower, dpen, True) + behind[:1, :keys]
            behind[:1, :keys] += jnp.sum(dpen, axis=0, keepdims=True)
            ds_low = jnp.where(select, positive * dchosen * (2.0 / sz.block), 0.0).astype(BF16)
            dq = jnp.where(last, dot(ds_low, k), dq)
            dk_sum[:keys, :] += dot_tn(ds_low, q_slot)
            dqkv_ref[rows, :lw] = (dq * sz.scale).astype(BF16)
        dqkv_ref[:, lw : 2 * lw] = dk_sum[...].astype(BF16)
        dqkv_ref[:, 2 * lw :] = dv_sum[...].astype(BF16)
        sums_ref[...] = jnp.sum(dqkv_ref[...].astype(F32), axis=0, keepdims=True)
        gain_sum = jnp.zeros((1, sz.width), F32)
        bias_sum = jnp.zeros((1, sz.width), F32)
        for i in range(sz.groups):
            for t in range(sz.parts):
                at = block_rows(sz, place_ref, peer(sz, quarter, i, 1), t)
                dnorm = dot_nt(dqkv_ref[at, :], w_ref[...])
                dnorm_refs[i][t * sz.block : (t + 1) * sz.block, :] = dnorm.astype(BF16)
                bias_sum += jnp.sum(dnorm, axis=0, keepdims=True)
                gain_sum += jnp.sum(dnorm * hat_ref[at, :].astype(F32), axis=0, keepdims=True)
        lnsum_ref[0:1, :] = gain_sum
        lnsum_ref[1:2, :] = bias_sum

    outs = [((sz.span, 3 * lw), BF16), ((1, 3 * lw), F32), ((2, sz.width), F32)]
    outs += [((sz.rows, sz.width), BF16)] * sz.groups
    scratch = [
        pltpu.VMEM((sz.span, lw), BF16),
        pltpu.VMEM((sz.span, lw), F32),
        pltpu.VMEM((sz.span, lw), F32),
        pltpu.VMEM((8, sz.span), F32),
    ]
    out = whole_call(
        body, outs, 2, (place, docs, qkv, hat, lse, att, carry, w_sel, *grads), "attend_backward", scratch, 17e9
    )
    return out[0], out[1], out[2], out[3:]


def project_out(sz, place, att, tokens, out_weight, out_bias, gain, bias):
    def body(place_ref, *refs):
        att_refs = refs[: sz.groups]
        tok_ref, w_ref, b_ref, gain_ref, bias_ref, middle_ref, second_ref = refs[sz.groups :]
        total = tok_ref[...].astype(F32) + b_ref[...]
        for k in range(sz.groups):
            at = pl.multiple_of(peer(sz, place_ref[QUARTER], k, -1) * sz.used, 16)
            total += dot(att_refs[k][...], w_ref[pl.ds(at, sz.used), :])
        middle_ref[...] = total
        hat, _ = normalize(total)
        second_ref[...] = (hat * gain_ref[...] + bias_ref[...]).astype(BF16)

    outs = [((sz.rows, sz.width), F32), ((sz.rows, sz.width), BF16)]
    return whole_call(
        body, outs, 1, (place, *att, tokens, out_weight, out_bias, gain, bias), "project_out"
    )


def feed_forward(sz, second, cot, fc, fc_bias, proj, name):
    n = len(second)
    units = fc.shape[1]
    root = math.sqrt(2.0 / math.pi)

    def body(*refs):
        second_refs, cot_refs = refs[:n], refs[n : 2 * n]
        fc_ref, bias_ref, proj_ref = refs[2 * n : 2 * n + 3]
        outs = refs[2 * n + 3 :]
        act_refs, grad_refs, back_refs, sums_ref = outs[:n], outs[n : 2 * n], outs[2 * n : 3 * n], outs[3 * n]
        total = jnp.zeros((1, units), F32)
        for i in range(n):
            hidden = dot(second_refs[i][...], fc_ref[...]) + bias_ref[...]
            square = hidden * hidden
            t = jnp.tanh(root * (hidden + 0.044715 * hidden * square))
            half = 0.5 * (1.0 + t)
            act_refs[i][...] = (hidden * half).astype(BF16)
            slope = half + 0.5 * hidden * (1.0 - t * t) * (root * (1.0 + 3.0 * 0.044715 * square))
            grad = (dot_nt(cot_refs[i][...], proj_ref[...]) * slope).astype(BF16)
            grad_refs[i][...] = grad
            back_refs[i][...] = dot_nt(grad, fc_ref[...]).astype(BF16)
            total += jnp.sum(grad.astype(F32), axis=0, keepdims=True)
        sums_ref[...] = total

    outs = [((sz.rows, units), BF16)] * (2 * n) + [((sz.rows, sz.width), BF16)] * n + [((1, units), F32)]
    out = whole_call(body, outs, 0, (*second, *cot, fc, fc_bias, proj), name)
    return out[:n], out[n : 2 * n], out[2 * n : 3 * n], out[3 * n]


def middle_backward(sz, place, back, middle, cot, out_weight, gain, att):
    n_back = len(back)
    half = sz.width // 2

    def body(place_ref, *refs):
        back_refs = refs[:n_back]
        att_refs = refs[n_back : n_back + sz.groups]
        rest = refs[n_back + sz.groups :]
        cot_ref, middle_ref, w_ref, gain_ref, grad_ref, own_ref, other_ref, sums_ref = rest[:8]
        datt_refs = rest[8:]
        cot = cot_ref[...].astype(F32)
        e = back_refs[0][...].astype(F32)
        for ref in back_refs[1:]:
            e += ref[...].astype(F32)
        hat, r = normalize(middle_ref[...])
        eg = e * gain_ref[...]
        inner = eg - jnp.mean(eg, axis=-1, keepdims=True)
        inner -= hat * jnp.mean(eg * hat, axis=-1, keepdims=True)
        grad = cot + r * inner
        grad_ref[...] = grad
        branch = grad.astype(BF16)
        core = place_ref[CORE]
        for k in range(sz.groups):
            at = pl.multiple_of(peer(sz, place_ref[QUARTER], k, -1) * sz.used, 16)

            @pl.when(at < sz.width)
            def _():
                grad_w = dot_tn(att_refs[k][...], branch).astype(BF16)
                left, right = grad_w[:, :half], grad_w[:, half:]
                own_ref[pl.ds(at, sz.used), :] = jnp.where(core == 0, left, right)
                other_ref[pl.ds(at, sz.used), :] = jnp.where(core == 0, right, left)

        for k in range(sz.groups):
            at = pl.multiple_of(peer(sz, place_ref[QUARTER], k, 1) * sz.used, 16)
            datt_refs[k][...] = dot_nt(branch, w_ref[pl.ds(at, sz.used), :]).astype(BF16)
        sums_ref[0:1, :] = jnp.sum(e * hat, axis=0, keepdims=True)
        sums_ref[1:2, :] = jnp.sum(e, axis=0, keepdims=True)
        sums_ref[2:3, :] = jnp.sum(branch.astype(F32), axis=0, keepdims=True)
        sums_ref[3:4, :] = jnp.sum(cot, axis=0, keepdims=True)

    outs = [((sz.rows, sz.width), F32)] + [((sz.width, half), BF16)] * 2 + [((4, sz.width), F32)]
    outs += [((sz.rows, sz.used), BF16)] * sz.groups
    out = whole_call(body, outs, 1, (place, *back, *att, cot, middle, out_weight, gain), "middle_backward")
    return out[0], out[1:3], out[3], out[4:]


def feed_forward_weights(sz, second, grad_hidden, act, cot):
    n = len(second)
    width, units = sz.width, act[0].shape[1]
    band, share = width // sz.n_ctx, units // sz.n_ctx
    both = band * units // width + share

    if not sz.aligned:
        second, grad_hidden, act, cot = (jnp.concatenate(v, axis=0) for v in (second, grad_hidden, act, cot))
        d_fc = dot_tn(second, grad_hidden).astype(BF16).reshape(sz.groups, sz.parts, -1, width)
        d_proj = dot_tn(act, cot).astype(BF16).reshape(sz.groups, sz.parts, -1, width)
        return jnp.concatenate([d_fc, d_proj], axis=2)

    def body(*refs):
        second_refs, grad_refs, act_refs, cot_refs = (refs[i * n : (i + 1) * n] for i in range(4))
        out_ref = refs[-1]
        d_fc = sum(dot_tn(x[...], g[...]) for x, g in zip(second_refs, grad_refs)).astype(BF16)
        for i in range(sz.n_ctx):
            out_ref[i // sz.parts, i % sz.parts, :band, :] = d_fc[i * band : (i + 1) * band, :]
        d_proj = sum(dot_tn(a[...], c[...]) for a, c in zip(act_refs, cot_refs)).astype(BF16)
        for i in range(sz.n_ctx):
            out_ref[i // sz.parts, i % sz.parts, band:, :] = d_proj[i * share : (i + 1) * share, :]

    return whole_call(
        body,
        [((sz.groups, sz.parts, both, width), BF16)],
        0,
        (*second, *grad_hidden, *act, *cot),
        "feed_forward_weights",
    )[0]


def feed_forward_out(sz, act, proj):
    n = len(act)

    def body(*refs):
        for i in range(n):
            refs[n + 1 + i][...] = dot(refs[i][...], refs[n][...]).astype(BF16)

    return whole_call(body, [((sz.rows, sz.width), BF16)] * n, 0, (*act, proj), "feed_forward_out")


def sum_arrays(sz, pieces, name):
    def body(*refs):
        refs[-1][...] = sum(r[...].astype(F32) for r in refs[:-1]).astype(BF16)

    return whole_call(body, [(pieces[0].shape, BF16)], 0, tuple(pieces), name)[0]


def sum_groups(sz, place, got):
    shape = got.shape[2:]
    if not sz.aligned:
        total = jnp.roll(got.astype(F32).sum(axis=0), -place[ROW], axis=0).astype(BF16)
        return [total[s] for s in range(sz.parts)]

    def body(place_ref, got_ref, *outs):
        for s in range(sz.parts):
            at = (place_ref[ROW] + s) % sz.parts
            outs[s][...] = sum(got_ref[k, at].astype(F32) for k in range(sz.groups)).astype(BF16)

    return whole_call(body, [(shape, BF16)] * sz.parts, 1, (place, got), "sum_groups")


def pack_sums(sz, place, sel, out, tail):
    rows, lanes = sel[0].shape[1:]
    n_tail, n_out = tail.shape[1], out[0].shape[1] // 2
    full = rows + n_tail + n_out
    if not sz.packed:
        sel = sum(t.astype(F32) for t in sel).astype(BF16)
        out = sum(t.astype(F32) for t in out).astype(BF16)
        out = jnp.concatenate([out[:, :n_out], out[:, n_out:]], axis=2)
        both = jnp.concatenate([sel, tail, out], axis=1).reshape((sz.groups, sz.parts, full, lanes))
        both = jnp.roll(both, (-place[HG], -place[ROW]), axis=(0, 1))
        return [both[:, s] for s in range(sz.parts)]
    n = len(sel)

    def body(place_ref, *refs):
        tail_ref, outs = refs[n + 2], refs[n + 3 :]
        for k in range(sz.groups):
            for s in range(sz.parts):
                to = ((place_ref[HG] + k) % sz.groups) * sz.parts + (place_ref[ROW] + s) % sz.parts
                outs[s][k, :rows, :] = sum(r[to].astype(F32) for r in refs[:n]).astype(BF16)
                outs[s][k, rows : rows + n_tail, :] = tail_ref[to]
                total = (refs[n][to].astype(F32) + refs[n + 1][to].astype(F32)).astype(BF16)
                outs[s][k, rows + n_tail :, : lanes // 2] = total[:n_out]
                outs[s][k, rows + n_tail :, lanes // 2 :] = total[n_out:]

    return whole_call(
        body, [((sz.groups, full, lanes), BF16)] * sz.parts, 1, (place, *sel, *out, tail), "pack_sums"
    )


def add_halves(value):
    half = value.shape[-2] // 2
    value = value.astype(F32)
    return value[..., :half, :] + value[..., half:, :]


def split_halves(value, axis):
    high = value.astype(BF16)
    return jnp.concatenate([high, (value - high.astype(F32)).astype(BF16)], axis=axis)


def sum_packed(sz, pieces, rows, n_tail):
    end = rows + n_tail
    if not sz.packed:
        total = sum(p.astype(F32) for p in pieces).astype(BF16)
        tail = split_halves(sum(add_halves(p[:, rows:end]) for p in pieces), 1)
        total = jnp.concatenate([total[:, :rows], tail, total[:, end:]], axis=1)
        return [total[k] for k in range(sz.groups)]
    n = len(pieces)

    def body(*refs):
        for k in range(sz.groups):
            out = refs[n + k]
            for cut in (slice(0, rows), slice(end, None)):
                out[cut, :] = sum(r[k, cut, :].astype(F32) for r in refs[:n]).astype(BF16)
            out[rows:end, :] = split_halves(sum(add_halves(r[k, rows:end, :]) for r in refs[:n]), 0)

    return whole_call(body, [(pieces[0].shape[1:], BF16)] * sz.groups, 0, tuple(pieces), "sum_packed")


def unpack_sums(sz, place, blocks, rows, n_tail):
    full, lanes = blocks[0].shape
    end = rows + n_tail
    if not sz.packed:
        got = jnp.stack(blocks)
        total = got.astype(F32).sum(axis=0).astype(BF16)
        sel = got[:, :rows].astype(F32)
        sel = sel[: sz.half] + sel[sz.half :]
        sel = jnp.roll(sel[::-1], place[HG] + 1, axis=0).astype(BF16).reshape(-1, lanes)
        tail = split_halves(add_halves(got[:, rows:end]).sum(axis=0), 0)
        return jnp.concatenate([sel, tail, total[end:]], axis=0)

    def body(place_ref, *refs):
        blocks, out_ref = refs[: sz.groups], refs[sz.groups]
        for k in range(sz.half):
            at = pl.multiple_of(((place_ref[HG] - k) % sz.half) * rows, 16)
            total = blocks[k][:rows, :].astype(F32) + blocks[k + sz.half][:rows, :].astype(F32)
            out_ref[pl.ds(at, rows), :] = total.astype(BF16)
        at = sz.half * rows
        out_ref[at : at + n_tail, :] = split_halves(sum(add_halves(r[rows:end, :]) for r in blocks), 0)
        out_ref[at + n_tail :, :] = sum(r[end:, :].astype(F32) for r in blocks).astype(BF16)

    shape = (sz.half * rows + full - rows, lanes)
    return whole_call(body, [(shape, BF16)], 1, (place, *blocks), "unpack_sums")[0]


def small_cuts(sz):
    band, units = sz.width // sz.n_ctx, sz.hidden // sz.n_ctx
    one = [(0, i * band, band) for i in range(6)]
    return one[:2] + [(1, 0, 3 * band)] + one[2:5] + [(1, 3 * band, units)] + one[5:]


def pack_vectors(sz, place, ln1, qkv, middle, fc_sums):
    band, units = sz.width // sz.n_ctx, sz.hidden // sz.n_ctx
    share = units // sz.n_grp
    w3 = 3 * sz.lanes
    lanes = w3

    if not sz.packed:
        hg, mine = place[QUARTER], place[GX] * 2 + place[CORE]
        placed = jnp.zeros((sz.groups, 1, w3), F32)
        placed = lax.dynamic_update_slice(placed, qkv[None], (hg, 0, 0))
        fc_placed = jnp.zeros((sz.n_ctx, sz.n_grp, share), F32)
        fc_placed = lax.dynamic_update_slice(fc_placed, sum(fc_sums).reshape(sz.n_ctx, 1, share), (0, mine, 0))
        vectors = [ln1[0], ln1[1], join_slots(sz, placed)[0], middle[2], middle[0], middle[1]]
        vectors += [fc_placed.reshape(-1), middle[3]]
        out = jnp.zeros((sz.n_ctx, 8, lanes), F32)
        for v, (row, at, n) in zip(vectors, small_cuts(sz)):
            out = out.at[:, row, at : at + n].set(v.reshape(sz.n_ctx, n))
        return split_halves(out, 1)

    def body(place_ref, ln1_ref, qkv_ref, mid_ref, *refs):
        out_ref, held, fc_held, whole = refs[len(fc_sums) :]
        hg, mine = place_ref[QUARTER], place_ref[GX] * 2 + place_ref[CORE]
        held[...] = jnp.zeros_like(held)
        for g in range(sz.groups):

            @pl.when(hg == g)
            def _():
                for third in range(3):
                    at = third * sz.width + g * sz.used
                    held[0:1, at : at + sz.used] = qkv_ref[:, third * sz.lanes : third * sz.lanes + sz.used]

        for third in range(3):
            at, base = third * sz.width, third * sz.lanes + sz.used
            held[0:1, at : at + sz.head] += qkv_ref[:, base : base + sz.head]
        fc = sum(r[...] for r in refs[: len(fc_sums)])
        fc_held[...] = jnp.zeros_like(fc_held)
        for q in range(sz.n_grp):

            @pl.when(mine == q)
            def _():
                for j in range(sz.n_ctx):
                    fc_held[j : j + 1, q * share : (q + 1) * share] = fc[:, j * share : (j + 1) * share]

        whole[...] = jnp.zeros_like(whole)
        for j in range(sz.n_ctx):
            cut = slice(j * band, (j + 1) * band)
            singles = [ln1_ref[0:1, cut], ln1_ref[1:2, cut], mid_ref[2:3, cut], mid_ref[0:1, cut]]
            singles += [mid_ref[1:2, cut], mid_ref[3:4, cut]]
            whole[j, 0:1, : 6 * band] = jnp.concatenate(singles, axis=1)
            seconds = [held[0:1, 3 * j * band : 3 * (j + 1) * band], fc_held[j : j + 1, :]]
            whole[j, 1:2, : 3 * band + units] = jnp.concatenate(seconds, axis=1)
            out_ref[j] = split_halves(whole[j], 0)

    return whole_call(
        body,
        [((sz.n_ctx, 16, lanes), BF16)],
        1,
        (place, ln1, qkv, middle, *fc_sums),
        "pack_vectors",
        [
            pltpu.VMEM((8, 3 * sz.width), F32),
            pltpu.VMEM((sz.n_ctx, units), F32),
            pltpu.VMEM((sz.n_ctx, 8, lanes), F32),
        ],
    )[0]


def join_shares(sz, place, shares):
    band, width = sz.width // sz.n_ctx, sz.width
    share = sz.hidden // (sz.n_ctx * sz.n_grp)
    n = sz.n_grp
    n_fc = shares[0].shape[0] - share

    def body(place_ref, *refs):
        fc_ref, proj_ref, held = refs[n:]
        core, gx = place_ref[CORE], place_ref[GX]
        for c in range(2):
            for k in range(sz.gx):
                held[((gx - k) % sz.gx) * 2 + (core + c) % 2] = refs[c * sz.gx + k][...]
        for j in range(sz.n_ctx):
            cut = slice(j * share, (j + 1) * share)
            fc_ref[:, j * share * n : (j + 1) * share * n] = jnp.concatenate(
                [held[q, :n_fc, cut].astype(F32) for q in range(n)], axis=1
            )
        for q in range(n):
            proj_ref[q * share : (q + 1) * share, :] = held[q, n_fc:, :].astype(F32)

    if not sz.aligned:
        held = order_grp(sz, place, shares).reshape((n,) + shares[0].shape)
        fc = held[:, :n_fc].reshape(n, band, sz.n_ctx, share)
        fc = fc.transpose(1, 2, 0, 3).reshape(band, sz.hidden)
        return fc, held[:, n_fc:].reshape(n * share, width)
    return whole_call(
        body,
        [((band, sz.hidden), F32), ((n * share, width), F32)],
        1,
        (place, *shares),
        "join_shares",
        [pltpu.VMEM((n,) + shares[0].shape, BF16)],
    )


def order_grp(sz, place, values):
    held = jnp.stack(values).reshape((2, sz.gx) + values[0].shape)
    held = jnp.roll(held[:, ::-1], place[GX] + 1, axis=1)
    return jnp.roll(held, place[CORE], axis=0).swapaxes(0, 1).astype(F32)


def qkv_weights(sz, place, normed, dqkv):
    band = sz.width // sz.n_ctx
    rows = band // sz.gx
    w3 = 3 * sz.lanes

    if not sz.packed:
        grad = dot_tn(normed, dqkv).astype(BF16).reshape(sz.n_ctx, sz.gx, rows, w3)
        grad = jnp.roll(grad, -place[GX], axis=1)
        return [grad[:, k] for k in range(sz.gx)]

    def body(place_ref, normed_ref, dqkv_ref, *refs):
        held = refs[-1]
        held[...] = dot_tn(normed_ref[...], dqkv_ref[...]).astype(BF16)
        for k in range(sz.gx):
            to = (place_ref[GX] + k) % sz.gx
            for i in range(sz.n_ctx):
                at = pl.multiple_of(i * band + to * rows, 16)
                refs[k][i] = held[pl.ds(at, rows), :]

    return whole_call(
        body,
        [((sz.n_ctx, rows, w3), BF16)] * sz.gx,
        1,
        (place, normed, dqkv),
        "qkv_weights",
        [pltpu.VMEM((sz.width, w3), BF16)],
    )


def join_heads(sz, place, pieces, rows, n_tail):
    lanes = pieces[0].shape[1]
    start = sz.half * rows
    end = start + n_tail
    half = sz.width // 2
    if not sz.packed:
        held = order_grp(sz, place, pieces)
        sel = held[:, :, :start].reshape(sz.gx, 2, sz.half, rows, lanes)
        sel = sel.transpose(2, 1, 0, 3, 4).reshape(sz.groups, sz.gx * rows, lanes)
        out = held[:, :, end:].sum(axis=0).reshape(2, sz.gx * rows // 2, 2, half)
        out = out.transpose(2, 1, 0, 3).reshape(sz.gx * rows, sz.width)
        small = add_halves(held[:, :, start:end]).sum(axis=(0, 1))
        return join_slots(sz, sel), out, *(small[row, at : at + n] for row, at, n in small_cuts(sz))

    def body(place_ref, *refs):
        sel_ref, out_ref = refs[sz.n_grp : sz.n_grp + 2]
        small_refs, held = refs[sz.n_grp + 2 : -1], refs[-1]
        core, gx = place_ref[CORE], place_ref[GX]
        small = sum(add_halves(r[start:end, :]) for r in refs[: sz.n_grp])
        for ref, (row, at, n) in zip(small_refs, small_cuts(sz)):
            ref[...] = small[row, at : at + n]
        for c in range(2):
            for k in range(sz.gx):
                held[((gx - k) % sz.gx) * 2 + (core + c) % 2] = refs[c * sz.gx + k][...]
        for x in range(sz.gx):
            at_rows = slice(x * rows, (x + 1) * rows)
            both = [
                held[2 * x + g % 2, (g // 2) * rows : (g // 2 + 1) * rows, :].astype(F32) for g in range(sz.groups)
            ]
            for third in range(3):
                at = third * sz.lanes
                own = jnp.concatenate([b[:, at : at + sz.used] for b in both], axis=1)[:, : sz.width]
                first = sum(b[:, at + sz.used : at + sz.used + sz.head] for b in both)
                rest = jnp.zeros((rows, sz.width - sz.head), F32)
                sel_ref[at_rows, third * sz.width : (third + 1) * sz.width] = own + jnp.concatenate(
                    [first, rest], axis=1
                )
        mid = sz.gx * rows // 2
        for c in range(2):
            piece = sum(held[2 * x + c, end:, :].astype(F32) for x in range(sz.gx))
            out_ref[:mid, c * half : (c + 1) * half] = piece[:, :half]
            out_ref[mid:, c * half : (c + 1) * half] = piece[:, half:]

    return whole_call(
        body,
        [((sz.gx * rows, 3 * sz.width), F32), ((sz.gx * rows, sz.width), F32)]
        + [((n,), F32) for _, _, n in small_cuts(sz)],
        1,
        (place, *pieces),
        "join_heads",
        [pltpu.VMEM((sz.n_grp,) + pieces[0].shape, BF16)],
    )


def join_slots(sz, sel):
    n = sel.shape[1]
    thirds = sel.reshape(sz.groups, n, 3, sz.lanes)
    own = thirds[..., : sz.used].transpose(2, 1, 0, 3).reshape(3, n, sz.groups * sz.used)
    own = own[..., : sz.width]
    first = thirds[..., sz.used : sz.used + sz.head].sum(axis=0).transpose(1, 0, 2)
    own = own.at[:, :, : sz.head].add(first)
    return own.transpose(1, 0, 2).reshape(n, 3 * sz.width)


def finish_tokens(sz, dnorm, tokens, grad_middle, gain):
    n = len(dnorm)

    def body(*refs):
        tok_ref, grad_ref, gain_ref = refs[n : n + 3]
        outs = refs[n + 3 :]
        e = refs[0][...].astype(F32)
        for ref in refs[1:n]:
            e += ref[...].astype(F32)
        hat, r = normalize(tok_ref[...].astype(F32))
        eg = e * gain_ref[...]
        inner = eg - jnp.mean(eg, axis=-1, keepdims=True)
        inner -= hat * jnp.mean(eg * hat, axis=-1, keepdims=True)
        total = (grad_ref[...] + r * inner).astype(BF16)
        for t in range(sz.parts):
            outs[t][...] = total[t * sz.block : (t + 1) * sz.block]

    return whole_call(
        body,
        [((sz.block, sz.width), BF16)] * sz.parts,
        0,
        (*dnorm, tokens, grad_middle, gain),
        "finish_tokens",
    )


def finish_middle(sz, mixed, middle, proj_bias):
    n = len(mixed)

    def body(*refs):
        middle_ref, bias_ref = refs[n : n + 2]
        outs = refs[n + 2 :]
        total = middle_ref[...] + bias_ref[...]
        for ref in refs[:n]:
            total += ref[...].astype(F32)
        total = total.astype(BF16)
        for t in range(sz.parts):
            outs[t][...] = total[t * sz.block : (t + 1) * sz.block]

    return whole_call(
        body,
        [((sz.block, sz.width), BF16)] * sz.parts,
        0,
        (*mixed, middle, proj_bias),
        "finish_middle",
    )


def unsort_rows(sz, place, docs, *arrays):
    n = len(arrays)

    def body(place_ref, doc_ref, *refs):
        outs = refs[n * sz.parts :]
        for t in range(sz.parts):
            for a in range(4):
                src = source_grain(sz, doc_ref, 4 * ((place_ref[ROW] + t) % sz.parts) + a)
                at = pl.ds(a * sz.grain, sz.grain)
                for i in range(n):
                    outs[i][src] = refs[i * sz.parts + t][at, :].astype(F32)

    out = whole_call(
        body,
        [((sz.grains, sz.grain, sz.width), F32)] * n,
        2,
        (place, docs, *(b for blocks in arrays for b in blocks)),
        "unsort_rows",
    )
    return [o.reshape(sz.rows, sz.width) for o in out]


def gather_near(sz, block):
    return [block, shift(block, "core", 2, 1)]


def gather_far(sz, block, before):
    far = []
    for k in range(1, sz.gx):
        along = after(before, shift(block, "gx", sz.gx, k))
        far += [along, shift(along, "core", 2, 1)]
    return far


def return_rows(sz, near, far, later):
    terms = [near[0], shift(near[1], "core", 2, 1)]
    for k in range(1, sz.gx):
        mine, other = far[2 * k - 2 : 2 * k]
        mine = (mine.astype(F32) + shift(other, "core", 2, 1).astype(F32)).astype(BF16)
        mine, later = lax.optimization_barrier((mine, later))
        terms.append(shift(mine, "gx", sz.gx, -k))
    return terms, later


def return_direct(sz, near, far):
    terms = [near[0], shift(near[1], "core", 2, 1)]
    for k in range(1, sz.gx):
        for c in range(2):
            pairs = [
                (2 * x + core, 2 * ((x - k) % sz.gx) + (core + c) % 2) for x in range(sz.gx) for core in range(2)
            ]
            terms.append(lax.ppermute(far[2 * k - 2 + c], GRP, pairs))
    return terms


def all_grp(sz, value, before=None):
    along = [value] + [shift(value, "gx", sz.gx, k) for k in range(1, sz.gx)]
    if before is not None:
        along = after(before, along)
    return along + [shift(v, "core", 2, 1) for v in along]


def after(gate, value):
    return lax.optimization_barrier((gate, value))[1]


def head_columns(sz, weight, hg):
    lead = weight.shape[:-1]
    pieces = []
    for third in range(3):
        full = weight[..., third * sz.width : (third + 1) * sz.width]
        spare = sz.groups * sz.used - sz.width
        if spare:
            full = jnp.pad(full, [(0, 0)] * len(lead) + [(0, spare)])
        own = lax.dynamic_slice_in_dim(full, hg * sz.used, sz.used, axis=len(lead))
        first = full[..., : sz.head] if third < 2 else jnp.zeros(lead + (sz.head,), weight.dtype)
        rest = sz.lanes - sz.used - sz.head
        pieces += [own, first]
        if rest:
            pieces.append(jnp.zeros(lead + (rest,), weight.dtype))
    return jnp.concatenate(pieces, axis=-1)


def weight_shares(sz, place, qkv_weight, fc_weight, proj_weight):
    share = sz.hidden // (sz.n_ctx * sz.n_grp)
    units = sz.n_ctx * share
    if not sz.aligned:
        mine = place[GX] * 2 + place[CORE]
        w_sel = head_columns(sz, qkv_weight, place[QUARTER])
        fc = fc_weight.reshape(sz.width, sz.n_ctx, sz.n_grp, share)
        fc = lax.dynamic_index_in_dim(fc, mine, 2, keepdims=False).reshape(sz.width, units)
        proj = proj_weight.reshape(sz.n_ctx, sz.n_grp, share, sz.width)
        proj = lax.dynamic_index_in_dim(proj, mine, 1, keepdims=False).reshape(units, sz.width)
        return w_sel, fc, proj

    def body(place_ref, qkv_ref, fc_in, proj_in, sel_ref, fc_ref, proj_ref):
        hg, mine = place_ref[QUARTER], place_ref[GX] * 2 + place_ref[CORE]
        for third in range(3):
            to, base = third * sz.lanes, third * sz.width
            end = jnp.zeros((sz.width, sz.lanes - sz.used), BF16)
            if third < 2:
                end = qkv_ref[:, base : base + 128][:, : sz.head]
                if sz.lanes - sz.used > sz.head:
                    end = jnp.concatenate(
                        [end, jnp.zeros((sz.width, sz.lanes - sz.used - sz.head), BF16)], axis=1
                    )
            for g in range(sz.groups):

                @pl.when(hg == g)
                def _():
                    own = qkv_ref[:, base : base + sz.width][:, g * sz.used : (g + 1) * sz.used]
                    sel_ref[:, to : to + sz.lanes] = jnp.concatenate([own, end], axis=1)

        wide = share * sz.n_grp
        for q in range(sz.n_grp):

            @pl.when(mine == q)
            def _():
                fc_ref[...] = jnp.concatenate(
                    [
                        fc_in[:, j * wide : (j + 1) * wide][:, q * share : (q + 1) * share]
                        for j in range(sz.n_ctx)
                    ],
                    axis=1,
                )

        for j in range(sz.n_ctx):
            at = pl.multiple_of(j * wide + mine * share, 16)
            proj_ref[j * share : (j + 1) * share, :] = proj_in[pl.ds(at, share), :]

    return whole_call(
        body,
        [((sz.width, 3 * sz.lanes), BF16), ((sz.width, units), BF16), ((units, sz.width), BF16)],
        1,
        (place, qkv_weight, fc_weight, proj_weight),
        "weight_shares",
    )


def body(
    tokens,
    ln1_gain,
    ln1_bias,
    qkv_weight,
    qkv_bias,
    out_weight,
    out_bias,
    ln2_gain,
    ln2_bias,
    fc_weight,
    fc_bias,
    proj_weight,
    proj_bias,
    doc_blocks,
    cotangent,
):
    rows, width = tokens.shape
    hidden = fc_weight.shape[1]
    n_ctx = lax.axis_size("hg") * lax.axis_size("part")
    n_grp = lax.axis_size("gx") * 2
    sz = Sizes(rows, width, hidden, doc_blocks.shape[1], n_ctx, n_grp)
    hg, part = lax.axis_index("hg"), lax.axis_index("part")
    gx, core = lax.axis_index("gx"), lax.axis_index("core")
    quarter = hg % sz.half * 2 + core
    my_part = part // 2 * 2 + hg // sz.half
    place = jnp.stack([quarter, my_part, core, gx, hg, part]).astype(jnp.int32)
    mine = gx * 2 + core

    def vector(v):
        return v.astype(F32)[None, :]

    gain1, bias1 = vector(ln1_gain), vector(ln1_bias)
    gain2, bias2 = vector(ln2_gain), vector(ln2_bias)
    share = hidden // (n_ctx * n_grp)
    b_sel = head_columns(sz, vector(qkv_bias), quarter)
    fc_b = lax.dynamic_index_in_dim(
        vector(fc_bias).reshape(1, n_ctx, n_grp, share), mine, 2, keepdims=False
    ).reshape(1, n_ctx * share)
    spare = sz.groups * sz.used - sz.width
    w_out = jnp.pad(out_weight, ((0, spare), (0, 0))) if spare else out_weight

    tok_parts, cot_parts = sort_rows(sz, place, doc_blocks, tokens, cotangent)
    tok_rows = jnp.concatenate(to_owner(sz, tok_parts), axis=0)
    docs = jnp.where(core == part % 2, doc_blocks, shift(doc_blocks, "core", 2, 1))

    w_sel, fc, proj = weight_shares(sz, place, *after(tok_rows, (qkv_weight, fc_weight, proj_weight)))
    chunks = []
    for k in range(sz.half):
        block = after(w_sel, to_peer(sz, tok_rows, 2 * k)) if k else tok_rows
        chunks += [block, to_peer(sz, block, 1)]

    cot_rows = jnp.concatenate(to_owner(sz, after(tok_rows, cot_parts)), axis=0)
    cot_near = gather_near(sz, cot_rows)
    cot_far = gather_far(sz, cot_rows, place)

    saved, att_out = attend_forward(sz, place, docs, chunks, gain1, bias1, w_sel, b_sel)
    att_out = after(cot_rows, att_out)
    att = [to_peer(sz, att_out[k], k) for k in range(sz.groups)]
    middle, second = project_out(
        sz, place, att, tok_rows, w_out, vector(out_bias), gain2, bias2
    )

    sec_near = gather_near(sz, second)
    act_n, gh_n, back_n, fc_sum_n = feed_forward(sz, sec_near, cot_near, fc, fc_b, proj, "feed_forward_near")
    mixed_n = feed_forward_out(sz, act_n, proj)
    sec_far = gather_far(sz, second, (back_n, mixed_n))
    act_f, gh_f, back_f, fc_sum_f = feed_forward(sz, sec_far, cot_far, fc, fc_b, proj, "feed_forward_far")
    back, act_f = return_rows(sz, back_n, back_f, act_f)
    ff_sent = feed_forward_weights(sz, sec_near + sec_far, gh_n + gh_f, act_n + act_f, cot_near + cot_far)
    mixed_f = feed_forward_out(sz, after(ff_sent, act_f), proj)
    back = after(mixed_f, back)
    grad_middle, d_out, mid_sums, datt_out = middle_backward(
        sz, place, back, middle, cot_rows, w_out, gain2, att
    )
    datt = [to_peer(sz, datt_out[k], k) for k in range(sz.groups)]

    band = width // n_ctx
    half = width // 2
    n_rows = band // sz.gx
    datt[1:], ff_sent = lax.optimization_barrier((datt[1:], ff_sent))
    ff_far = lax.all_to_all(ff_sent, "hg", 0, 0, tiled=True)
    mixed = return_direct(sz, mixed_n, mixed_f)

    out_terms = [d.reshape(n_ctx, band, half) for d in (d_out[0], shift(d_out[1], "core", 2, 1))]

    dqkv, qkv_sum, ln1_sums, dnorm_out = attend_backward(sz, place, docs, saved, w_sel, datt)
    dnorm_out, dqkv = after((mixed, out_terms), (dnorm_out, dqkv))
    dnorm = [dnorm_out[0], to_peer(sz, dnorm_out[1], 1)]
    for k in range(1, sz.half):
        both = dnorm_out[2 * k].astype(F32) + to_peer(sz, dnorm_out[2 * k + 1], 1).astype(F32)
        both = both.astype(BF16)
        dnorm.append(to_peer(sz, both, 2 * k))
    grad_parts = finish_tokens(sz, dnorm, tok_rows, grad_middle, gain1)
    grad_back = from_owner(sz, grad_parts)
    out_parts = finish_middle(sz, after(dqkv, mixed), middle, vector(proj_bias))

    sel_terms = qkv_weights(sz, place, saved[1], dqkv)
    sel_terms = [sel_terms[0]] + [shift(sel_terms[k], "gx", sz.gx, k) for k in range(1, sz.gx)]
    tail = pack_vectors(sz, place, ln1_sums, qkv_sum, mid_sums, [fc_sum_n, fc_sum_f])
    n_tail = tail.shape[1]
    pieces = pack_sums(sz, place, sel_terms, out_terms, after(out_parts, tail))
    got = [pieces[0]] + [shift(pieces[s], "part", sz.parts, s) for s in range(1, sz.parts)]
    out_back = from_owner(sz, out_parts)
    blocks = sum_packed(sz, after((grad_parts, out_back), got), n_rows, n_tail)
    got = [blocks[0]] + [shift(blocks[k], "hg", sz.groups, k) for k in range(1, sz.groups)]
    sums = unpack_sums(sz, place, after(grad_back, got), n_rows, n_tail)
    grad_qkv, grad_out, *cuts = join_heads(sz, place, all_grp(sz, sums), n_rows, n_tail)
    output, grad_tokens = unsort_rows(sz, place, doc_blocks, out_back, grad_back)

    ff_parts = sum_groups(sz, place, after(pieces, ff_far))
    ff_parts = [ff_parts[0]] + [shift(ff_parts[s], "part", sz.parts, s) for s in range(1, sz.parts)]
    ff_share = sum_arrays(sz, after(blocks, ff_parts), "sum_parts")
    grad_fc, grad_proj = join_shares(sz, place, all_grp(sz, ff_share, sums))

    g_ln1_gain, g_ln1_bias, g_qkv_bias, g_out_bias, g_ln2_gain, g_ln2_bias, g_fc_bias, g_proj_bias = cuts
    return (
        output,
        grad_tokens,
        g_ln1_gain,
        g_ln1_bias,
        grad_qkv,
        g_qkv_bias,
        grad_out,
        g_out_bias,
        g_ln2_gain,
        g_ln2_bias,
        grad_fc,
        g_fc_bias,
        grad_proj,
        g_proj_bias,
    )


def solution(mesh):
    n_grp, n_ctx = mesh.devices.shape
    split = P(GRP + CTX, None)

    def run(tokens, *rest):
        rows = tokens.shape[0] // (n_grp * n_ctx)
        parts = rows // min(rows // 2, SEQ_LEN // n_ctx)
        fine = Mesh(mesh.devices.reshape(n_grp // 2, 2, n_ctx // parts, parts), GRP + CTX)
        each = jax.shard_map(
            body,
            mesh=fine,
            in_specs=(split,) + (P(),) * 12 + (P(GRP, None), split),
            out_specs=(
                split,
                split,
                P(CTX),
                P(CTX),
                P(CTX, None),
                P(CTX),
                P(CTX, None),
                P(CTX),
                P(CTX),
                P(CTX),
                P(CTX, None),
                P(CTX),
                P(CTX, None),
                P(CTX),
            ),
            check_vma=False,
        )
        return each(tokens, *rest)

    return run
```

```python
import functools
import math

import jax
import jax.numpy as jnp
from jax import lax
from jax.experimental import pallas as pl
from jax.experimental.pallas import tpu as pltpu
from jax.sharding import Mesh
from jax.sharding import PartitionSpec as P

HEADS = 12
SEQ_LEN = 2048
FAR = 1e30
F32 = jnp.float32
BF16 = jnp.bfloat16
GRP = ("gx", "core")
CTX = ("hg", "part")
VMEM_BYTES = 56 * 1024 * 1024


QUARTER, PART, CORE, GX, HG, ROW = range(6)


class Sizes:
    def __init__(self, rows, width, hidden, docs, n_ctx, n_grp):
        self.rows, self.width, self.hidden, self.docs = rows, width, hidden, docs
        self.n_ctx, self.n_grp = n_ctx, n_grp
        self.head = width // HEADS
        self.block = min(rows // 2, SEQ_LEN // n_ctx)
        self.parts = rows // self.block
        self.groups = n_ctx // self.parts
        self.grain = self.block // 4
        self.grains = rows // self.grain
        self.per = -(-HEADS // self.groups)
        self.used = self.per * self.head
        self.lanes = -(-((self.per + 1) * self.head) // 128) * 128
        self.span = n_ctx * self.block
        self.half = self.groups // 2
        self.tile = 256
        self.steps = self.span // self.tile
        self.gx = n_grp // 2
        self.scale = self.head ** (-0.5)
        band, share = width // n_ctx, hidden // (n_ctx * n_grp)
        whole = self.groups * self.used == width
        self.aligned = whole and band % 32 == 0 and share % 32 == 0 and share * n_ctx == width
        self.packed = whole and band % (32 * self.gx // 2) == 0 and 3 * self.lanes == width


def peer(sz, quarter, at, sign):
    return (((quarter >> 1) + sign * (at >> 1)) % sz.half) * 2 + ((quarter + at) & 1)


def dot(a, b):
    return lax.dot_general(a, b, (((1,), (0,)), ((), ())), preferred_element_type=F32)


def dot_nt(a, b):
    return lax.dot_general(a, b, (((1,), (1,)), ((), ())), preferred_element_type=F32)


def dot_tn(a, b):
    return lax.dot_general(a, b, (((0,), (0,)), ((), ())), preferred_element_type=F32)


def dot_split(mask, value, transposed):
    high = value.astype(BF16)
    low = (value - high.astype(F32)).astype(BF16)
    mul = dot_tn if transposed else dot
    return mul(mask, high) + mul(mask, low)


def shift(value, axis, size, step):
    return lax.ppermute(value, axis, [(i, (i + step) % size) for i in range(size)])


def to_peer(sz, value, at):
    if at == 0:
        return value
    pairs = []
    for core in range(2):
        for hg in range(sz.groups):
            to = (hg // sz.half) * sz.half + (hg + at // 2) % sz.half
            pairs.append((core * sz.groups + hg, ((core + at) % 2) * sz.groups + to))
    return lax.ppermute(value, ("core", "hg"), pairs)


def owner_pairs(sz, t):
    pairs = []
    for core in range(2):
        for hg in range(sz.groups):
            for row in range(sz.parts):
                part = (row + t) % sz.parts
                to_hg = (part % 2) * sz.half + hg // 2
                to_row = (part // 2) * 2 + core
                to = ((hg % 2) * sz.groups + to_hg) * sz.parts + to_row
                pairs.append(((core * sz.groups + hg) * sz.parts + row, to))
    return pairs


def to_owner(sz, blocks):
    return [lax.ppermute(b, ("core",) + CTX, owner_pairs(sz, t)) for t, b in enumerate(blocks)]


def from_owner(sz, blocks):
    return [
        lax.ppermute(b, ("core",) + CTX, [(b_, a_) for a_, b_ in owner_pairs(sz, t)])
        for t, b in enumerate(blocks)
    ]


def cost(flops, *arrays):
    size = sum(math.prod(a.shape) * a.dtype.itemsize for a in arrays)
    return pl.CostEstimate(flops=int(flops), bytes_accessed=int(size), transcendentals=0)


def whole_call(body, outs, n_scalars, args, name, scratch=(), flops=0):
    shapes = [jax.ShapeDtypeStruct(s, t) for s, t in outs]
    specs = [pl.BlockSpec(memory_space=pltpu.SMEM)] * n_scalars
    specs += [pl.BlockSpec(memory_space=pltpu.VMEM)] * (len(args) - n_scalars)
    return pl.pallas_call(
        body,
        out_shape=shapes,
        in_specs=specs,
        out_specs=[pl.BlockSpec(memory_space=pltpu.VMEM)] * len(outs),
        scratch_shapes=list(scratch),
        compiler_params=pltpu.CompilerParams(vmem_limit_bytes=VMEM_BYTES),
        cost_estimate=cost(flops, *args, *shapes),
        name=name,
    )(*args)


def source_grain(sz, doc_ref, place):
    is_long = [(doc_ref[0, d] == sz.block).astype(jnp.int32) for d in range(sz.docs)]
    longs = sum(is_long)
    seen_long, seen_short, begin, source = 0, 0, 0, 0
    for d in range(sz.docs):
        count = doc_ref[0, d] // sz.grain
        first = jnp.where(is_long[d] == 1, 4 * seen_long, 4 * longs + seen_short)
        inside = (place >= first) & (place < first + count)
        source = source + jnp.where(inside, begin + place - first, 0)
        seen_long = seen_long + is_long[d]
        seen_short = seen_short + jnp.where(is_long[d] == 1, 0, count)
        begin = begin + count
    return source


def part_is_long(sz, doc_ref, part):
    longs = sum((doc_ref[0, d] == sz.block).astype(jnp.int32) for d in range(sz.docs))
    return part < longs


def sort_rows(sz, place, docs, tokens, cotangent):
    def body(place_ref, doc_ref, tok_ref, cot_ref, *outs):
        for t in range(sz.parts):
            for a in range(4):
                src = source_grain(sz, doc_ref, 4 * ((place_ref[ROW] + t) % sz.parts) + a)
                at = pl.ds(a * sz.grain, sz.grain)
                outs[t][at, :] = tok_ref[src]
                outs[sz.parts + t][at, :] = cot_ref[src]

    shape = (sz.grains, sz.grain, sz.width)
    out = whole_call(
        body,
        [((sz.block, sz.width), BF16)] * (2 * sz.parts),
        2,
        (place, docs, tokens.reshape(shape), cotangent.reshape(shape)),
        "sort_rows",
    )
    return out[: sz.parts], out[sz.parts :]


def block_rows(sz, place_ref, quarter, t):
    at = quarter * sz.parts + (place_ref[PART] - t) % sz.parts
    return pl.ds(pl.multiple_of(at * sz.block, sz.block), sz.block)


def normalize(x):
    center = x - jnp.mean(x, axis=-1, keepdims=True)
    spread = jnp.mean(center * center, axis=-1, keepdims=True)
    r = lax.rsqrt(spread + 1e-05)
    return center * r, r


def pair_masks(sz, step, long_part):
    keys = (step + 1) * sz.tile
    q_row = step * sz.tile + lax.broadcasted_iota(jnp.int32, (sz.tile, 1), 0)
    k_row = lax.broadcasted_iota(jnp.int32, (1, keys), 1)
    q_doc = jnp.where(long_part, 0, (q_row % sz.block) // sz.grain)
    k_doc = jnp.where(long_part, 0, (k_row % sz.block) // sz.grain)
    k_in = jnp.where(long_part, k_row % sz.block, k_row % sz.grain)
    first = (k_row < sz.block) & (k_in == 0)
    same = q_doc == k_doc
    visible = same & (k_row <= q_row)
    select = same & (k_row < q_row) & jnp.logical_not(first)
    return visible, select


def slot_mask(sz, slot):
    lane = lax.broadcasted_iota(jnp.int32, (1, sz.lanes), 1)
    return lane // sz.head == slot


def lower_mask(sz):
    row = lax.broadcasted_iota(jnp.int32, (sz.tile, sz.tile), 0)
    col = lax.broadcasted_iota(jnp.int32, (sz.tile, sz.tile), 1)
    return jnp.where(row > col, 1.0, 0.0).astype(BF16)


def penalty_of(sz, step, long_part, lower, q_slot, k, carry):
    visible, select = pair_masks(sz, step, long_part)
    positive = jnp.maximum(dot_nt(q_slot, k), 0.0)
    chosen = jnp.where(select, positive * positive * (1.0 / sz.block), 0.0)
    penalty = dot_split(lower, chosen, False) + carry
    return jnp.where(visible, penalty, FAR), chosen, positive, select


def attend_forward(sz, place, docs, chunks, gain, bias, w_sel, b_sel):
    lw = sz.lanes
    n = len(chunks)

    def body(place_ref, doc_ref, *refs):
        xs = refs[:n]
        gain_ref, bias_ref, w_ref, b_ref = refs[n : n + 4]
        qkv_ref, normed_ref, hat_ref, lse_ref, out_ref, carry_ref = refs[n + 4 : n + 10]
        att_refs = refs[n + 10 :]
        quarter = place_ref[QUARTER]
        long_part = part_is_long(sz, doc_ref, place_ref[PART])
        for i in range(n):
            hat, _ = normalize(xs[i][...].astype(F32))
            normed = (hat * gain_ref[...] + bias_ref[...]).astype(BF16)
            packed = (dot(normed, w_ref[...]) + b_ref[...]).astype(BF16)
            low = hat.astype(BF16)
            for t in range(sz.parts):
                at = block_rows(sz, place_ref, peer(sz, quarter, i, -1), t)
                here = slice(t * sz.block, (t + 1) * sz.block)
                hat_ref[at, :] = low[here]
                normed_ref[at, :] = normed[here]
                qkv_ref[at, :] = packed[here]
        lower = lower_mask(sz)
        lane = lax.broadcasted_iota(jnp.int32, (1, 128), 1)
        carry_ref[...] = jnp.zeros_like(carry_ref)
        for step in range(sz.steps):
            keys = (step + 1) * sz.tile
            rows = slice(step * sz.tile, keys)
            q = qkv_ref[rows, :lw] * sz.scale
            k = qkv_ref[:keys, lw : 2 * lw]
            v = qkv_ref[:keys, 2 * lw :]
            q_slot = jnp.where(slot_mask(sz, sz.per), q, 0)
            pen, chosen, _, _ = penalty_of(
                sz, step, long_part, lower, q_slot, k, carry_ref[step : step + 1, :keys]
            )
            if step + 1 < sz.steps:
                carry_ref[step + 1 : step + 2, :keys] = carry_ref[step : step + 1, :keys] + jnp.sum(
                    chosen, axis=0, keepdims=True
                )
            total = jnp.zeros((sz.tile, lw), F32)
            lse = jnp.zeros((sz.tile, 128), F32)
            for h in range(sz.per):
                mask = slot_mask(sz, h)
                logits = dot_nt(jnp.where(mask, q, 0), k) - pen
                top = jnp.max(logits, axis=1, keepdims=True)
                weights = jnp.exp(logits - top)
                weight = jnp.sum(weights, axis=1, keepdims=True)
                mixed = dot(weights.astype(BF16), v) / weight
                total = jnp.where(mask, mixed, total)
                lse = jnp.where(lane == h, top + jnp.log(weight), lse)
            out_ref[rows, :] = total
            lse_ref[rows, :] = lse
        for i in range(n):
            for t in range(sz.parts):
                at = block_rows(sz, place_ref, peer(sz, quarter, i, 1), t)
                att_refs[i][t * sz.block : (t + 1) * sz.block, :] = out_ref[at, : sz.used].astype(BF16)

    outs = [
        ((sz.span, 3 * lw), BF16),
        ((sz.span, sz.width), BF16),
        ((sz.span, sz.width), BF16),
        ((sz.span, 128), F32),
        ((sz.span, lw), F32),
        ((sz.steps, sz.span), F32),
    ] + [((sz.rows, sz.used), BF16)] * sz.groups
    out = whole_call(body, outs, 2, (place, docs, *chunks, gain, bias, w_sel, b_sel), "attend_forward", flops=9e9)
    return out[:6], out[6:]


def attend_backward(sz, place, docs, saved, w_sel, grads):
    lw = sz.lanes
    qkv, normed, hat, lse, att, carry = saved
    band = sz.width // sz.n_ctx
    share = band // sz.gx
    n_sel = sz.gx if sz.packed else 1

    def body(place_ref, doc_ref, qkv_ref, normed_ref, hat_ref, lse_ref, att_ref, carry_ref, w_ref, *refs):
        grad_refs = refs[: sz.groups]
        outs = refs[sz.groups :]
        sums_ref, lnsum_ref = outs[:2]
        dnorm_refs = outs[2 : 2 + sz.groups]
        sel_refs = outs[2 + sz.groups : 2 + sz.groups + n_sel]
        rest = outs[2 + sz.groups + n_sel :]
        dout, dk_sum, dv_sum, behind = rest[:4]
        dqkv_ref = rest[4] if sz.packed else sel_refs[0]
        quarter = place_ref[QUARTER]
        long_part = part_is_long(sz, doc_ref, place_ref[PART])
        dout[...] = jnp.zeros_like(dout)
        for i in range(sz.groups):
            for t in range(sz.parts):
                at = block_rows(sz, place_ref, peer(sz, quarter, i, -1), t)
                dout[at, : sz.used] = grad_refs[i][t * sz.block : (t + 1) * sz.block, :]
        dk_sum[...] = jnp.zeros_like(dk_sum)
        dv_sum[...] = jnp.zeros_like(dv_sum)
        behind[...] = jnp.zeros_like(behind)
        lower = lower_mask(sz)
        for step in reversed(range(sz.steps)):
            keys = (step + 1) * sz.tile
            rows = slice(step * sz.tile, keys)
            q = qkv_ref[rows, :lw] * sz.scale
            k = qkv_ref[:keys, lw : 2 * lw]
            v = qkv_ref[:keys, 2 * lw :]
            d_rows = dout[rows, :]
            dot_rows = d_rows.astype(F32) * att_ref[rows, :]
            last = slot_mask(sz, sz.per)
            q_slot = jnp.where(last, q, 0)
            pen, _, positive, select = penalty_of(
                sz, step, long_part, lower, q_slot, k, carry_ref[step : step + 1, :keys]
            )
            dpen = jnp.zeros((sz.tile, keys), F32)
            dq = jnp.zeros((sz.tile, lw), F32)
            for h in range(sz.per):
                mask = slot_mask(sz, h)
                q_h = jnp.where(mask, q, 0)
                d_h = jnp.where(mask, d_rows, 0)
                probs = jnp.exp(dot_nt(q_h, k) - pen - lse_ref[rows, h : h + 1])
                delta = jnp.sum(jnp.where(mask, dot_rows, 0.0), axis=1, keepdims=True)
                ds = probs * (dot_nt(d_h, v) - delta)
                dpen = dpen - ds
                ds_low = ds.astype(BF16)
                dq = jnp.where(mask, dot(ds_low, k), dq)
                dk_sum[:keys, :] += dot_tn(ds_low, q_h)
                dv_sum[:keys, :] += dot_tn(probs.astype(BF16), d_h)
            dchosen = dot_split(lower, dpen, True) + behind[:1, :keys]
            behind[:1, :keys] += jnp.sum(dpen, axis=0, keepdims=True)
            ds_low = jnp.where(select, positive * dchosen * (2.0 / sz.block), 0.0).astype(BF16)
            dq = jnp.where(last, dot(ds_low, k), dq)
            dk_sum[:keys, :] += dot_tn(ds_low, q_slot)
            dqkv_ref[rows, :lw] = (dq * sz.scale).astype(BF16)
        dqkv_ref[:, lw : 2 * lw] = dk_sum[...].astype(BF16)
        dqkv_ref[:, 2 * lw :] = dv_sum[...].astype(BF16)
        sums_ref[...] = jnp.sum(dqkv_ref[...].astype(F32), axis=0, keepdims=True)
        gain_sum = jnp.zeros((1, sz.width), F32)
        bias_sum = jnp.zeros((1, sz.width), F32)
        for i in range(sz.groups):
            for t in range(sz.parts):
                at = block_rows(sz, place_ref, peer(sz, quarter, i, 1), t)
                dnorm = dot_nt(dqkv_ref[at, :], w_ref[...])
                dnorm_refs[i][t * sz.block : (t + 1) * sz.block, :] = dnorm.astype(BF16)
                bias_sum += jnp.sum(dnorm, axis=0, keepdims=True)
                gain_sum += jnp.sum(dnorm * hat_ref[at, :].astype(F32), axis=0, keepdims=True)
        lnsum_ref[0:1, :] = gain_sum
        lnsum_ref[1:2, :] = bias_sum
        if sz.packed:
            held = rest[5]
            held[...] = dot_tn(normed_ref[...], dqkv_ref[...]).astype(BF16)
            for k in range(sz.gx):
                to = (place_ref[GX] + k) % sz.gx
                for i in range(sz.n_ctx):
                    at = pl.multiple_of(i * band + to * share, 16)
                    sel_refs[k][i] = held[pl.ds(at, share), :]

    outs = [((1, 3 * lw), F32), ((2, sz.width), F32)]
    outs += [((sz.rows, sz.width), BF16)] * sz.groups
    if sz.packed:
        outs += [((sz.n_ctx, share, 3 * lw), BF16)] * sz.gx
    else:
        outs += [((sz.span, 3 * lw), BF16)]
    scratch = [
        pltpu.VMEM((sz.span, lw), BF16),
        pltpu.VMEM((sz.span, lw), F32),
        pltpu.VMEM((sz.span, lw), F32),
        pltpu.VMEM((8, sz.span), F32),
    ]
    if sz.packed:
        scratch += [pltpu.VMEM((sz.span, 3 * lw), BF16), pltpu.VMEM((sz.width, 3 * lw), BF16)]
    args = (place, docs, qkv, normed, hat, lse, att, carry, w_sel, *grads)
    out = whole_call(body, outs, 2, args, "attend_backward", scratch)
    sel = out[2 + sz.groups :]
    if not sz.packed:
        grad = dot_tn(normed, sel[0]).astype(BF16).reshape(sz.n_ctx, sz.gx, share, 3 * lw)
        grad = jnp.roll(grad, -place[GX], axis=1)
        sel = [grad[:, k] for k in range(sz.gx)]
    return out[0], out[1], out[2 : 2 + sz.groups], sel


def project_out(sz, place, att, tokens, out_weight, out_bias, gain, bias):
    def body(place_ref, *refs):
        att_refs = refs[: sz.groups]
        tok_ref, w_ref, b_ref, gain_ref, bias_ref, middle_ref, second_ref = refs[sz.groups :]
        total = tok_ref[...].astype(F32) + b_ref[...]
        for k in range(sz.groups):
            at = pl.multiple_of(peer(sz, place_ref[QUARTER], k, -1) * sz.used, 16)
            total += dot(att_refs[k][...], w_ref[pl.ds(at, sz.used), :])
        middle_ref[...] = total
        hat, _ = normalize(total)
        second_ref[...] = (hat * gain_ref[...] + bias_ref[...]).astype(BF16)

    outs = [((sz.rows, sz.width), F32), ((sz.rows, sz.width), BF16)]
    return whole_call(
        body, outs, 1, (place, *att, tokens, out_weight, out_bias, gain, bias), "project_out"
    )


def feed_forward(sz, second, cot, fc, fc_bias, proj, name):
    n = len(second)
    units = fc.shape[1]
    root = math.sqrt(2.0 / math.pi)

    def body(*refs):
        second_refs, cot_refs = refs[:n], refs[n : 2 * n]
        fc_ref, bias_ref, proj_ref = refs[2 * n : 2 * n + 3]
        outs = refs[2 * n + 3 :]
        act_refs, grad_refs, back_refs, sums_ref = outs[:n], outs[n : 2 * n], outs[2 * n : 3 * n], outs[3 * n]
        total = jnp.zeros((1, units), F32)
        for i in range(n):
            hidden = dot(second_refs[i][...], fc_ref[...]) + bias_ref[...]
            square = hidden * hidden
            t = jnp.tanh(root * (hidden + 0.044715 * hidden * square))
            half = 0.5 * (1.0 + t)
            act_refs[i][...] = (hidden * half).astype(BF16)
            slope = half + 0.5 * hidden * (1.0 - t * t) * (root * (1.0 + 3.0 * 0.044715 * square))
            grad = (dot_nt(cot_refs[i][...], proj_ref[...]) * slope).astype(BF16)
            grad_refs[i][...] = grad
            back_refs[i][...] = dot_nt(grad, fc_ref[...]).astype(BF16)
            total += jnp.sum(grad.astype(F32), axis=0, keepdims=True)
        sums_ref[...] = total

    outs = [((sz.rows, units), BF16)] * (2 * n) + [((sz.rows, sz.width), BF16)] * n + [((1, units), F32)]
    out = whole_call(body, outs, 0, (*second, *cot, fc, fc_bias, proj), name)
    return out[:n], out[n : 2 * n], out[2 * n : 3 * n], out[3 * n]


def middle_backward(sz, place, back, middle, cot, out_weight, gain, att):
    n_back = len(back)
    half = sz.width // 2

    def body(place_ref, *refs):
        back_refs = refs[:n_back]
        att_refs = refs[n_back : n_back + sz.groups]
        rest = refs[n_back + sz.groups :]
        cot_ref, middle_ref, w_ref, gain_ref, grad_ref, own_ref, other_ref, sums_ref = rest[:8]
        datt_refs = rest[8:]
        cot = cot_ref[...].astype(F32)
        e = back_refs[0][...].astype(F32)
        for ref in back_refs[1:]:
            e += ref[...].astype(F32)
        hat, r = normalize(middle_ref[...])
        eg = e * gain_ref[...]
        inner = eg - jnp.mean(eg, axis=-1, keepdims=True)
        inner -= hat * jnp.mean(eg * hat, axis=-1, keepdims=True)
        grad = cot + r * inner
        grad_ref[...] = grad
        branch = grad.astype(BF16)
        core = place_ref[CORE]
        for k in range(sz.groups):
            at = pl.multiple_of(peer(sz, place_ref[QUARTER], k, -1) * sz.used, 16)

            @pl.when(at < sz.width)
            def _():
                grad_w = dot_tn(att_refs[k][...], branch).astype(BF16)
                left, right = grad_w[:, :half], grad_w[:, half:]
                own_ref[pl.ds(at, sz.used), :] = jnp.where(core == 0, left, right)
                other_ref[pl.ds(at, sz.used), :] = jnp.where(core == 0, right, left)

        for k in range(sz.groups):
            at = pl.multiple_of(peer(sz, place_ref[QUARTER], k, 1) * sz.used, 16)
            datt_refs[k][...] = dot_nt(branch, w_ref[pl.ds(at, sz.used), :]).astype(BF16)
        sums_ref[0:1, :] = jnp.sum(e * hat, axis=0, keepdims=True)
        sums_ref[1:2, :] = jnp.sum(e, axis=0, keepdims=True)
        sums_ref[2:3, :] = jnp.sum(branch.astype(F32), axis=0, keepdims=True)
        sums_ref[3:4, :] = jnp.sum(cot, axis=0, keepdims=True)

    outs = [((sz.rows, sz.width), F32)] + [((sz.width, half), BF16)] * 2 + [((4, sz.width), F32)]
    outs += [((sz.rows, sz.used), BF16)] * sz.groups
    out = whole_call(body, outs, 1, (place, *back, *att, cot, middle, out_weight, gain), "middle_backward")
    return out[0], out[1:3], out[3], out[4:]


def feed_forward_weights(sz, second, grad_hidden, act, cot):
    n = len(second)
    width, units = sz.width, act[0].shape[1]
    band, share = width // sz.n_ctx, units // sz.n_ctx
    both = band * units // width + share

    if not sz.aligned:
        second, grad_hidden, act, cot = (jnp.concatenate(v, axis=0) for v in (second, grad_hidden, act, cot))
        d_fc = dot_tn(second, grad_hidden).astype(BF16).reshape(sz.groups, sz.parts, -1, width)
        d_proj = dot_tn(act, cot).astype(BF16).reshape(sz.groups, sz.parts, -1, width)
        return jnp.concatenate([d_fc, d_proj], axis=2)

    def body(*refs):
        second_refs, grad_refs, act_refs, cot_refs = (refs[i * n : (i + 1) * n] for i in range(4))
        out_ref = refs[-1]
        d_fc = sum(dot_tn(x[...], g[...]) for x, g in zip(second_refs, grad_refs)).astype(BF16)
        for i in range(sz.n_ctx):
            out_ref[i // sz.parts, i % sz.parts, :band, :] = d_fc[i * band : (i + 1) * band, :]
        d_proj = sum(dot_tn(a[...], c[...]) for a, c in zip(act_refs, cot_refs)).astype(BF16)
        for i in range(sz.n_ctx):
            out_ref[i // sz.parts, i % sz.parts, band:, :] = d_proj[i * share : (i + 1) * share, :]

    return whole_call(
        body,
        [((sz.groups, sz.parts, both, width), BF16)],
        0,
        (*second, *grad_hidden, *act, *cot),
        "feed_forward_weights",
    )[0]


def feed_forward_out(sz, act, proj):
    n = len(act)

    def body(*refs):
        for i in range(n):
            refs[n + 1 + i][...] = dot(refs[i][...], refs[n][...]).astype(BF16)

    return whole_call(body, [((sz.rows, sz.width), BF16)] * n, 0, (*act, proj), "feed_forward_out")


def sum_arrays(sz, pieces, name):
    def body(*refs):
        refs[-1][...] = sum(r[...].astype(F32) for r in refs[:-1]).astype(BF16)

    return whole_call(body, [(pieces[0].shape, BF16)], 0, tuple(pieces), name)[0]


def sum_groups(sz, place, got):
    shape = got.shape[2:]
    if not sz.aligned:
        total = jnp.roll(got.astype(F32).sum(axis=0), -place[ROW], axis=0).astype(BF16)
        return [total[s] for s in range(sz.parts)]

    def body(place_ref, got_ref, *outs):
        for s in range(sz.parts):
            at = (place_ref[ROW] + s) % sz.parts
            outs[s][...] = sum(got_ref[k, at].astype(F32) for k in range(sz.groups)).astype(BF16)

    return whole_call(body, [(shape, BF16)] * sz.parts, 1, (place, got), "sum_groups")


def pack_sums(sz, place, sel, out, tail):
    rows, lanes = sel[0].shape[1:]
    n_tail, n_out = tail.shape[1], out[0].shape[1] // 2
    full = rows + n_tail + n_out
    if not sz.packed:
        sel = sum(t.astype(F32) for t in sel).astype(BF16)
        out = sum(t.astype(F32) for t in out).astype(BF16)
        out = jnp.concatenate([out[:, :n_out], out[:, n_out:]], axis=2)
        both = jnp.concatenate([sel, tail, out], axis=1).reshape((sz.groups, sz.parts, full, lanes))
        both = jnp.roll(both, (-place[HG], -place[ROW]), axis=(0, 1))
        return [both[:, s] for s in range(sz.parts)]
    n = len(sel)

    def body(place_ref, *refs):
        tail_ref, outs = refs[n + 2], refs[n + 3 :]
        for k in range(sz.groups):
            for s in range(sz.parts):
                to = ((place_ref[HG] + k) % sz.groups) * sz.parts + (place_ref[ROW] + s) % sz.parts
                outs[s][k, :rows, :] = sum(r[to].astype(F32) for r in refs[:n]).astype(BF16)
                outs[s][k, rows : rows + n_tail, :] = tail_ref[to]
                total = (refs[n][to].astype(F32) + refs[n + 1][to].astype(F32)).astype(BF16)
                outs[s][k, rows + n_tail :, : lanes // 2] = total[:n_out]
                outs[s][k, rows + n_tail :, lanes // 2 :] = total[n_out:]

    return whole_call(
        body, [((sz.groups, full, lanes), BF16)] * sz.parts, 1, (place, *sel, *out, tail), "pack_sums"
    )


def add_halves(value):
    half = value.shape[-2] // 2
    value = value.astype(F32)
    return value[..., :half, :] + value[..., half:, :]


def split_halves(value, axis):
    high = value.astype(BF16)
    return jnp.concatenate([high, (value - high.astype(F32)).astype(BF16)], axis=axis)


def sum_packed(sz, pieces, rows, n_tail):
    end = rows + n_tail
    if not sz.packed:
        total = sum(p.astype(F32) for p in pieces).astype(BF16)
        tail = split_halves(sum(add_halves(p[:, rows:end]) for p in pieces), 1)
        total = jnp.concatenate([total[:, :rows], tail, total[:, end:]], axis=1)
        return [total[k] for k in range(sz.groups)]
    n = len(pieces)

    def body(*refs):
        for k in range(sz.groups):
            out = refs[n + k]
            for cut in (slice(0, rows), slice(end, None)):
                out[cut, :] = sum(r[k, cut, :].astype(F32) for r in refs[:n]).astype(BF16)
            out[rows:end, :] = split_halves(sum(add_halves(r[k, rows:end, :]) for r in refs[:n]), 0)

    return whole_call(body, [(pieces[0].shape[1:], BF16)] * sz.groups, 0, tuple(pieces), "sum_packed")


def unpack_sums(sz, place, blocks, rows, n_tail):
    full, lanes = blocks[0].shape
    end = rows + n_tail
    if not sz.packed:
        got = jnp.stack(blocks)
        total = got.astype(F32).sum(axis=0).astype(BF16)
        sel = got[:, :rows].astype(F32)
        sel = sel[: sz.half] + sel[sz.half :]
        sel = jnp.roll(sel[::-1], place[HG] + 1, axis=0).astype(BF16).reshape(-1, lanes)
        tail = split_halves(add_halves(got[:, rows:end]).sum(axis=0), 0)
        return jnp.concatenate([sel, tail, total[end:]], axis=0)

    def body(place_ref, *refs):
        blocks, out_ref = refs[: sz.groups], refs[sz.groups]
        for k in range(sz.half):
            at = pl.multiple_of(((place_ref[HG] - k) % sz.half) * rows, 16)
            total = blocks[k][:rows, :].astype(F32) + blocks[k + sz.half][:rows, :].astype(F32)
            out_ref[pl.ds(at, rows), :] = total.astype(BF16)
        at = sz.half * rows
        out_ref[at : at + n_tail, :] = split_halves(sum(add_halves(r[rows:end, :]) for r in blocks), 0)
        out_ref[at + n_tail :, :] = sum(r[end:, :].astype(F32) for r in blocks).astype(BF16)

    shape = (sz.half * rows + full - rows, lanes)
    return whole_call(body, [(shape, BF16)], 1, (place, *blocks), "unpack_sums")[0]


def small_cuts(sz):
    band, units = sz.width // sz.n_ctx, sz.hidden // sz.n_ctx
    one = [(0, i * band, band) for i in range(6)]
    return one[:2] + [(1, 0, 3 * band)] + one[2:5] + [(1, 3 * band, units)] + one[5:]


def pack_vectors(sz, place, ln1, qkv, middle, fc_sums):
    band, units = sz.width // sz.n_ctx, sz.hidden // sz.n_ctx
    share = units // sz.n_grp
    w3 = 3 * sz.lanes
    lanes = w3

    if not sz.packed:
        hg, mine = place[QUARTER], place[GX] * 2 + place[CORE]
        placed = jnp.zeros((sz.groups, 1, w3), F32)
        placed = lax.dynamic_update_slice(placed, qkv[None], (hg, 0, 0))
        fc_placed = jnp.zeros((sz.n_ctx, sz.n_grp, share), F32)
        fc_placed = lax.dynamic_update_slice(fc_placed, sum(fc_sums).reshape(sz.n_ctx, 1, share), (0, mine, 0))
        vectors = [ln1[0], ln1[1], join_slots(sz, placed)[0], middle[2], middle[0], middle[1]]
        vectors += [fc_placed.reshape(-1), middle[3]]
        out = jnp.zeros((sz.n_ctx, 8, lanes), F32)
        for v, (row, at, n) in zip(vectors, small_cuts(sz)):
            out = out.at[:, row, at : at + n].set(v.reshape(sz.n_ctx, n))
        return split_halves(out, 1)

    def body(place_ref, ln1_ref, qkv_ref, mid_ref, *refs):
        out_ref, held, fc_held, whole = refs[len(fc_sums) :]
        hg, mine = place_ref[QUARTER], place_ref[GX] * 2 + place_ref[CORE]
        held[...] = jnp.zeros_like(held)
        for g in range(sz.groups):

            @pl.when(hg == g)
            def _():
                for third in range(3):
                    at = third * sz.width + g * sz.used
                    held[0:1, at : at + sz.used] = qkv_ref[:, third * sz.lanes : third * sz.lanes + sz.used]

        for third in range(3):
            at, base = third * sz.width, third * sz.lanes + sz.used
            held[0:1, at : at + sz.head] += qkv_ref[:, base : base + sz.head]
        fc = sum(r[...] for r in refs[: len(fc_sums)])
        fc_held[...] = jnp.zeros_like(fc_held)
        for q in range(sz.n_grp):

            @pl.when(mine == q)
            def _():
                for j in range(sz.n_ctx):
                    fc_held[j : j + 1, q * share : (q + 1) * share] = fc[:, j * share : (j + 1) * share]

        whole[...] = jnp.zeros_like(whole)
        for j in range(sz.n_ctx):
            cut = slice(j * band, (j + 1) * band)
            singles = [ln1_ref[0:1, cut], ln1_ref[1:2, cut], mid_ref[2:3, cut], mid_ref[0:1, cut]]
            singles += [mid_ref[1:2, cut], mid_ref[3:4, cut]]
            whole[j, 0:1, : 6 * band] = jnp.concatenate(singles, axis=1)
            seconds = [held[0:1, 3 * j * band : 3 * (j + 1) * band], fc_held[j : j + 1, :]]
            whole[j, 1:2, : 3 * band + units] = jnp.concatenate(seconds, axis=1)
            out_ref[j] = split_halves(whole[j], 0)

    return whole_call(
        body,
        [((sz.n_ctx, 16, lanes), BF16)],
        1,
        (place, ln1, qkv, middle, *fc_sums),
        "pack_vectors",
        [
            pltpu.VMEM((8, 3 * sz.width), F32),
            pltpu.VMEM((sz.n_ctx, units), F32),
            pltpu.VMEM((sz.n_ctx, 8, lanes), F32),
        ],
    )[0]


def join_shares(sz, place, shares):
    band, width = sz.width // sz.n_ctx, sz.width
    share = sz.hidden // (sz.n_ctx * sz.n_grp)
    n = sz.n_grp
    n_fc = shares[0].shape[0] - share

    def body(place_ref, *refs):
        fc_ref, proj_ref, held = refs[n:]
        core, gx = place_ref[CORE], place_ref[GX]
        for c in range(2):
            for k in range(sz.gx):
                held[((gx - k) % sz.gx) * 2 + (core + c) % 2] = refs[c * sz.gx + k][...]
        for j in range(sz.n_ctx):
            cut = slice(j * share, (j + 1) * share)
            fc_ref[:, j * share * n : (j + 1) * share * n] = jnp.concatenate(
                [held[q, :n_fc, cut].astype(F32) for q in range(n)], axis=1
            )
        for q in range(n):
            proj_ref[q * share : (q + 1) * share, :] = held[q, n_fc:, :].astype(F32)

    if not sz.aligned:
        held = order_grp(sz, place, shares).reshape((n,) + shares[0].shape)
        fc = held[:, :n_fc].reshape(n, band, sz.n_ctx, share)
        fc = fc.transpose(1, 2, 0, 3).reshape(band, sz.hidden)
        return fc, held[:, n_fc:].reshape(n * share, width)
    return whole_call(
        body,
        [((band, sz.hidden), F32), ((n * share, width), F32)],
        1,
        (place, *shares),
        "join_shares",
        [pltpu.VMEM((n,) + shares[0].shape, BF16)],
    )


def order_grp(sz, place, values):
    held = jnp.stack(values).reshape((2, sz.gx) + values[0].shape)
    held = jnp.roll(held[:, ::-1], place[GX] + 1, axis=1)
    return jnp.roll(held, place[CORE], axis=0).swapaxes(0, 1).astype(F32)


def join_heads(sz, place, pieces, rows, n_tail):
    lanes = pieces[0].shape[1]
    start = sz.half * rows
    end = start + n_tail
    half = sz.width // 2
    if not sz.packed:
        held = order_grp(sz, place, pieces)
        sel = held[:, :, :start].reshape(sz.gx, 2, sz.half, rows, lanes)
        sel = sel.transpose(2, 1, 0, 3, 4).reshape(sz.groups, sz.gx * rows, lanes)
        out = held[:, :, end:].sum(axis=0).reshape(2, sz.gx * rows // 2, 2, half)
        out = out.transpose(2, 1, 0, 3).reshape(sz.gx * rows, sz.width)
        small = add_halves(held[:, :, start:end]).sum(axis=(0, 1))
        return join_slots(sz, sel), out, *(small[row, at : at + n] for row, at, n in small_cuts(sz))

    def body(place_ref, *refs):
        sel_ref, out_ref = refs[sz.n_grp : sz.n_grp + 2]
        small_refs, held = refs[sz.n_grp + 2 : -1], refs[-1]
        core, gx = place_ref[CORE], place_ref[GX]
        small = sum(add_halves(r[start:end, :]) for r in refs[: sz.n_grp])
        for ref, (row, at, n) in zip(small_refs, small_cuts(sz)):
            ref[...] = small[row, at : at + n]
        for c in range(2):
            for k in range(sz.gx):
                held[((gx - k) % sz.gx) * 2 + (core + c) % 2] = refs[c * sz.gx + k][...]
        for x in range(sz.gx):
            at_rows = slice(x * rows, (x + 1) * rows)
            both = [
                held[2 * x + g % 2, (g // 2) * rows : (g // 2 + 1) * rows, :].astype(F32) for g in range(sz.groups)
            ]
            for third in range(3):
                at = third * sz.lanes
                own = jnp.concatenate([b[:, at : at + sz.used] for b in both], axis=1)[:, : sz.width]
                first = sum(b[:, at + sz.used : at + sz.used + sz.head] for b in both)
                rest = jnp.zeros((rows, sz.width - sz.head), F32)
                sel_ref[at_rows, third * sz.width : (third + 1) * sz.width] = own + jnp.concatenate(
                    [first, rest], axis=1
                )
        mid = sz.gx * rows // 2
        for c in range(2):
            piece = sum(held[2 * x + c, end:, :].astype(F32) for x in range(sz.gx))
            out_ref[:mid, c * half : (c + 1) * half] = piece[:, :half]
            out_ref[mid:, c * half : (c + 1) * half] = piece[:, half:]

    return whole_call(
        body,
        [((sz.gx * rows, 3 * sz.width), F32), ((sz.gx * rows, sz.width), F32)]
        + [((n,), F32) for _, _, n in small_cuts(sz)],
        1,
        (place, *pieces),
        "join_heads",
        [pltpu.VMEM((sz.n_grp,) + pieces[0].shape, BF16)],
    )


def join_slots(sz, sel):
    n = sel.shape[1]
    thirds = sel.reshape(sz.groups, n, 3, sz.lanes)
    own = thirds[..., : sz.used].transpose(2, 1, 0, 3).reshape(3, n, sz.groups * sz.used)
    own = own[..., : sz.width]
    first = thirds[..., sz.used : sz.used + sz.head].sum(axis=0).transpose(1, 0, 2)
    own = own.at[:, :, : sz.head].add(first)
    return own.transpose(1, 0, 2).reshape(n, 3 * sz.width)


def finish_tokens(sz, dnorm, tokens, grad_middle, gain):
    n = len(dnorm)

    def body(*refs):
        tok_ref, grad_ref, gain_ref = refs[n : n + 3]
        outs = refs[n + 3 :]
        e = refs[0][...].astype(F32)
        for ref in refs[1:n]:
            e += ref[...].astype(F32)
        hat, r = normalize(tok_ref[...].astype(F32))
        eg = e * gain_ref[...]
        inner = eg - jnp.mean(eg, axis=-1, keepdims=True)
        inner -= hat * jnp.mean(eg * hat, axis=-1, keepdims=True)
        total = (grad_ref[...] + r * inner).astype(BF16)
        for t in range(sz.parts):
            outs[t][...] = total[t * sz.block : (t + 1) * sz.block]

    return whole_call(
        body,
        [((sz.block, sz.width), BF16)] * sz.parts,
        0,
        (*dnorm, tokens, grad_middle, gain),
        "finish_tokens",
    )


def finish_middle(sz, mixed, middle, proj_bias):
    n = len(mixed)

    def body(*refs):
        middle_ref, bias_ref = refs[n : n + 2]
        outs = refs[n + 2 :]
        total = middle_ref[...] + bias_ref[...]
        for ref in refs[:n]:
            total += ref[...].astype(F32)
        total = total.astype(BF16)
        for t in range(sz.parts):
            outs[t][...] = total[t * sz.block : (t + 1) * sz.block]

    return whole_call(
        body,
        [((sz.block, sz.width), BF16)] * sz.parts,
        0,
        (*mixed, middle, proj_bias),
        "finish_middle",
    )


def unsort_rows(sz, place, docs, *arrays):
    n = len(arrays)

    def body(place_ref, doc_ref, *refs):
        outs = refs[n * sz.parts :]
        for t in range(sz.parts):
            for a in range(4):
                src = source_grain(sz, doc_ref, 4 * ((place_ref[ROW] + t) % sz.parts) + a)
                at = pl.ds(a * sz.grain, sz.grain)
                for i in range(n):
                    outs[i][src] = refs[i * sz.parts + t][at, :].astype(F32)

    out = whole_call(
        body,
        [((sz.grains, sz.grain, sz.width), F32)] * n,
        2,
        (place, docs, *(b for blocks in arrays for b in blocks)),
        "unsort_rows",
    )
    return [o.reshape(sz.rows, sz.width) for o in out]


def gather_near(sz, block):
    return [block, shift(block, "core", 2, 1)]


def gather_far(sz, block, before):
    far = []
    for k in range(1, sz.gx):
        along = after(before, shift(block, "gx", sz.gx, k))
        far += [along, shift(along, "core", 2, 1)]
    return far


def return_rows(sz, near, far, later):
    terms = [near[0], shift(near[1], "core", 2, 1)]
    for k in range(1, sz.gx):
        mine, other = far[2 * k - 2 : 2 * k]
        mine = (mine.astype(F32) + shift(other, "core", 2, 1).astype(F32)).astype(BF16)
        mine, later = lax.optimization_barrier((mine, later))
        terms.append(shift(mine, "gx", sz.gx, -k))
    return terms, later


def return_direct(sz, near, far):
    terms = [near[0], shift(near[1], "core", 2, 1)]
    for k in range(1, sz.gx):
        for c in range(2):
            pairs = [
                (2 * x + core, 2 * ((x - k) % sz.gx) + (core + c) % 2) for x in range(sz.gx) for core in range(2)
            ]
            terms.append(lax.ppermute(far[2 * k - 2 + c], GRP, pairs))
    return terms


def all_grp(sz, value, before=None):
    along = [value] + [shift(value, "gx", sz.gx, k) for k in range(1, sz.gx)]
    if before is not None:
        along = after(before, along)
    return along + [shift(v, "core", 2, 1) for v in along]


def after(gate, value):
    return lax.optimization_barrier((gate, value))[1]


def head_columns(sz, weight, hg):
    lead = weight.shape[:-1]
    pieces = []
    for third in range(3):
        full = weight[..., third * sz.width : (third + 1) * sz.width]
        spare = sz.groups * sz.used - sz.width
        if spare:
            full = jnp.pad(full, [(0, 0)] * len(lead) + [(0, spare)])
        own = lax.dynamic_slice_in_dim(full, hg * sz.used, sz.used, axis=len(lead))
        first = full[..., : sz.head] if third < 2 else jnp.zeros(lead + (sz.head,), weight.dtype)
        rest = sz.lanes - sz.used - sz.head
        pieces += [own, first]
        if rest:
            pieces.append(jnp.zeros(lead + (rest,), weight.dtype))
    return jnp.concatenate(pieces, axis=-1)


def weight_shares(sz, place, qkv_weight, fc_weight, proj_weight):
    share = sz.hidden // (sz.n_ctx * sz.n_grp)
    units = sz.n_ctx * share
    if not sz.aligned:
        mine = place[GX] * 2 + place[CORE]
        w_sel = head_columns(sz, qkv_weight, place[QUARTER])
        fc = fc_weight.reshape(sz.width, sz.n_ctx, sz.n_grp, share)
        fc = lax.dynamic_index_in_dim(fc, mine, 2, keepdims=False).reshape(sz.width, units)
        proj = proj_weight.reshape(sz.n_ctx, sz.n_grp, share, sz.width)
        proj = lax.dynamic_index_in_dim(proj, mine, 1, keepdims=False).reshape(units, sz.width)
        return w_sel, fc, proj

    def body(place_ref, qkv_ref, fc_in, proj_in, sel_ref, fc_ref, proj_ref):
        hg, mine = place_ref[QUARTER], place_ref[GX] * 2 + place_ref[CORE]
        for third in range(3):
            to, base = third * sz.lanes, third * sz.width
            end = jnp.zeros((sz.width, sz.lanes - sz.used), BF16)
            if third < 2:
                end = qkv_ref[:, base : base + 128][:, : sz.head]
                if sz.lanes - sz.used > sz.head:
                    end = jnp.concatenate(
                        [end, jnp.zeros((sz.width, sz.lanes - sz.used - sz.head), BF16)], axis=1
                    )
            for g in range(sz.groups):

                @pl.when(hg == g)
                def _():
                    own = qkv_ref[:, base : base + sz.width][:, g * sz.used : (g + 1) * sz.used]
                    sel_ref[:, to : to + sz.lanes] = jnp.concatenate([own, end], axis=1)

        wide = share * sz.n_grp
        for q in range(sz.n_grp):

            @pl.when(mine == q)
            def _():
                fc_ref[...] = jnp.concatenate(
                    [
                        fc_in[:, j * wide : (j + 1) * wide][:, q * share : (q + 1) * share]
                        for j in range(sz.n_ctx)
                    ],
                    axis=1,
                )

        for j in range(sz.n_ctx):
            at = pl.multiple_of(j * wide + mine * share, 16)
            proj_ref[j * share : (j + 1) * share, :] = proj_in[pl.ds(at, share), :]

    return whole_call(
        body,
        [((sz.width, 3 * sz.lanes), BF16), ((sz.width, units), BF16), ((units, sz.width), BF16)],
        1,
        (place, qkv_weight, fc_weight, proj_weight),
        "weight_shares",
    )


def body(
    tokens,
    ln1_gain,
    ln1_bias,
    qkv_weight,
    qkv_bias,
    out_weight,
    out_bias,
    ln2_gain,
    ln2_bias,
    fc_weight,
    fc_bias,
    proj_weight,
    proj_bias,
    doc_blocks,
    cotangent,
):
    rows, width = tokens.shape
    hidden = fc_weight.shape[1]
    n_ctx = lax.axis_size("hg") * lax.axis_size("part")
    n_grp = lax.axis_size("gx") * 2
    sz = Sizes(rows, width, hidden, doc_blocks.shape[1], n_ctx, n_grp)
    hg, part = lax.axis_index("hg"), lax.axis_index("part")
    gx, core = lax.axis_index("gx"), lax.axis_index("core")
    quarter = hg % sz.half * 2 + core
    my_part = part // 2 * 2 + hg // sz.half
    place = jnp.stack([quarter, my_part, core, gx, hg, part]).astype(jnp.int32)
    mine = gx * 2 + core

    def vector(v):
        return v.astype(F32)[None, :]

    gain1, bias1 = vector(ln1_gain), vector(ln1_bias)
    gain2, bias2 = vector(ln2_gain), vector(ln2_bias)
    share = hidden // (n_ctx * n_grp)
    b_sel = head_columns(sz, vector(qkv_bias), quarter)
    fc_b = lax.dynamic_index_in_dim(
        vector(fc_bias).reshape(1, n_ctx, n_grp, share), mine, 2, keepdims=False
    ).reshape(1, n_ctx * share)
    spare = sz.groups * sz.used - sz.width
    w_out = jnp.pad(out_weight, ((0, spare), (0, 0))) if spare else out_weight

    tok_parts, cot_parts = sort_rows(sz, place, doc_blocks, tokens, cotangent)
    tok_rows = jnp.concatenate(to_owner(sz, tok_parts), axis=0)
    docs = jnp.where(core == part % 2, doc_blocks, shift(doc_blocks, "core", 2, 1))

    w_sel, fc, proj = weight_shares(sz, place, *after(tok_rows, (qkv_weight, fc_weight, proj_weight)))
    chunks = []
    for k in range(sz.half):
        block = after(w_sel, to_peer(sz, tok_rows, 2 * k)) if k else tok_rows
        chunks += [block, to_peer(sz, block, 1)]

    cot_rows = jnp.concatenate(to_owner(sz, after(tok_rows, cot_parts)), axis=0)
    cot_near = gather_near(sz, cot_rows)
    cot_far = gather_far(sz, cot_rows, place)

    saved, att_out = attend_forward(sz, place, docs, chunks, gain1, bias1, w_sel, b_sel)
    att_out = after(cot_rows, att_out)
    att = [to_peer(sz, att_out[k], k) for k in range(sz.groups)]
    middle, second = project_out(
        sz, place, att, tok_rows, w_out, vector(out_bias), gain2, bias2
    )

    sec_near = gather_near(sz, second)
    act_n, gh_n, back_n, fc_sum_n = feed_forward(sz, sec_near, cot_near, fc, fc_b, proj, "feed_forward_near")
    mixed_n = feed_forward_out(sz, act_n, proj)
    sec_far = gather_far(sz, second, (back_n, mixed_n))
    act_f, gh_f, back_f, fc_sum_f = feed_forward(sz, sec_far, cot_far, fc, fc_b, proj, "feed_forward_far")
    back, act_f = return_rows(sz, back_n, back_f, act_f)
    ff_sent = feed_forward_weights(sz, sec_near + sec_far, gh_n + gh_f, act_n + act_f, cot_near + cot_far)
    mixed_f = feed_forward_out(sz, after(ff_sent, act_f), proj)
    back = after(mixed_f, back)
    grad_middle, d_out, mid_sums, datt_out = middle_backward(
        sz, place, back, middle, cot_rows, w_out, gain2, att
    )
    datt = [to_peer(sz, datt_out[k], k) for k in range(sz.groups)]

    band = width // n_ctx
    half = width // 2
    n_rows = band // sz.gx
    datt[1:], ff_sent = lax.optimization_barrier((datt[1:], ff_sent))
    ff_far = lax.all_to_all(ff_sent, "hg", 0, 0, tiled=True)
    mixed = return_direct(sz, mixed_n, mixed_f)

    out_terms = [d.reshape(n_ctx, band, half) for d in (d_out[0], shift(d_out[1], "core", 2, 1))]

    qkv_sum, ln1_sums, dnorm_out, sel_sent = attend_backward(sz, place, docs, saved, w_sel, datt)
    dnorm_out, sel_sent = after((mixed, out_terms), (dnorm_out, sel_sent))
    dnorm = [dnorm_out[0], to_peer(sz, dnorm_out[1], 1)]
    for k in range(1, sz.half):
        both = dnorm_out[2 * k].astype(F32) + to_peer(sz, dnorm_out[2 * k + 1], 1).astype(F32)
        both = both.astype(BF16)
        dnorm.append(to_peer(sz, both, 2 * k))
    grad_parts = finish_tokens(sz, dnorm, tok_rows, grad_middle, gain1)
    grad_back = from_owner(sz, grad_parts)
    out_parts = finish_middle(sz, after(sel_sent, mixed), middle, vector(proj_bias))

    sel_terms = [sel_sent[0]] + [shift(sel_sent[k], "gx", sz.gx, k) for k in range(1, sz.gx)]
    tail = pack_vectors(sz, place, ln1_sums, qkv_sum, mid_sums, [fc_sum_n, fc_sum_f])
    n_tail = tail.shape[1]
    pieces = pack_sums(sz, place, sel_terms, out_terms, after(out_parts, tail))
    got = [pieces[0]] + [shift(pieces[s], "part", sz.parts, s) for s in range(1, sz.parts)]
    out_back = from_owner(sz, out_parts)
    blocks = sum_packed(sz, after((grad_parts, out_back), got), n_rows, n_tail)
    got = [blocks[0]] + [shift(blocks[k], "hg", sz.groups, k) for k in range(1, sz.groups)]
    sums = unpack_sums(sz, place, after(grad_back, got), n_rows, n_tail)
    output, grad_tokens = unsort_rows(sz, place, doc_blocks, out_back, grad_back)
    grad_qkv, grad_out, *cuts = join_heads(sz, place, all_grp(sz, sums, output), n_rows, n_tail)

    ff_parts = sum_groups(sz, place, after(pieces, ff_far))
    ff_parts = [ff_parts[0]] + [shift(ff_parts[s], "part", sz.parts, s) for s in range(1, sz.parts)]
    ff_share = sum_arrays(sz, after(blocks, ff_parts), "sum_parts")
    grad_fc, grad_proj = join_shares(sz, place, all_grp(sz, ff_share, sums))

    g_ln1_gain, g_ln1_bias, g_qkv_bias, g_out_bias, g_ln2_gain, g_ln2_bias, g_fc_bias, g_proj_bias = cuts
    return (
        output,
        grad_tokens,
        g_ln1_gain,
        g_ln1_bias,
        grad_qkv,
        g_qkv_bias,
        grad_out,
        g_out_bias,
        g_ln2_gain,
        g_ln2_bias,
        grad_fc,
        g_fc_bias,
        grad_proj,
        g_proj_bias,
    )


def solution(mesh):
    n_grp, n_ctx = mesh.devices.shape
    split = P(GRP + CTX, None)

    def run(tokens, *rest):
        rows = tokens.shape[0] // (n_grp * n_ctx)
        parts = rows // min(rows // 2, SEQ_LEN // n_ctx)
        fine = Mesh(mesh.devices.reshape(n_grp // 2, 2, n_ctx // parts, parts), GRP + CTX)
        each = jax.shard_map(
            body,
            mesh=fine,
            in_specs=(split,) + (P(),) * 12 + (P(GRP, None), split),
            out_specs=(
                split,
                split,
                P(CTX),
                P(CTX),
                P(CTX, None),
                P(CTX),
                P(CTX, None),
                P(CTX),
                P(CTX),
                P(CTX),
                P(CTX, None),
                P(CTX),
                P(CTX, None),
                P(CTX),
            ),
            check_vma=False,
        )
        return each(tokens, *rest)

    return run
```
